512 devices in a mesh: seq: 2 (over y_lo), head: 8 (over x, y_hi), dp: 32 (over z, core).
Axes of the slice: x: 4, y: 4 (y_hi: 2, y_lo: 2; y = y_hi * 2 + y_lo), z: 16, core: 2. Of those that a mesh axis runs over, the one named last changes fastest.
Arguments:
- latents: bfloat16 [32, 4, 512, 1152], P('dp', 'seq', 'head'), may hold values from -6 to 6
- cotangent: bfloat16 [32, 4, 512, 1152], P('dp', 'seq', 'head'), may hold values from -6 to 6
- w_qkv: bfloat16 [2, 8, 3, 72, 1152], P(None, 'head'), may hold values from -0.1875 to 0.1875
- w_out: bfloat16 [2, 8, 72, 1152], P(None, 'head'), may hold values from -0.25 to 0.25
Outputs:
- output: bfloat16 [32, 4, 512, 1152], P('dp', 'seq', 'head')
- latent_grads: bfloat16 [32, 4, 512, 1152], P('dp', 'seq', 'head')
- grad_w_qkv: float32 [2, 8, 3, 72, 1152], P(None, 'head')
- grad_w_out: float32 [2, 8, 72, 1152], P(None, 'head')
The draws below stay inside these ranges and needn't reach their ends.
All inputs are finite; a program needn't handle non-finite values.
Results may differ from the reference program's by a relative error of at most 0.022.
Values may be sent and summed in bfloat16 or wider, within the bound.
No kernel may reach another device: no remote copies, remote signals or barrier semaphores. Data moves between devices by JAX's collectives and lax.ppermute only.
A program may use at most 64 MiB of HBM per device.

```python
import jax
import jax.numpy as jnp
from jax import lax

D = 1152
HEADS = 8
HEAD_SIZE = 72
FRAMES = 4
SPATIAL = 512
VIDEOS = 32
N_HEAD = 8


def shard_levels(key, extent, pieces, low, high):
    level, own = 1.0, jax.random.fold_in(key, 6)
    for axis_at, parts in pieces:
        heights = jnp.exp(jax.random.uniform(jax.random.fold_in(own, axis_at), (parts,), jnp.float32, low / len(pieces), high / len(pieces)))
        level = level * jnp.repeat(heights, extent[axis_at] // parts).reshape([-1 if axis == axis_at else 1 for axis in range(len(extent))])
    return level


def normal_values(stream_key, dims, spread, bound, pieces=(), dtype=jnp.bfloat16):
    values = jax.random.normal(stream_key, dims, jnp.float32) * spread
    if len(pieces) > 0:
        values = shard_levels(stream_key, dims, pieces, -0.22, 0.18) * values
    return jnp.clip(values, min=-bound, max=bound).astype(dtype)


def setup_inputs(seed: int = 0) -> dict:
    key_of = jax.random.split(jax.random.key(seed), 5)
    latents = normal_values(key_of[0], (VIDEOS, FRAMES, SPATIAL, D), 1.0, 6.0, ((0, 32), (1, 2), (2, 8)))
    cotangent = normal_values(key_of[1], (VIDEOS, FRAMES, SPATIAL, D), 1.0, 6.0, ((0, 32), (1, 2), (2, 8)))
    w_qkv = normal_values(key_of[2], (2, HEADS, 3, HEAD_SIZE, D), D ** -0.5, 0.1875, ((1, 8),))
    w_out = normal_values(key_of[3], (2, HEADS, HEAD_SIZE, D), (HEADS * HEAD_SIZE) ** -0.5, 0.25, ((1, 8),))
    return {"latents": latents, "cotangent": cotangent, "w_qkv": w_qkv, "w_out": w_out}


EPSILON = 1e-06
SPATIAL_FORM = (('hfeq,hfek->hfqk', 'hfqk,hfek->hfeq', 'hfqk,hfeq->hfek', 'hfqk,hfek->hfeq', 'hfqk,hfeq->hfek'), 3)
TEMPORAL_FORM = (('hqea,hkea->hqka', 'hqka,hkea->hqea', 'hqka,hqea->hkea', 'hqka,hkea->hqea', 'hqka,hqea->hkea'), 2)

def settle(values):
    return lax.optimization_barrier(values.astype(jnp.bfloat16))

def product(pattern, first_op, second_op):
    return jnp.einsum(pattern, first_op.astype(jnp.float32), second_op.astype(jnp.float32))

def normalize(inputs):
    widened = inputs.astype(jnp.float32)
    centered = widened - lax.optimization_barrier(jnp.mean(widened, axis=-1, keepdims=True))
    inverse = lax.rsqrt(lax.optimization_barrier(jnp.mean(centered * centered, axis=-1, keepdims=True)) + EPSILON)
    return (centered * inverse, inverse)

def attend(queries, key_rows, value_rows, form):
    patterns, key_axis = form
    score_scale = queries.shape[-2] ** (-0.5)
    exponent = jnp.exp(product(patterns[0], queries, key_rows) * score_scale)
    attn_probs = exponent / lax.optimization_barrier(jnp.sum(exponent, axis=key_axis, keepdims=True))
    rounded = settle(attn_probs)
    heads_out = settle(product(patterns[1], rounded, value_rows))
    return (heads_out, attn_probs, rounded)

def attend_back(queries, key_rows, value_rows, attn_probs, rounded, grad_heads, form):
    patterns, key_axis = form
    score_scale = queries.shape[-2] ** (-0.5)
    grad_values = product(patterns[2], rounded, grad_heads)
    grad_probs = product(patterns[0], grad_heads, value_rows)
    centered = grad_probs - lax.optimization_barrier(jnp.sum(attn_probs * grad_probs, axis=key_axis, keepdims=True))
    score_grads = settle(attn_probs * centered * score_scale)
    grad_queries = product(patterns[3], score_grads, key_rows)
    grad_keys = product(patterns[4], score_grads, queries)
    return settle(jnp.stack([grad_queries, grad_keys, grad_values], axis=0))

def block_forward(inputs, w_qkv, w_out, form):
    normed, inverse = normalize(inputs)
    hidden = settle(normed)
    projected = settle(product('fad,hced->chfea', hidden, w_qkv))
    heads_out, attn_probs, rounded = attend(projected[0], projected[1], projected[2], form)
    result = settle(inputs.astype(jnp.float32) + product('hfea,hed->fad', heads_out, w_out))
    return (result, (normed, inverse, hidden, projected, attn_probs, rounded, heads_out))

def block_backward(grad_in, saved, w_qkv, w_out, form):
    normed, inverse, hidden, projected, attn_probs, rounded, heads_out = saved
    grad_w_out = product('hfea,fad->hed', heads_out, grad_in)
    grad_heads = settle(product('fad,hed->hfea', grad_in, w_out))
    qkv_grads = attend_back(projected[0], projected[1], projected[2], attn_probs, rounded, grad_heads, form)
    grad_w_qkv = product('chfea,fad->hced', qkv_grads, hidden)
    split_grads = qkv_grads.reshape(3, N_HEAD, -1, qkv_grads.shape[2], qkv_grads.shape[3], qkv_grads.shape[4])
    split_weights = w_qkv.reshape(N_HEAD, -1, 3, w_qkv.shape[-2], w_qkv.shape[-1])
    partial_terms = settle(product('cgjfea,gjced->gfad', split_grads, split_weights))
    normed_grads = lax.optimization_barrier(jnp.sum(partial_terms.astype(jnp.float32), axis=0))
    mean_grad = lax.optimization_barrier(jnp.mean(normed_grads, axis=-1, keepdims=True))
    mean_cross = lax.optimization_barrier(jnp.mean(normed_grads * normed, axis=-1, keepdims=True))
    total_grad = grad_in.astype(jnp.float32) + inverse * (normed_grads - mean_grad - normed * mean_cross)
    return (total_grad, grad_w_qkv, grad_w_out)

def reference(latents, cotangent, w_qkv, w_out):

    def one_video(totals, pair):
        video, grad_video = pair
        mid_rows, saved_one = block_forward(video, w_qkv[0], w_out[0], SPATIAL_FORM)
        result, saved_two = block_forward(mid_rows, w_qkv[1], w_out[1], TEMPORAL_FORM)
        total_two, qkv_two, out_two = block_backward(grad_video, saved_two, w_qkv[1], w_out[1], TEMPORAL_FORM)
        total_one, qkv_one, out_one = block_backward(settle(total_two), saved_one, w_qkv[0], w_out[0], SPATIAL_FORM)
        new_totals = (totals[0] + jnp.stack([qkv_one, qkv_two]), totals[1] + jnp.stack([out_one, out_two]))
        return (new_totals, (result, settle(total_one)))
    start_totals = (jnp.zeros(w_qkv.shape, jnp.float32), jnp.zeros(w_out.shape, jnp.float32))
    totals, outputs = lax.scan(one_video, start_totals, (latents, cotangent))
    return (outputs[0], outputs[1], totals[0], totals[1])
```

```python
import functools

import jax
import jax.numpy as jnp
from jax import lax
from jax.experimental import pallas as pl
from jax.experimental.pallas import tpu as pltpu
from jax.sharding import PartitionSpec as P

EPSILON = 1e-06
E = 72
SCALE = E ** (-0.5)
RING = [[0, 2, 4, 6, 7, 5, 3, 1]]
BF = jnp.bfloat16
F32 = jnp.float32


def nn(a, b):
    return lax.dot_general(a, b, (((1,), (0,)), ((), ())), preferred_element_type=F32)


def nt(a, b):
    return lax.dot_general(a, b, (((1,), (1,)), ((), ())), preferred_element_type=F32)


def tn(a, b):
    return lax.dot_general(a, b, (((0,), (0,)), ((), ())), preferred_element_type=F32)


def normalize(rows):
    wide = rows.astype(F32)
    centered = wide - jnp.mean(wide, axis=-1, keepdims=True)
    inverse = lax.rsqrt(jnp.mean(centered * centered, axis=-1, keepdims=True) + EPSILON)
    return centered * inverse, inverse


def normalize_back(grad, inverse, normed, normed_grads):
    mean_grad = jnp.mean(normed_grads, axis=-1, keepdims=True)
    mean_cross = jnp.mean(normed_grads * normed, axis=-1, keepdims=True)
    return grad.astype(F32) + inverse * (normed_grads - mean_grad - normed * mean_cross)


def regroup(first, second):
    low = lax.broadcasted_iota(jnp.int32, first.shape, 1) < 64
    return (
        jnp.where(low, first, pltpu.roll(second, 64, 1)),
        jnp.where(low, pltpu.roll(first, 64, 1), second),
    )


def norm_kernel(x_ref, out_ref):
    hidden = normalize(x_ref[...])[0].astype(BF)
    for j in range(8):
        out_ref[j] = hidden


def frame_rows(hidden_ref, f):
    return hidden_ref[:, f * 64 : (f + 1) * 64, :].reshape(512, hidden_ref.shape[2])


def softmax(queries, key_rows):
    exponent = jnp.exp(tn(queries, key_rows) * SCALE)
    return exponent / jnp.sum(exponent, axis=1, keepdims=True)


def split3(stacked):
    return tuple(stacked[i * E : (i + 1) * E].astype(BF) for i in range(3))


def spatial_kernel(hidden_ref, w_ref, heads_ref, qkv_ref):
    outs = []
    for f in range(2):
        qkv = nt(w_ref[...], frame_rows(hidden_ref, f))
        qkv_ref[f] = qkv.astype(BF)
        q, k, v = split3(qkv)
        weights = softmax(q, k).astype(BF)
        outs.append(nt(v, weights))
    for m in range(4):
        lanes = slice(m * 128, (m + 1) * 128)
        a, b = regroup(outs[0][:, lanes], outs[1][:, lanes])
        heads_ref[2 * m] = a.astype(BF)
        heads_ref[2 * m + 1] = b.astype(BF)


def middle_kernel(x_ref, g_ref, heads_ref, wo_ref, out_ref):
    y = (x_ref[...].astype(F32) + tn(heads_ref[...], wo_ref[...])).astype(BF)
    g = g_ref[...]
    for s in range(2):
        for f in range(2):
            rows = slice((2 * f + s) * 32, (2 * f + s + 1) * 32)
            out_ref[s, 0, f] = y[rows]
            out_ref[s, 1, f] = g[rows]


def temporal_kernel(
    core_ref, pair_ref, mine_ref, other_ref,
    back_ref, keep_ref, send_ref,
    w_ref, gw_ref, qk_ref, vg_ref, g0_ref, g1_ref, sems,
):
    core = core_ref[0]
    loads = (
        pltpu.make_async_copy(mine_ref, w_ref.at[core], sems.at[0]),
        pltpu.make_async_copy(other_ref, w_ref.at[1 - core], sems.at[1]),
    )
    for load in loads:
        load.start()
    depth = pair_ref.shape[-1]
    rows = jnp.concatenate([pair_ref[s, 0, f] for s in range(2) for f in range(2)], axis=0)
    grad = jnp.concatenate([pair_ref[s, 1, f] for s in range(2) for f in range(2)], axis=0)
    normed, inverse = normalize(rows)
    hidden = normed.astype(BF)
    both = jnp.concatenate([hidden, grad], axis=0)
    for load in loads:
        load.wait()
    qk_ref[...] = nt(w_ref[0], hidden)
    vg_ref[...] = nt(w_ref[1], both)

    def rounded(value):
        return value.astype(BF).astype(F32)

    def ahead(value, r):
        return pltpu.roll(value, 128 - 32 * r, 1) if r else value

    def behind(value, r):
        return pltpu.roll(value, 32 * r, 1) if r else value

    zeros = jnp.zeros((E, 128), F32)
    for h in range(8):
        base = h * 2 * E
        q = rounded(qk_ref[base : base + E])
        k = rounded(qk_ref[base + E : base + 2 * E])
        v = rounded(vg_ref[base : base + E, :128])
        gh = rounded(vg_ref[base + E : base + 2 * E, 128:])
        ks = [ahead(k, r) for r in range(4)]
        vs = [ahead(v, r) for r in range(4)]
        exps = [jnp.exp(jnp.sum(q * kr, axis=0, keepdims=True) * SCALE) for kr in ks]
        total = exps[0] + exps[1] + exps[2] + exps[3]
        probs = [e / total for e in exps]
        weights = [rounded(p) for p in probs]
        heads = sum(w * vr for w, vr in zip(weights, vs))
        gps = [jnp.sum(gh * vr, axis=0, keepdims=True) for vr in vs]
        inner = sum(p * gp for p, gp in zip(probs, gps))
        sgs = [rounded(p * (gp - inner) * SCALE) for p, gp in zip(probs, gps)]
        gq = sum(sg * kr for sg, kr in zip(sgs, ks))
        gk = sum(behind(sg * q, r) for r, sg in enumerate(sgs))
        gv = sum(behind(w * gh, r) for r, w in enumerate(weights))
        g0_ref[base : base + 2 * E] = jnp.concatenate([gq, gk], axis=0).astype(BF)
        g1_ref[base : base + 2 * E, :128] = jnp.concatenate([gv, zeros], axis=0).astype(BF)
        g1_ref[base : base + 2 * E, 128:] = jnp.concatenate([zeros, heads], axis=0).astype(BF)
    for h in range(8):
        span = slice(h * 2 * E, (h + 1) * 2 * E)
        gw_ref[0, span] = nn(g0_ref[span], hidden).astype(BF)
        gw_ref[1, span] = nn(g1_ref[span], both).astype(BF)
    stores = (
        pltpu.make_async_copy(gw_ref.at[core], keep_ref, sems.at[0]),
        pltpu.make_async_copy(gw_ref.at[1 - core], send_ref, sems.at[1]),
    )
    for store in stores:
        store.start()
    mixed = tn(g1_ref[...], w_ref[1])
    normed_grads = tn(g0_ref[...], w_ref[0]) + mixed[:128]
    result = (rows.astype(F32) + mixed[128:]).astype(BF)
    total_grad = normalize_back(grad, inverse, normed, normed_grads).astype(BF)
    for s in range(2):
        for f in range(2):
            at = slice((2 * s + f) * 32, (2 * s + f + 1) * 32)
            back_ref[s, 0, f] = result[at]
            back_ref[s, 1, f] = total_grad[at]
    for store in stores:
        store.wait()


def local_rows(pair_ref, which):
    return jnp.concatenate([pair_ref[s, which, f] for f in range(2) for s in range(2)], axis=0)


def turn_kernel(back_ref, heads_ref, wo_ref, gh_ref, gw_ref, out_ref, grad_ref):
    out_ref[...] = local_rows(back_ref, 0)
    grad = local_rows(back_ref, 1)
    grad_ref[...] = grad
    gh_ref[...] = nt(wo_ref[...], grad).astype(BF)
    gw_ref[...] = nn(heads_ref[...], grad).astype(BF)


def spatial_back_kernel(qkv_ref, gh_ref, hidden_ref, w_ref, terms_ref, gw_ref):
    frames = ([], [])
    for m in range(4):
        pair = regroup(gh_ref[2 * m].astype(F32), gh_ref[2 * m + 1].astype(F32))
        for f in range(2):
            frames[f].append(pair[f])
    total = None
    for f in range(2):
        q, k, v = split3(qkv_ref[f].astype(F32))
        gh = jnp.concatenate(frames[f], axis=1).astype(BF)
        probs = softmax(q, k)
        gv = nn(gh, probs.astype(BF))
        gp = tn(gh, v)
        inner = jnp.sum(probs * gp, axis=1, keepdims=True)
        sg = (probs * (gp - inner) * SCALE).astype(BF)
        grads = jnp.concatenate([nt(k, sg), nn(q, sg), gv], axis=0).astype(BF)
        gw = nn(grads, frame_rows(hidden_ref, f))
        total = gw if total is None else total + gw
        terms = tn(grads, w_ref[...]).astype(BF)
        for j in range(8):
            terms_ref[j, f * 64 : (f + 1) * 64, :] = terms[j * 64 : (j + 1) * 64]
    gw_ref[...] = total.astype(BF)


def last_kernel(terms_ref, x_ref, g_ref, out_ref):
    normed, inverse = normalize(x_ref[...])
    normed_grads = terms_ref[0].astype(F32)
    for j in range(1, 8):
        normed_grads = normed_grads + terms_ref[j].astype(F32)
    out_ref[...] = normalize_back(g_ref[...], inverse, normed, normed_grads).astype(BF)


VMEM = pl.BlockSpec(memory_space=pltpu.VMEM)
SMEM = pl.BlockSpec(memory_space=pltpu.SMEM)
ANY = pl.BlockSpec(memory_space=pl.ANY)
PARAMS = pltpu.CompilerParams(vmem_limit_bytes=48 * 1024 * 1024)


def shape(*dims):
    return jax.ShapeDtypeStruct(dims, BF)


def call(kernel, outs, *args, **more):
    return pl.pallas_call(
        kernel,
        out_shape=outs,
        in_specs=more.pop("in_specs", [VMEM] * len(args)),
        out_specs=more.pop("out_specs", jax.tree.map(lambda _: VMEM, outs)),
        compiler_params=PARAMS,
        **more,
    )(*args)


def over_head(blocks):
    return lax.all_to_all(blocks, "head", 0, 0, tiled=True, axis_index_groups=RING)


def over_seq(blocks):
    return lax.all_to_all(blocks, "seq", 0, 0, tiled=True)


def swap_cores(value, n_dp):
    return lax.ppermute(value, "dp", [(i, i ^ 1) for i in range(n_dp)])


def in_order(core, mine, other):
    return jnp.where(core == 0, jnp.stack([mine, other]), jnp.stack([other, mine]))


def pick(stacked, at):
    return lax.dynamic_index_in_dim(stacked, at, 0, keepdims=False)


def sum_all(grads, n_dp):
    n_z = n_dp // 2
    low = min(4, n_z)
    high = n_z // low
    rows, depth = grads.shape
    near = [
        [s * n_dp + 2 * (b * low + a) + c for s in range(2) for a in range(low)]
        for b in range(high)
        for c in range(2)
    ]
    far = [
        [2 * (b * low + a) + c for b in range(high)] for a in range(low) for c in range(2)
    ]
    parts = lax.all_to_all(
        grads.reshape(2 * low, rows // (2 * low), depth), ("seq", "dp"), 0, 0,
        tiled=True, axis_index_groups=near,
    )
    part = jnp.sum(parts.astype(F32), axis=0).astype(BF)
    if high > 1:
        copies = jnp.broadcast_to(part[None], (high, *part.shape))
        parts = lax.all_to_all(copies, "dp", 0, 0, tiled=True, axis_index_groups=far)
        part = jnp.sum(parts.astype(F32), axis=0).astype(BF)
    copies = jnp.broadcast_to(part[None], (2 * low, *part.shape))
    whole = lax.all_to_all(
        copies, ("seq", "dp"), 0, 0, tiled=True, axis_index_groups=near
    )
    return whole.reshape(rows, depth)


def on_device(n_dp, latents, cotangent, w_qkv, w_out):
    depth = latents.shape[-1]
    core = lax.axis_index("dp") % 2
    x = latents.reshape(128, depth)
    g = cotangent.reshape(128, depth)
    w_own = w_qkv[0].reshape(3 * E, depth)

    half_out = pick(w_out[0].reshape(2, E // 2, depth), core)
    half_two = pick(
        jnp.concatenate([w_qkv[1].reshape(3 * E, depth), w_out[1].reshape(E, depth)]).reshape(
            2, 2 * E, depth
        ),
        core,
    )
    mine_out = lax.all_gather(half_out, "head", axis_index_groups=RING)
    mine_two = lax.all_gather(half_two, "head", axis_index_groups=RING).reshape(16 * E, depth)
    other_out = swap_cores(mine_out, n_dp)
    wo = in_order(core, mine_out, other_out).transpose(1, 0, 2, 3).reshape(8 * E, depth)

    hidden = over_head(call(norm_kernel, shape(8, 128, depth), x))
    heads, qkv = call(spatial_kernel, (shape(8, E, 128), shape(2, 3 * E, 512)), hidden, w_own)
    heads = over_head(heads).reshape(8 * E, 128)
    pair = over_seq(call(middle_kernel, shape(2, 2, 2, 32, depth), x, g, heads, wo))
    other_two = swap_cores(mine_two, n_dp)
    big = shape(16 * E, depth)
    back, keep, send = call(
        temporal_kernel,
        (shape(2, 2, 2, 32, depth), big, big),
        core.reshape(1).astype(jnp.int32), pair, mine_two, other_two,
        in_specs=[SMEM, VMEM, ANY, ANY],
        out_specs=(VMEM, ANY, ANY),
        scratch_shapes=[
            pltpu.VMEM((2, 16 * E, depth), BF),
            pltpu.VMEM((2, 16 * E, depth), BF),
            pltpu.VMEM((16 * E, 128), F32),
            pltpu.VMEM((16 * E, 256), F32),
            pltpu.VMEM((16 * E, 128), BF),
            pltpu.VMEM((16 * E, 256), BF),
            pltpu.SemaphoreType.DMA((2,)),
        ],
    )
    back = over_seq(back)
    two = (keep.astype(F32) + swap_cores(send, n_dp).astype(F32)).astype(BF)
    two = lax.psum_scatter(
        two, "head", scatter_dimension=0, tiled=True, axis_index_groups=RING
    )
    gh, out_one, output, grad_one = call(
        turn_kernel,
        (shape(8 * E, 128), shape(8 * E, depth), shape(128, depth), shape(128, depth)),
        back, heads, wo,
    )
    out_one = lax.psum_scatter(
        out_one, "head", scatter_dimension=0, tiled=True, axis_index_groups=RING
    )
    gh = over_head(gh.reshape(8, E, 128))
    terms, qkv_one = call(
        spatial_back_kernel, (shape(8, 128, depth), shape(3 * E, depth)), qkv, gh, hidden, w_own
    )
    latent_grads = call(last_kernel, shape(128, depth), over_head(terms), x, grad_one)

    one = jnp.concatenate([qkv_one, out_one]).reshape(2, 2 * E, depth)
    one = pick(one, core).astype(F32) + swap_cores(pick(one, 1 - core), n_dp).astype(F32)
    sums = sum_all(jnp.concatenate([one.astype(BF), two]), n_dp)
    sums = in_order(core, sums, swap_cores(sums, n_dp)).astype(F32)
    sums = sums.reshape(2, 2, 2 * E, depth).transpose(1, 0, 2, 3).reshape(2, 4, E, depth)
    return (
        output.reshape(latents.shape),
        latent_grads.reshape(latents.shape),
        sums[:, None, :3],
        sums[:, 3:],
    )


def solution(mesh):
    rows = P("dp", "seq", "head", None)
    specs = (rows, rows, P(None, "head", None, None, None), P(None, "head", None, None))
    return jax.shard_map(
        functools.partial(on_device, mesh.shape["dp"]),
        mesh=mesh, in_specs=specs, out_specs=specs, check_vma=False,
    )
```

```python
import functools

import jax
import jax.numpy as jnp
from jax import lax
from jax.experimental import pallas as pl
from jax.experimental.pallas import tpu as pltpu
from jax.sharding import PartitionSpec as P

EPSILON = 1e-06
E = 72
SCALE = E ** (-0.5)
RING = [[0, 2, 4, 6, 7, 5, 3, 1]]
BF = jnp.bfloat16
F32 = jnp.float32


def nn(a, b):
    return lax.dot_general(a, b, (((1,), (0,)), ((), ())), preferred_element_type=F32)


def nt(a, b):
    return lax.dot_general(a, b, (((1,), (1,)), ((), ())), preferred_element_type=F32)


def tn(a, b):
    return lax.dot_general(a, b, (((0,), (0,)), ((), ())), preferred_element_type=F32)


def normalize(rows):
    wide = rows.astype(F32)
    centered = wide - jnp.mean(wide, axis=-1, keepdims=True)
    inverse = lax.rsqrt(jnp.mean(centered * centered, axis=-1, keepdims=True) + EPSILON)
    return centered * inverse, inverse


def normalize_back(grad, inverse, normed, normed_grads):
    mean_grad = jnp.mean(normed_grads, axis=-1, keepdims=True)
    mean_cross = jnp.mean(normed_grads * normed, axis=-1, keepdims=True)
    return grad.astype(F32) + inverse * (normed_grads - mean_grad - normed * mean_cross)


def regroup(first, second):
    low = lax.broadcasted_iota(jnp.int32, first.shape, 1) < 64
    return (
        jnp.where(low, first, pltpu.roll(second, 64, 1)),
        jnp.where(low, pltpu.roll(first, 64, 1), second),
    )


def norm_kernel(x_ref, wo_ref, out_ref, copies_ref):
    hidden = normalize(x_ref[...])[0].astype(BF)
    for j in range(8):
        out_ref[j] = hidden
        copies_ref[j] = wo_ref[...]


def frame_rows(hidden_ref, f):
    return hidden_ref[:, f * 64 : (f + 1) * 64, :].reshape(512, hidden_ref.shape[2])


def softmax(queries, key_rows):
    exponent = jnp.exp(tn(queries, key_rows) * SCALE)
    return exponent / jnp.sum(exponent, axis=1, keepdims=True)


def split3(stacked):
    return tuple(stacked[i * E : (i + 1) * E].astype(BF) for i in range(3))


def spatial_kernel(hidden_ref, w_ref, heads_ref, qkv_ref):
    outs = []
    for f in range(2):
        qkv = nt(w_ref[...], frame_rows(hidden_ref, f))
        qkv_ref[f] = qkv.astype(BF)
        q, k, v = split3(qkv)
        weights = softmax(q, k).astype(BF)
        outs.append(nt(v, weights))
    for m in range(4):
        lanes = slice(m * 128, (m + 1) * 128)
        a, b = regroup(outs[0][:, lanes], outs[1][:, lanes])
        heads_ref[2 * m] = a.astype(BF)
        heads_ref[2 * m + 1] = b.astype(BF)


def middle_kernel(x_ref, g_ref, heads_ref, wo_ref, pass_ref, out_ref, same_ref):
    y = (x_ref[...].astype(F32) + tn(heads_ref[...], wo_ref[...])).astype(BF)
    g = g_ref[...]
    for s in range(2):
        for f in range(2):
            rows = slice((2 * f + s) * 32, (2 * f + s + 1) * 32)
            out_ref[s, 0, f] = y[rows]
            out_ref[s, 1, f] = g[rows]


def temporal_kernel(
    core_ref, pair_ref, mine_ref, other_ref,
    back_ref, keep_ref, send_ref,
    w_ref, gw_ref, qk_ref, vg_ref, g0_ref, g1_ref, sems,
):
    core = core_ref[0]
    loads = (
        pltpu.make_async_copy(mine_ref, w_ref.at[core], sems.at[0]),
        pltpu.make_async_copy(other_ref, w_ref.at[1 - core], sems.at[1]),
    )
    for load in loads:
        load.start()
    depth = pair_ref.shape[-1]
    rows = jnp.concatenate([pair_ref[s, 0, f] for s in range(2) for f in range(2)], axis=0)
    grad = jnp.concatenate([pair_ref[s, 1, f] for s in range(2) for f in range(2)], axis=0)
    normed, inverse = normalize(rows)
    hidden = normed.astype(BF)
    both = jnp.concatenate([hidden, grad], axis=0)
    for load in loads:
        load.wait()
    qk_ref[...] = nt(w_ref[0], hidden)
    vg_ref[...] = nt(w_ref[1], both)

    def rounded(value):
        return value.astype(BF).astype(F32)

    def ahead(value, r):
        return pltpu.roll(value, 128 - 32 * r, 1) if r else value

    def behind(value, r):
        return pltpu.roll(value, 32 * r, 1) if r else value

    zeros = jnp.zeros((E, 128), F32)
    for h in range(8):
        base = h * 2 * E
        q = rounded(qk_ref[base : base + E])
        k = rounded(qk_ref[base + E : base + 2 * E])
        v = rounded(vg_ref[base : base + E, :128])
        gh = rounded(vg_ref[base + E : base + 2 * E, 128:])
        ks = [ahead(k, r) for r in range(4)]
        vs = [ahead(v, r) for r in range(4)]
        exps = [jnp.exp(jnp.sum(q * kr, axis=0, keepdims=True) * SCALE) for kr in ks]
        total = exps[0] + exps[1] + exps[2] + exps[3]
        probs = [e / total for e in exps]
        weights = [rounded(p) for p in probs]
        heads = sum(w * vr for w, vr in zip(weights, vs))
        gps = [jnp.sum(gh * vr, axis=0, keepdims=True) for vr in vs]
        inner = sum(p * gp for p, gp in zip(probs, gps))
        sgs = [rounded(p * (gp - inner) * SCALE) for p, gp in zip(probs, gps)]
        gq = sum(sg * kr for sg, kr in zip(sgs, ks))
        gk = sum(behind(sg * q, r) for r, sg in enumerate(sgs))
        gv = sum(behind(w * gh, r) for r, w in enumerate(weights))
        g0_ref[base : base + 2 * E] = jnp.concatenate([gq, gk], axis=0).astype(BF)
        g1_ref[base : base + 2 * E, :128] = jnp.concatenate([gv, zeros], axis=0).astype(BF)
        g1_ref[base : base + 2 * E, 128:] = jnp.concatenate([zeros, heads], axis=0).astype(BF)
    for h in range(8):
        span = slice(h * 2 * E, (h + 1) * 2 * E)
        gw_ref[0, span] = nn(g0_ref[span], hidden).astype(BF)
        gw_ref[1, span] = nn(g1_ref[span], both).astype(BF)
    stores = (
        pltpu.make_async_copy(gw_ref.at[core], keep_ref, sems.at[0]),
        pltpu.make_async_copy(gw_ref.at[1 - core], send_ref, sems.at[1]),
    )
    for store in stores:
        store.start()
    mixed = tn(g1_ref[...], w_ref[1])
    normed_grads = tn(g0_ref[...], w_ref[0]) + mixed[:128]
    result = (rows.astype(F32) + mixed[128:]).astype(BF)
    total_grad = normalize_back(grad, inverse, normed, normed_grads).astype(BF)
    for s in range(2):
        for f in range(2):
            at = slice((2 * s + f) * 32, (2 * s + f + 1) * 32)
            back_ref[s, 0, f] = result[at]
            back_ref[s, 1, f] = total_grad[at]
    for store in stores:
        store.wait()


def local_rows(pair_ref, which):
    return jnp.concatenate([pair_ref[s, which, f] for f in range(2) for s in range(2)], axis=0)


def turn_kernel(
    back_ref, heads_ref, wo_ref, keep_ref, recv_ref, gh_ref, parts_ref, out_ref, grad_ref
):
    out_ref[...] = local_rows(back_ref, 0)
    grad = local_rows(back_ref, 1)
    grad_ref[...] = grad
    gh_ref[...] = nt(wo_ref[...], grad).astype(BF)
    gw = nn(heads_ref[...], grad)
    for h in range(8):
        span = slice(h * 2 * E, (h + 1) * 2 * E)
        two = keep_ref[span].astype(F32) + recv_ref[span].astype(F32)
        parts_ref[h] = jnp.concatenate([two, gw[h * E : (h + 1) * E]], axis=0).astype(BF)


def spatial_back_kernel(qkv_ref, gh_ref, hidden_ref, w_ref, terms_ref, gw_ref):
    frames = ([], [])
    for m in range(4):
        pair = regroup(gh_ref[2 * m].astype(F32), gh_ref[2 * m + 1].astype(F32))
        for f in range(2):
            frames[f].append(pair[f])
    total = None
    for f in range(2):
        q, k, v = split3(qkv_ref[f].astype(F32))
        gh = jnp.concatenate(frames[f], axis=1).astype(BF)
        probs = softmax(q, k)
        gv = nn(gh, probs.astype(BF))
        gp = tn(gh, v)
        inner = jnp.sum(probs * gp, axis=1, keepdims=True)
        sg = (probs * (gp - inner) * SCALE).astype(BF)
        grads = jnp.concatenate([nt(k, sg), nn(q, sg), gv], axis=0).astype(BF)
        gw = nn(grads, frame_rows(hidden_ref, f))
        total = gw if total is None else total + gw
        terms = tn(grads, w_ref[...]).astype(BF)
        for j in range(8):
            terms_ref[j, f * 64 : (f + 1) * 64, :] = terms[j * 64 : (j + 1) * 64]
    gw_ref[...] = total.astype(BF)


def gather_kernel(core_ref, parts_ref, qkv_ref, two_ref, keep_ref, send_ref, halves_ref):
    core = core_ref[0]
    total = parts_ref[0].astype(F32)
    for j in range(1, 8):
        total = total + parts_ref[j].astype(F32)
    two_ref[...] = total[: 2 * E].astype(BF)
    qkv = qkv_ref[...].astype(F32)
    halves_ref[0] = qkv[: 2 * E]
    halves_ref[1] = jnp.concatenate([qkv[2 * E :], total[2 * E :]], axis=0)
    keep_ref[...] = halves_ref[core].astype(BF)
    send_ref[...] = halves_ref[1 - core].astype(BF)


def result_kernel(core_ref, mine_ref, other_ref, qkv_ref, out_ref, halves_ref):
    core = core_ref[0]
    halves_ref[core] = mine_ref[...].astype(F32)
    halves_ref[1 - core] = other_ref[...].astype(F32)
    for b in range(2):
        at = b * 2 * E
        qkv_ref[b, 0] = halves_ref[0, at : at + E]
        qkv_ref[b, 1] = halves_ref[0, at + E : at + 2 * E]
        qkv_ref[b, 2] = halves_ref[1, at : at + E]
        out_ref[b] = halves_ref[1, at + E : at + 2 * E]


def last_kernel(terms_ref, x_ref, g_ref, pass_ref, out_ref, same_ref):
    normed, inverse = normalize(x_ref[...])
    normed_grads = terms_ref[0].astype(F32)
    for j in range(1, 8):
        normed_grads = normed_grads + terms_ref[j].astype(F32)
    out_ref[...] = normalize_back(g_ref[...], inverse, normed, normed_grads).astype(BF)


VMEM = pl.BlockSpec(memory_space=pltpu.VMEM)
SMEM = pl.BlockSpec(memory_space=pltpu.SMEM)
ANY = pl.BlockSpec(memory_space=pl.ANY)
PARAMS = pltpu.CompilerParams(vmem_limit_bytes=48 * 1024 * 1024)


def shape(*dims):
    return jax.ShapeDtypeStruct(dims, BF)


def call(kernel, outs, *args, **more):
    return pl.pallas_call(
        kernel,
        out_shape=outs,
        in_specs=more.pop("in_specs", [VMEM] * len(args)),
        out_specs=more.pop("out_specs", jax.tree.map(lambda _: VMEM, outs)),
        compiler_params=PARAMS,
        **more,
    )(*args)


def over_head(blocks):
    return lax.all_to_all(blocks, "head", 0, 0, tiled=True, axis_index_groups=RING)


def over_seq(blocks):
    return lax.all_to_all(blocks, "seq", 0, 0, tiled=True)


def swap_cores(value, n_dp):
    return lax.ppermute(value, "dp", [(i, i ^ 1) for i in range(n_dp)])


def pick(stacked, at):
    return lax.dynamic_index_in_dim(stacked, at, 0, keepdims=False)


def groups_of(n_dp):
    n_z = n_dp // 2
    low = min(4, n_z)
    high = n_z // low
    near = [
        [s * n_dp + 2 * (b * low + a) + c for s in range(2) for a in range(low)]
        for b in range(high)
        for c in range(2)
    ]
    far = [
        [2 * (b * low + a) + c for b in range(high)] for a in range(low) for c in range(2)
    ]
    return near, far


def sum_near(grads, near):
    rows, depth = grads.shape
    n = len(near[0])
    parts = lax.all_to_all(
        grads.reshape(n, rows // n, depth), ("seq", "dp"), 0, 0,
        tiled=True, axis_index_groups=near,
    )
    return jnp.sum(parts.astype(F32), axis=0).astype(BF)


def sum_far(part, far):
    if len(far[0]) == 1:
        return part
    copies = jnp.broadcast_to(part[None], (len(far[0]), *part.shape))
    parts = lax.all_to_all(copies, "dp", 0, 0, tiled=True, axis_index_groups=far)
    return jnp.sum(parts.astype(F32), axis=0).astype(BF)


def spread(part, near):
    copies = jnp.broadcast_to(part[None], (len(near[0]), *part.shape))
    whole = lax.all_to_all(
        copies, ("seq", "dp"), 0, 0, tiled=True, axis_index_groups=near
    )
    return whole.reshape(len(near[0]) * part.shape[0], part.shape[1])


def on_device(n_dp, latents, cotangent, w_qkv, w_out):
    depth = latents.shape[-1]
    core = lax.axis_index("dp") % 2
    core_arg = core.reshape(1).astype(jnp.int32)
    near, far = groups_of(n_dp)
    x = latents.reshape(128, depth)
    g = cotangent.reshape(128, depth)
    w_own = w_qkv[0].reshape(3 * E, depth)

    half_two = pick(
        jnp.concatenate([w_qkv[1].reshape(3 * E, depth), w_out[1].reshape(E, depth)]).reshape(
            2, 2 * E, depth
        ),
        core,
    )
    mine_two = lax.all_gather(half_two, "head", axis_index_groups=RING).reshape(16 * E, depth)

    hidden, wo = call(
        norm_kernel, (shape(8, 128, depth), shape(8, E, depth)), x, w_out[0].reshape(E, depth)
    )
    hidden = over_head(hidden)
    wo = over_head(wo).reshape(8 * E, depth)
    heads, qkv = call(spatial_kernel, (shape(8, E, 128), shape(2, 3 * E, 512)), hidden, w_own)
    heads = over_head(heads).reshape(8 * E, 128)
    big = shape(16 * E, depth)
    pair, mine_two = call(
        middle_kernel, (shape(2, 2, 2, 32, depth), big), x, g, heads, wo, mine_two,
        in_specs=[VMEM] * 4 + [ANY],
        out_specs=(VMEM, ANY),
        input_output_aliases={4: 1},
    )
    pair = over_seq(pair)
    other_two = swap_cores(mine_two, n_dp)
    back, keep, send = call(
        temporal_kernel,
        (shape(2, 2, 2, 32, depth), big, big),
        core_arg, pair, mine_two, other_two,
        in_specs=[SMEM, VMEM, ANY, ANY],
        out_specs=(VMEM, ANY, ANY),
        scratch_shapes=[
            pltpu.VMEM((2, 16 * E, depth), BF),
            pltpu.VMEM((2, 16 * E, depth), BF),
            pltpu.VMEM((16 * E, 128), F32),
            pltpu.VMEM((16 * E, 256), F32),
            pltpu.VMEM((16 * E, 128), BF),
            pltpu.VMEM((16 * E, 256), BF),
            pltpu.SemaphoreType.DMA((2,)),
        ],
    )
    back = over_seq(back)
    gh, parts, output, grad_one = call(
        turn_kernel,
        (shape(8 * E, 128), shape(8, 3 * E, depth), shape(128, depth), shape(128, depth)),
        back, heads, wo, keep, swap_cores(send, n_dp),
    )
    gh = over_head(gh.reshape(8, E, 128))
    parts = over_head(parts)
    terms, qkv_one = call(
        spatial_back_kernel, (shape(8, 128, depth), shape(3 * E, depth)), qkv, gh, hidden, w_own
    )
    half = shape(2 * E, depth)
    two, keep, send = call(
        gather_kernel, (half, half, half), core_arg, parts, qkv_one,
        in_specs=[SMEM, VMEM, VMEM],
        scratch_shapes=[pltpu.VMEM((2, 2 * E, depth), F32)],
    )
    one = (keep.astype(F32) + swap_cores(send, n_dp).astype(F32)).astype(BF)
    part = sum_near(jnp.concatenate([one, two]), near)
    latent_grads, part = call(
        last_kernel, (shape(128, depth), shape(*part.shape)), over_head(terms), x, grad_one, part,
        in_specs=[VMEM] * 3 + [ANY],
        out_specs=(VMEM, ANY),
        input_output_aliases={3: 1},
    )
    mine = spread(sum_far(part, far), near)
    grad_qkv, grad_out = call(
        result_kernel,
        (
            jax.ShapeDtypeStruct((2, 3, E, depth), F32),
            jax.ShapeDtypeStruct((2, E, depth), F32),
        ),
        core_arg, mine, swap_cores(mine, n_dp),
        in_specs=[SMEM, VMEM, VMEM],
        scratch_shapes=[pltpu.VMEM((2, 4 * E, depth), F32)],
    )
    return (
        output.reshape(latents.shape),
        latent_grads.reshape(latents.shape),
        grad_qkv[:, None],
        grad_out[:, None],
    )


def solution(mesh):
    rows = P("dp", "seq", "head", None)
    specs = (rows, rows, P(None, "head", None, None, None), P(None, "head", None, None))
    return jax.shard_map(
        functools.partial(on_device, mesh.shape["dp"]),
        mesh=mesh, in_specs=specs, out_specs=specs, check_vma=False,
    )
```

```python
import functools

import jax
import jax.numpy as jnp
from jax import lax
from jax.experimental import pallas as pl
from jax.experimental.pallas import tpu as pltpu
from jax.sharding import PartitionSpec as P

EPSILON = 1e-06
E = 72
SCALE = E ** (-0.5)
RING = [[0, 2, 4, 6, 7, 5, 3, 1]]
BF = jnp.bfloat16
F32 = jnp.float32


def nn(a, b):
    return lax.dot_general(a, b, (((1,), (0,)), ((), ())), preferred_element_type=F32)


def nt(a, b):
    return lax.dot_general(a, b, (((1,), (1,)), ((), ())), preferred_element_type=F32)


def tn(a, b):
    return lax.dot_general(a, b, (((0,), (0,)), ((), ())), preferred_element_type=F32)


def normalize(rows):
    wide = rows.astype(F32)
    centered = wide - jnp.mean(wide, axis=-1, keepdims=True)
    inverse = lax.rsqrt(jnp.mean(centered * centered, axis=-1, keepdims=True) + EPSILON)
    return centered * inverse, inverse


def normalize_back(grad, inverse, normed, normed_grads):
    mean_grad = jnp.mean(normed_grads, axis=-1, keepdims=True)
    mean_cross = jnp.mean(normed_grads * normed, axis=-1, keepdims=True)
    return grad.astype(F32) + inverse * (normed_grads - mean_grad - normed * mean_cross)


def regroup(first, second):
    low = lax.broadcasted_iota(jnp.int32, first.shape, 1) < 64
    return (
        jnp.where(low, first, pltpu.roll(second, 64, 1)),
        jnp.where(low, pltpu.roll(first, 64, 1), second),
    )


def norm_kernel(at_ref, x_ref, wq_ref, wo_ref, out_ref, own_ref, parts_ref):
    hidden = normalize(x_ref[...])[0].astype(BF)
    for j in range(8):
        out_ref[j] = hidden
    for i in range(3):
        parts_ref[i] = wq_ref[1, i].astype(F32)
    parts_ref[3] = wo_ref[1].astype(F32)
    first = wo_ref[0].astype(F32)
    half = jnp.where(at_ref[0] == 0, first[:40], first[32:])
    part = parts_ref[2 * at_ref[0] + at_ref[1]]
    own_ref[...] = jnp.concatenate([part, half], axis=0).astype(BF)


def frame_rows(hidden_ref, f):
    return hidden_ref[:, f * 64 : (f + 1) * 64, :].reshape(512, hidden_ref.shape[2])


def softmax(queries, key_rows):
    exponent = jnp.exp(tn(queries, key_rows) * SCALE)
    return exponent / jnp.sum(exponent, axis=1, keepdims=True)


def split3(stacked):
    return tuple(stacked[i * E : (i + 1) * E].astype(BF) for i in range(3))


def spatial_kernel(hidden_ref, w_ref, all_ref, heads_ref, qkv_ref, two_ref, one_ref):
    for h in range(8):
        both = all_ref[h].astype(F32)
        two_ref[h] = both[:E].astype(BF)
        one_ref[h] = both[E:].astype(BF)
    outs = []
    for f in range(2):
        qkv = nt(w_ref[...], frame_rows(hidden_ref, f))
        qkv_ref[f] = qkv.astype(BF)
        q, k, v = split3(qkv)
        weights = softmax(q, k).astype(BF)
        outs.append(nt(v, weights))
    for m in range(4):
        lanes = slice(m * 128, (m + 1) * 128)
        a, b = regroup(outs[0][:, lanes], outs[1][:, lanes])
        heads_ref[2 * m] = a.astype(BF)
        heads_ref[2 * m + 1] = b.astype(BF)


def middle_kernel(core_ref, x_ref, g_ref, heads_ref, mine_ref, other_ref, out_ref, split_ref):
    core = core_ref[0]
    for h in range(8):
        heads = heads_ref[h].astype(F32)
        split_ref[0, h * 40 : (h + 1) * 40] = heads[:40]
        low = jnp.zeros((8, 128), F32)
        split_ref[1, h * 40 : (h + 1) * 40] = jnp.concatenate([low, heads[40:]], axis=0)
    y = x_ref[...].astype(F32) + tn(split_ref[core].astype(BF), mine_ref[...])
    y = (y + tn(split_ref[1 - core].astype(BF), other_ref[...])).astype(BF)
    g = g_ref[...]
    for s in range(2):
        for f in range(2):
            rows = slice((2 * f + s) * 32, (2 * f + s + 1) * 32)
            out_ref[s, 0, f] = y[rows]
            out_ref[s, 1, f] = g[rows]


def temporal_kernel(
    at_ref, pair_ref, own_ref, z_ref, core_ref, both_ref,
    back_ref, keep_ref, send_ref,
    w_ref, gw_ref, in_ref, grads_ref, sems,
):
    core, odd = at_ref[0], at_ref[1]
    here, there = 2 * core, 2 * (1 - core)
    loads = (
        pltpu.make_async_copy(own_ref, w_ref.at[here + odd], sems.at[0]),
        pltpu.make_async_copy(z_ref, w_ref.at[here + 1 - odd], sems.at[1]),
        pltpu.make_async_copy(core_ref, w_ref.at[there + odd], sems.at[2]),
        pltpu.make_async_copy(both_ref, w_ref.at[there + 1 - odd], sems.at[3]),
    )
    for load in loads:
        load.start()
    depth = pair_ref.shape[-1]
    rows = jnp.concatenate([pair_ref[s, 0, f] for s in range(2) for f in range(2)], axis=0)
    grad = jnp.concatenate([pair_ref[s, 1, f] for s in range(2) for f in range(2)], axis=0)
    normed, inverse = normalize(rows)
    hidden = normed.astype(BF)
    for load in loads:
        load.wait()
    for i in range(4):
        in_ref[i] = nt(w_ref[i], grad if i == 3 else hidden)

    def rounded(value):
        return value.astype(BF).astype(F32)

    def ahead(value, r):
        return pltpu.roll(value, 128 - 32 * r, 1) if r else value

    def behind(value, r):
        return pltpu.roll(value, 32 * r, 1) if r else value

    for h in range(8):
        span = slice(h * E, (h + 1) * E)
        q, k, v, gh = (rounded(in_ref[i, span]) for i in range(4))
        ks = [ahead(k, r) for r in range(4)]
        vs = [ahead(v, r) for r in range(4)]
        exps = [jnp.exp(jnp.sum(q * kr, axis=0, keepdims=True) * SCALE) for kr in ks]
        total = exps[0] + exps[1] + exps[2] + exps[3]
        probs = [e / total for e in exps]
        weights = [rounded(p) for p in probs]
        heads = sum(w * vr for w, vr in zip(weights, vs))
        gps = [jnp.sum(gh * vr, axis=0, keepdims=True) for vr in vs]
        inner = sum(p * gp for p, gp in zip(probs, gps))
        sgs = [rounded(p * (gp - inner) * SCALE) for p, gp in zip(probs, gps)]
        gq = sum(sg * kr for sg, kr in zip(sgs, ks))
        gk = sum(behind(sg * q, r) for r, sg in enumerate(sgs))
        gv = sum(behind(w * gh, r) for r, w in enumerate(weights))
        for i, grads in enumerate((gq, gk, gv, heads)):
            grads_ref[i, span] = grads
        wide = slice(h * 2 * E, (h + 1) * 2 * E)
        qk_grads = jnp.concatenate([gq, gk], axis=0).astype(BF)
        gw_ref[0, wide] = nn(qk_grads, hidden).astype(BF)
        vo_grads = [nn(gv.astype(BF), hidden), nn(heads.astype(BF), grad)]
        gw_ref[1, wide] = jnp.concatenate(vo_grads, axis=0).astype(BF)
    stores = (
        pltpu.make_async_copy(gw_ref.at[core], keep_ref, sems.at[0]),
        pltpu.make_async_copy(gw_ref.at[1 - core], send_ref, sems.at[1]),
    )
    for store in stores:
        store.start()
    sums = [tn(grads_ref[i].astype(BF), w_ref[i]) for i in range(4)]
    normed_grads = sums[0] + sums[1] + sums[2]
    result = (rows.astype(F32) + sums[3]).astype(BF)
    total_grad = normalize_back(grad, inverse, normed, normed_grads).astype(BF)
    for s in range(2):
        for f in range(2):
            at = slice((2 * s + f) * 32, (2 * s + f + 1) * 32)
            back_ref[s, 0, f] = result[at]
            back_ref[s, 1, f] = total_grad[at]
    for store in stores:
        store.wait()


def local_rows(pair_ref, which):
    return jnp.concatenate([pair_ref[s, which, f] for f in range(2) for s in range(2)], axis=0)


def turn_kernel(
    core_ref, back_ref, heads_ref, mine_ref, other_ref,
    gh_ref, gw_ref, out_ref, grad_ref, split_ref,
):
    core = core_ref[0]
    out_ref[...] = local_rows(back_ref, 0)
    grad = local_rows(back_ref, 1)
    grad_ref[...] = grad
    split_ref[core] = nt(mine_ref[...], grad)
    split_ref[1 - core] = nt(other_ref[...], grad)
    for h in range(8):
        at = h * 40
        pieces = [split_ref[0, at : at + 40], split_ref[1, at + 8 : at + 40]]
        gh_ref[h] = jnp.concatenate(pieces, axis=0).astype(BF)
        gw_ref[h] = nn(heads_ref[h], grad).astype(BF)


def spatial_back_kernel(qkv_ref, gh_ref, hidden_ref, w_ref, terms_ref, gw_ref):
    frames = ([], [])
    for m in range(4):
        pair = regroup(gh_ref[2 * m].astype(F32), gh_ref[2 * m + 1].astype(F32))
        for f in range(2):
            frames[f].append(pair[f])
    total = None
    for f in range(2):
        q, k, v = split3(qkv_ref[f].astype(F32))
        gh = jnp.concatenate(frames[f], axis=1).astype(BF)
        probs = softmax(q, k)
        gv = nn(gh, probs.astype(BF))
        gp = tn(gh, v)
        inner = jnp.sum(probs * gp, axis=1, keepdims=True)
        sg = (probs * (gp - inner) * SCALE).astype(BF)
        grads = jnp.concatenate([nt(k, sg), nn(q, sg), gv], axis=0).astype(BF)
        gw = nn(grads, frame_rows(hidden_ref, f))
        total = gw if total is None else total + gw
        terms = tn(grads, w_ref[...]).astype(BF)
        for j in range(8):
            terms_ref[j, f * 64 : (f + 1) * 64, :] = terms[j * 64 : (j + 1) * 64]
    gw_ref[...] = total.astype(BF)


def gather_kernel(core_ref, parts_ref, qkv_ref, keep_ref, send_ref, halves_ref):
    core = core_ref[0]
    total = parts_ref[0].astype(F32)
    for j in range(1, 8):
        total = total + parts_ref[j].astype(F32)
    qkv = qkv_ref[...].astype(F32)
    halves_ref[0] = qkv[: 2 * E]
    halves_ref[1] = jnp.concatenate([qkv[2 * E :], total], axis=0)
    keep_ref[...] = halves_ref[core].astype(BF)
    send_ref[...] = halves_ref[1 - core].astype(BF)


def result_kernel(core_ref, mine_ref, other_ref, qkv_ref, out_ref, halves_ref):
    core = core_ref[0]
    halves_ref[core] = mine_ref[...].astype(F32)
    halves_ref[1 - core] = other_ref[...].astype(F32)
    for b in range(2):
        at = b * 2 * E
        qkv_ref[b, 0] = halves_ref[0, at : at + E]
        qkv_ref[b, 1] = halves_ref[0, at + E : at + 2 * E]
        qkv_ref[b, 2] = halves_ref[1, at : at + E]
        out_ref[b] = halves_ref[1, at + E : at + 2 * E]


def last_kernel(
    terms_ref, x_ref, g_ref, keep_ref, recv_ref, two_ref, out_ref, chain_ref, rows_ref
):
    rows_ref[: 2 * E] = keep_ref[...].astype(F32) + recv_ref[...].astype(F32)
    rows_ref[2 * E : 4 * E] = two_ref[...].astype(F32)
    rows_ref[4 * E :] = jnp.zeros_like(rows_ref[4 * E :])
    for i in range(8):
        chain_ref[i] = rows_ref[i * 40 : (i + 1) * 40].astype(BF)
    normed, inverse = normalize(x_ref[...])
    normed_grads = terms_ref[0].astype(F32)
    for j in range(1, 8):
        normed_grads = normed_grads + terms_ref[j].astype(F32)
    out_ref[...] = normalize_back(g_ref[...], inverse, normed, normed_grads).astype(BF)


VMEM = pl.BlockSpec(memory_space=pltpu.VMEM)
SMEM = pl.BlockSpec(memory_space=pltpu.SMEM)
ANY = pl.BlockSpec(memory_space=pl.ANY)
PARAMS = pltpu.CompilerParams(vmem_limit_bytes=48 * 1024 * 1024)


def shape(*dims):
    return jax.ShapeDtypeStruct(dims, BF)


def call(kernel, outs, *args, **more):
    return pl.pallas_call(
        kernel,
        out_shape=outs,
        in_specs=more.pop("in_specs", [VMEM] * len(args)),
        out_specs=more.pop("out_specs", jax.tree.map(lambda _: VMEM, outs)),
        compiler_params=PARAMS,
        **more,
    )(*args)


def over_head(blocks):
    return lax.all_to_all(blocks, "head", 0, 0, tiled=True, axis_index_groups=RING)


def over_seq(blocks):
    return lax.all_to_all(blocks, "seq", 0, 0, tiled=True)


def swap_cores(value, n_dp, bit=1):
    return lax.ppermute(value, "dp", [(i, i ^ bit) for i in range(n_dp)])


def groups_of(n_dp):
    n_z = n_dp // 2
    low = min(4, n_z)
    high = n_z // low
    near = [
        [s * n_dp + 2 * (b * low + a) + c for s in range(2) for a in range(low)]
        for b in range(high)
        for c in range(2)
    ]
    far = [
        [2 * (b * low + a) + c for b in range(high)] for a in range(low) for c in range(2)
    ]
    return near, far


def sum_near(grads, near):
    parts = lax.all_to_all(grads, ("seq", "dp"), 0, 0, tiled=True, axis_index_groups=near)
    return jnp.sum(parts.astype(F32), axis=0).astype(BF)


def sum_far(part, far):
    if len(far[0]) == 1:
        return part
    copies = jnp.broadcast_to(part[None], (len(far[0]), *part.shape))
    parts = lax.all_to_all(copies, "dp", 0, 0, tiled=True, axis_index_groups=far)
    return jnp.sum(parts.astype(F32), axis=0).astype(BF)


def spread(part, near):
    copies = jnp.broadcast_to(part[None], (len(near[0]), *part.shape))
    whole = lax.all_to_all(
        copies, ("seq", "dp"), 0, 0, tiled=True, axis_index_groups=near
    )
    return whole.reshape(len(near[0]) * part.shape[0], part.shape[1])


def on_device(n_dp, latents, cotangent, w_qkv, w_out):
    depth = latents.shape[-1]
    index = lax.axis_index("dp")
    at = jnp.stack([index % 2, index // 2 % 2]).astype(jnp.int32)
    near, far = groups_of(n_dp)
    x = latents.reshape(128, depth)
    g = cotangent.reshape(128, depth)
    w_own = w_qkv[0].reshape(3 * E, depth)

    hidden, own = call(
        norm_kernel, (shape(8, 128, depth), shape(E + 40, depth)),
        at, x, w_qkv.reshape(2, 3, E, depth), w_out.reshape(2, E, depth),
        in_specs=[SMEM] + [VMEM] * 3,
        scratch_shapes=[pltpu.VMEM((4, E, depth), F32)],
    )
    parts = lax.all_gather(own, "head", axis_index_groups=RING)
    hidden = over_head(hidden)
    heads, qkv, own, mine_one = call(
        spatial_kernel,
        (shape(8, E, 128), shape(2, 3 * E, 512), shape(8, E, depth), shape(8, 40, depth)),
        hidden, w_own, parts,
    )
    heads = over_head(heads)
    mine_one = mine_one.reshape(320, depth)
    other_one = swap_cores(mine_one, n_dp)
    own = own.reshape(8 * E, depth)
    from_z = swap_cores(own, n_dp, 2)
    from_core = swap_cores(own, n_dp)
    from_both = swap_cores(from_z, n_dp)
    pair = call(
        middle_kernel, shape(2, 2, 2, 32, depth), at, x, g, heads, mine_one, other_one,
        in_specs=[SMEM] + [VMEM] * 5,
        scratch_shapes=[pltpu.VMEM((2, 320, 128), F32)],
    )
    pair = over_seq(pair)
    big = shape(16 * E, depth)
    back, keep, send = call(
        temporal_kernel,
        (shape(2, 2, 2, 32, depth), big, big),
        at, pair, own, from_z, from_core, from_both,
        in_specs=[SMEM, VMEM] + [ANY] * 4,
        out_specs=(VMEM, ANY, ANY),
        scratch_shapes=[
            pltpu.VMEM((4, 8 * E, depth), BF),
            pltpu.VMEM((2, 16 * E, depth), BF),
            pltpu.VMEM((4, 8 * E, 128), F32),
            pltpu.VMEM((4, 8 * E, 128), F32),
            pltpu.SemaphoreType.DMA((4,)),
        ],
    )
    back = over_seq(back)
    two = (keep.astype(F32) + swap_cores(send, n_dp).astype(F32)).astype(BF)
    two = lax.psum_scatter(
        two, "head", scatter_dimension=0, tiled=True, axis_index_groups=RING
    )
    gh, parts, output, grad_one = call(
        turn_kernel,
        (shape(8, E, 128), shape(8, E, depth), shape(128, depth), shape(128, depth)),
        at, back, heads, mine_one, other_one,
        in_specs=[SMEM] + [VMEM] * 4,
        scratch_shapes=[pltpu.VMEM((2, 320, 128), F32)],
    )
    gh = over_head(gh)
    parts = over_head(parts)
    terms, qkv_one = call(
        spatial_back_kernel, (shape(8, 128, depth), shape(3 * E, depth)), qkv, gh, hidden, w_own
    )
    half = shape(2 * E, depth)
    keep, send = call(
        gather_kernel, (half, half), at, parts, qkv_one,
        in_specs=[SMEM, VMEM, VMEM],
        scratch_shapes=[pltpu.VMEM((2, 2 * E, depth), F32)],
    )
    n_near = len(near[0])
    latent_grads, chain = call(
        last_kernel, (shape(128, depth), shape(n_near, 320 // n_near, depth)),
        over_head(terms), x, grad_one, keep, swap_cores(send, n_dp), two,
        scratch_shapes=[pltpu.VMEM((320, depth), F32)],
    )
    part = sum_near(chain, near)
    mine = spread(sum_far(part, far), near)
    grad_qkv, grad_out = call(
        result_kernel,
        (
            jax.ShapeDtypeStruct((2, 3, E, depth), F32),
            jax.ShapeDtypeStruct((2, E, depth), F32),
        ),
        at, mine, swap_cores(mine, n_dp),
        in_specs=[SMEM, VMEM, VMEM],
        scratch_shapes=[pltpu.VMEM((2, 320, depth), F32)],
    )
    return (
        output.reshape(latents.shape),
        latent_grads.reshape(latents.shape),
        grad_qkv[:, None],
        grad_out[:, None],
    )


def solution(mesh):
    rows = P("dp", "seq", "head", None)
    specs = (rows, rows, P(None, "head", None, None, None), P(None, "head", None, None))
    return jax.shard_map(
        functools.partial(on_device, mesh.shape["dp"]),
        mesh=mesh, in_specs=specs, out_specs=specs, check_vma=False,
    )
```

```python
import functools

import jax
import jax.numpy as jnp
from jax import lax
from jax.experimental import pallas as pl
from jax.experimental.pallas import tpu as pltpu
from jax.sharding import PartitionSpec as P

EPSILON = 1e-06
E = 72
SCALE = E ** (-0.5)
RING = [[0, 2, 4, 6, 7, 5, 3, 1]]
BF = jnp.bfloat16
F32 = jnp.float32


def nn(a, b):
    return lax.dot_general(a, b, (((1,), (0,)), ((), ())), preferred_element_type=F32)


def nt(a, b):
    return lax.dot_general(a, b, (((1,), (1,)), ((), ())), preferred_element_type=F32)


def tn(a, b):
    return lax.dot_general(a, b, (((0,), (0,)), ((), ())), preferred_element_type=F32)


def normalize(rows):
    wide = rows.astype(F32)
    centered = wide - jnp.mean(wide, axis=-1, keepdims=True)
    inverse = lax.rsqrt(jnp.mean(centered * centered, axis=-1, keepdims=True) + EPSILON)
    return centered * inverse, inverse


def normalize_back(grad, inverse, normed, normed_grads):
    mean_grad = jnp.mean(normed_grads, axis=-1, keepdims=True)
    mean_cross = jnp.mean(normed_grads * normed, axis=-1, keepdims=True)
    return grad.astype(F32) + inverse * (normed_grads - mean_grad - normed * mean_cross)


def regroup(first, second):
    low = lax.broadcasted_iota(jnp.int32, first.shape, 1) < 64
    return (
        jnp.where(low, first, pltpu.roll(second, 64, 1)),
        jnp.where(low, pltpu.roll(first, 64, 1), second),
    )


def norm_kernel(at_ref, x_ref, wq_ref, wo_ref, out_ref, own_ref):
    core = at_ref[0]
    wide = wo_ref[0].astype(F32)
    half = jnp.where(core == 0, wide[:40], wide[32:])
    hidden = normalize(x_ref[...])[0]
    block = jnp.concatenate([hidden, half], axis=0).astype(BF)
    for j in range(8):
        out_ref[j] = block
    qk = jnp.concatenate([wq_ref[1, 0].astype(F32), wq_ref[1, 1].astype(F32)], axis=0)
    vo = jnp.concatenate([wq_ref[1, 2].astype(F32), wo_ref[1].astype(F32)], axis=0)
    own_ref[...] = jnp.where(core == 0, qk, vo).astype(BF)


def frame_rows(hidden_ref, f):
    return hidden_ref[:, f * 64 : (f + 1) * 64, :].reshape(512, hidden_ref.shape[2])


def softmax(queries, key_rows):
    exponent = jnp.exp(tn(queries, key_rows) * SCALE)
    return exponent / jnp.sum(exponent, axis=1, keepdims=True)


def split3(stacked):
    return tuple(stacked[i * E : (i + 1) * E].astype(BF) for i in range(3))


def spatial_kernel(hidden_ref, w_ref, heads_ref, qkv_ref, one_ref):
    for h in range(8):
        one_ref[h] = hidden_ref[h].astype(F32)[128:].astype(BF)
    outs = []
    for f in range(2):
        qkv = nt(w_ref[...], frame_rows(hidden_ref, f))
        qkv_ref[f] = qkv.astype(BF)
        q, k, v = split3(qkv)
        weights = softmax(q, k).astype(BF)
        outs.append(nt(v, weights))
    for m in range(4):
        lanes = slice(m * 128, (m + 1) * 128)
        a, b = regroup(outs[0][:, lanes], outs[1][:, lanes])
        heads_ref[2 * m] = a.astype(BF)
        heads_ref[2 * m + 1] = b.astype(BF)


def middle_kernel(
    core_ref, x_ref, g_ref, heads_ref, mine_ref, other_ref, pass_ref, out_ref, same_ref, split_ref
):
    core = core_ref[0]
    for h in range(8):
        heads = heads_ref[h].astype(F32)
        split_ref[0, h * 40 : (h + 1) * 40] = heads[:40]
        low = jnp.zeros((8, 128), F32)
        split_ref[1, h * 40 : (h + 1) * 40] = jnp.concatenate([low, heads[40:]], axis=0)
    y = x_ref[...].astype(F32) + tn(split_ref[core].astype(BF), mine_ref[...])
    y = (y + tn(split_ref[1 - core].astype(BF), other_ref[...])).astype(BF)
    g = g_ref[...]
    for s in range(2):
        for f in range(2):
            rows = slice((2 * f + s) * 32, (2 * f + s + 1) * 32)
            out_ref[s, 0, f] = y[rows]
            out_ref[s, 1, f] = g[rows]


def temporal_kernel(
    core_ref, pair_ref, mine_ref, other_ref,
    back_ref, keep_ref, send_ref,
    w_ref, gw_ref, qk_ref, vg_ref, g0_ref, g1_ref, sems,
):
    core = core_ref[0]
    loads = (
        pltpu.make_async_copy(mine_ref, w_ref.at[core], sems.at[0]),
        pltpu.make_async_copy(other_ref, w_ref.at[1 - core], sems.at[1]),
    )
    for load in loads:
        load.start()
    depth = pair_ref.shape[-1]
    rows = jnp.concatenate([pair_ref[s, 0, f] for s in range(2) for f in range(2)], axis=0)
    grad = jnp.concatenate([pair_ref[s, 1, f] for s in range(2) for f in range(2)], axis=0)
    normed, inverse = normalize(rows)
    hidden = normed.astype(BF)
    both = jnp.concatenate([hidden, grad], axis=0)
    for load in loads:
        load.wait()
    qk_ref[...] = nt(w_ref[0], hidden)
    vg_ref[...] = nt(w_ref[1], both)

    def rounded(value):
        return value.astype(BF).astype(F32)

    def ahead(value, r):
        return pltpu.roll(value, 128 - 32 * r, 1) if r else value

    def behind(value, r):
        return pltpu.roll(value, 32 * r, 1) if r else value

    zeros = jnp.zeros((E, 128), F32)
    for h in range(8):
        base = h * 2 * E
        q = rounded(qk_ref[base : base + E])
        k = rounded(qk_ref[base + E : base + 2 * E])
        v = rounded(vg_ref[base : base + E, :128])
        gh = rounded(vg_ref[base + E : base + 2 * E, 128:])
        ks = [ahead(k, r) for r in range(4)]
        vs = [ahead(v, r) for r in range(4)]
        exps = [jnp.exp(jnp.sum(q * kr, axis=0, keepdims=True) * SCALE) for kr in ks]
        total = exps[0] + exps[1] + exps[2] + exps[3]
        probs = [e / total for e in exps]
        weights = [rounded(p) for p in probs]
        heads = sum(w * vr for w, vr in zip(weights, vs))
        gps = [jnp.sum(gh * vr, axis=0, keepdims=True) for vr in vs]
        inner = sum(p * gp for p, gp in zip(probs, gps))
        sgs = [rounded(p * (gp - inner) * SCALE) for p, gp in zip(probs, gps)]
        gq = sum(sg * kr for sg, kr in zip(sgs, ks))
        gk = sum(behind(sg * q, r) for r, sg in enumerate(sgs))
        gv = sum(behind(w * gh, r) for r, w in enumerate(weights))
        g0_ref[base : base + 2 * E] = jnp.concatenate([gq, gk], axis=0).astype(BF)
        g1_ref[base : base + 2 * E, :128] = jnp.concatenate([gv, zeros], axis=0).astype(BF)
        g1_ref[base : base + 2 * E, 128:] = jnp.concatenate([zeros, heads], axis=0).astype(BF)
    for h in range(8):
        span = slice(h * 2 * E, (h + 1) * 2 * E)
        gw_ref[0, span] = nn(g0_ref[span], hidden).astype(BF)
        gw_ref[1, span] = nn(g1_ref[span], both).astype(BF)
    stores = (
        pltpu.make_async_copy(gw_ref.at[core], keep_ref, sems.at[0]),
        pltpu.make_async_copy(gw_ref.at[1 - core], send_ref, sems.at[1]),
    )
    for store in stores:
        store.start()
    mixed = tn(g1_ref[...], w_ref[1])
    normed_grads = tn(g0_ref[...], w_ref[0]) + mixed[:128]
    result = (rows.astype(F32) + mixed[128:]).astype(BF)
    total_grad = normalize_back(grad, inverse, normed, normed_grads).astype(BF)
    for s in range(2):
        for f in range(2):
            at = slice((2 * s + f) * 32, (2 * s + f + 1) * 32)
            back_ref[s, 0, f] = result[at]
            back_ref[s, 1, f] = total_grad[at]
    for store in stores:
        store.wait()


def halves(rows, size):
    return rows[:size], rows[rows.shape[0] - size :]


def local_rows(pair_ref, which):
    return jnp.concatenate([pair_ref[s, which, f] for f in range(2) for s in range(2)], axis=0)


def turn_kernel(
    core_ref, back_ref, heads_ref, mine_ref, other_ref,
    gh_ref, keep_ref, send_ref, out_ref, grad_ref, split_ref,
):
    core = core_ref[0]
    out_ref[...] = local_rows(back_ref, 0)
    grad = local_rows(back_ref, 1)
    grad_ref[...] = grad
    split_ref[core] = nt(mine_ref[...], grad)
    split_ref[1 - core] = nt(other_ref[...], grad)
    for h in range(8):
        at = h * 40
        pieces = [split_ref[0, at : at + 40], split_ref[1, at + 8 : at + 40]]
        gh_ref[h] = jnp.concatenate(pieces, axis=0).astype(BF)
        low, high = halves(nn(heads_ref[h], grad), 40)
        keep_ref[h] = jnp.where(core == 0, low, high).astype(BF)
        send_ref[h] = jnp.where(core == 0, high, low).astype(BF)


def spatial_back_kernel(
    core_ref, qkv_ref, gh_ref, hidden_ref, w_ref, mine_ref, recv_ref, terms_ref, keep_ref, send_ref
):
    for j in range(8):
        part = mine_ref[j].astype(F32) + recv_ref[j].astype(F32)
        low = jnp.zeros((8, part.shape[1]), F32)
        terms_ref[j, 128:176, :] = jnp.concatenate([part, low], axis=0).astype(BF)
    frames = ([], [])
    for m in range(4):
        pair = regroup(gh_ref[2 * m].astype(F32), gh_ref[2 * m + 1].astype(F32))
        for f in range(2):
            frames[f].append(pair[f])
    total = None
    for f in range(2):
        q, k, v = split3(qkv_ref[f].astype(F32))
        gh = jnp.concatenate(frames[f], axis=1).astype(BF)
        probs = softmax(q, k)
        gv = nn(gh, probs.astype(BF))
        gp = tn(gh, v)
        inner = jnp.sum(probs * gp, axis=1, keepdims=True)
        sg = (probs * (gp - inner) * SCALE).astype(BF)
        grads = jnp.concatenate([nt(k, sg), nn(q, sg), gv], axis=0).astype(BF)
        gw = nn(grads, frame_rows(hidden_ref, f))
        total = gw if total is None else total + gw
        terms = tn(grads, w_ref[...]).astype(BF)
        for j in range(8):
            terms_ref[j, f * 64 : (f + 1) * 64, :] = terms[j * 64 : (j + 1) * 64]
    low, high = halves(total, 112)
    keep_ref[...] = jnp.where(core_ref[0] == 0, low, high).astype(BF)
    send_ref[...] = jnp.where(core_ref[0] == 0, high, low).astype(BF)


def result_kernel(core_ref, mine_ref, other_ref, qkv_ref, out_ref, both_ref):
    core = core_ref[0]
    both_ref[core] = mine_ref[...].astype(F32)
    both_ref[1 - core] = other_ref[...].astype(F32)
    qkv = jnp.concatenate([both_ref[0, :112], both_ref[1, 8:112]], axis=0)
    for i in range(3):
        qkv_ref[0, i] = qkv[i * E : (i + 1) * E]
    out_ref[0] = jnp.concatenate([both_ref[0, 112:152], both_ref[1, 120:152]], axis=0)
    qkv_ref[1, 0] = both_ref[0, 152 : 152 + E]
    qkv_ref[1, 1] = both_ref[0, 152 + E : 152 + 2 * E]
    qkv_ref[1, 2] = both_ref[1, 152 : 152 + E]
    out_ref[1] = both_ref[1, 152 + E : 152 + 2 * E]


def last_kernel(
    terms_ref, x_ref, g_ref, keep_ref, recv_ref, two_ref, out_ref, chain_ref, rows_ref
):
    rows_ref[:112] = keep_ref[...].astype(F32) + recv_ref[...].astype(F32)
    total = terms_ref[0].astype(F32)
    for j in range(1, 8):
        total = total + terms_ref[j].astype(F32)
    rows_ref[112:152] = total[128:168]
    rows_ref[152:296] = two_ref[...].astype(F32)
    rows_ref[296:] = jnp.zeros_like(rows_ref[296:])
    for i in range(8):
        chain_ref[i] = rows_ref[i * 40 : (i + 1) * 40].astype(BF)
    normed, inverse = normalize(x_ref[...])
    out_ref[...] = normalize_back(g_ref[...], inverse, normed, total[:128]).astype(BF)


VMEM = pl.BlockSpec(memory_space=pltpu.VMEM)
SMEM = pl.BlockSpec(memory_space=pltpu.SMEM)
ANY = pl.BlockSpec(memory_space=pl.ANY)
PARAMS = pltpu.CompilerParams(vmem_limit_bytes=48 * 1024 * 1024)


def shape(*dims):
    return jax.ShapeDtypeStruct(dims, BF)


def call(kernel, outs, *args, **more):
    return pl.pallas_call(
        kernel,
        out_shape=outs,
        in_specs=more.pop("in_specs", [VMEM] * len(args)),
        out_specs=more.pop("out_specs", jax.tree.map(lambda _: VMEM, outs)),
        compiler_params=PARAMS,
        cost_estimate=pl.CostEstimate(flops=0, bytes_accessed=0, transcendentals=0),
        **more,
    )(*args)


def over_head(blocks):
    return lax.all_to_all(blocks, "head", 0, 0, tiled=True, axis_index_groups=RING)


def over_seq(blocks):
    return lax.all_to_all(blocks, "seq", 0, 0, tiled=True)


def swap_cores(value, n_dp, bit=1):
    return lax.ppermute(value, "dp", [(i, i ^ bit) for i in range(n_dp)])


def groups_of(n_dp):
    n_z = n_dp // 2
    low = min(4, n_z)
    high = n_z // low
    near = [
        [s * n_dp + 2 * (b * low + a) + c for s in range(2) for a in range(low)]
        for b in range(high)
        for c in range(2)
    ]
    far = [
        [2 * (b * low + a) + c for b in range(high)] for a in range(low) for c in range(2)
    ]
    return near, far


def sum_near(grads, near):
    parts = lax.all_to_all(grads, ("seq", "dp"), 0, 0, tiled=True, axis_index_groups=near)
    return jnp.sum(parts.astype(F32), axis=0).astype(BF)


def sum_far(part, far):
    if len(far[0]) == 1:
        return part
    copies = jnp.broadcast_to(part[None], (len(far[0]), *part.shape))
    parts = lax.all_to_all(copies, "dp", 0, 0, tiled=True, axis_index_groups=far)
    return jnp.sum(parts.astype(F32), axis=0).astype(BF)


def spread(part, near):
    copies = jnp.broadcast_to(part[None], (len(near[0]), *part.shape))
    whole = lax.all_to_all(
        copies, ("seq", "dp"), 0, 0, tiled=True, axis_index_groups=near
    )
    return whole.reshape(len(near[0]) * part.shape[0], part.shape[1])


def on_device(n_dp, latents, cotangent, w_qkv, w_out):
    depth = latents.shape[-1]
    at = (lax.axis_index("dp") % 2).reshape(1).astype(jnp.int32)
    near, far = groups_of(n_dp)
    x = latents.reshape(128, depth)
    g = cotangent.reshape(128, depth)
    w_own = w_qkv[0].reshape(3 * E, depth)

    hidden, own = call(
        norm_kernel, (shape(8, 168, depth), shape(2 * E, depth)),
        at, x, w_qkv.reshape(2, 3, E, depth), w_out.reshape(2, E, depth),
        in_specs=[SMEM] + [VMEM] * 3,
    )
    mine_two = lax.all_gather(own, "head", axis_index_groups=RING).reshape(16 * E, depth)
    hidden = over_head(hidden)
    heads, qkv, mine_one = call(
        spatial_kernel,
        (shape(8, E, 128), shape(2, 3 * E, 512), shape(8, 40, depth)), hidden, w_own,
    )
    heads = over_head(heads)
    mine_one = mine_one.reshape(320, depth)
    other_one = swap_cores(mine_one, n_dp)
    big = shape(16 * E, depth)
    pair, mine_two = call(
        middle_kernel, (shape(2, 2, 2, 32, depth), big),
        at, x, g, heads, mine_one, other_one, mine_two,
        in_specs=[SMEM] + [VMEM] * 5 + [ANY],
        out_specs=(VMEM, ANY),
        input_output_aliases={6: 1},
        scratch_shapes=[pltpu.VMEM((2, 320, 128), F32)],
    )
    pair = over_seq(pair)
    other_two = swap_cores(mine_two, n_dp)
    back, keep, send = call(
        temporal_kernel,
        (shape(2, 2, 2, 32, depth), big, big),
        at, pair, mine_two, other_two,
        in_specs=[SMEM, VMEM, ANY, ANY],
        out_specs=(VMEM, ANY, ANY),
        scratch_shapes=[
            pltpu.VMEM((2, 16 * E, depth), BF),
            pltpu.VMEM((2, 16 * E, depth), BF),
            pltpu.VMEM((16 * E, 128), F32),
            pltpu.VMEM((16 * E, 256), F32),
            pltpu.VMEM((16 * E, 128), BF),
            pltpu.VMEM((16 * E, 256), BF),
            pltpu.SemaphoreType.DMA((2,)),
        ],
    )
    back = over_seq(back)
    two = (keep.astype(F32) + swap_cores(send, n_dp).astype(F32)).astype(BF)
    two = lax.psum_scatter(
        two, "head", scatter_dimension=0, tiled=True, axis_index_groups=RING
    )
    half = shape(8, 40, depth)
    gh, keep, send, output, grad_one = call(
        turn_kernel,
        (shape(8, E, 128), half, half, shape(128, depth), shape(128, depth)),
        at, back, heads, mine_one, other_one,
        in_specs=[SMEM] + [VMEM] * 4,
        scratch_shapes=[pltpu.VMEM((2, 320, 128), F32)],
    )
    gh = over_head(gh)
    half = shape(112, depth)
    terms, keep, send = call(
        spatial_back_kernel, (shape(8, 176, depth), half, half),
        at, qkv, gh, hidden, w_own, keep, swap_cores(send, n_dp),
        in_specs=[SMEM] + [VMEM] * 6,
    )
    n_near = len(near[0])
    latent_grads, chain = call(
        last_kernel, (shape(128, depth), shape(n_near, 320 // n_near, depth)),
        over_head(terms), x, grad_one, keep, swap_cores(send, n_dp), two,
        scratch_shapes=[pltpu.VMEM((320, depth), F32)],
    )
    part = sum_near(chain, near)
    mine = spread(sum_far(part, far), near)
    grad_qkv, grad_out = call(
        result_kernel,
        (
            jax.ShapeDtypeStruct((2, 3, E, depth), F32),
            jax.ShapeDtypeStruct((2, E, depth), F32),
        ),
        at, mine, swap_cores(mine, n_dp),
        in_specs=[SMEM, VMEM, VMEM],
        scratch_shapes=[pltpu.VMEM((2, 320, depth), F32)],
    )
    return (
        output.reshape(latents.shape),
        latent_grads.reshape(latents.shape),
        grad_qkv[:, None],
        grad_out[:, None],
    )


def solution(mesh):
    rows = P("dp", "seq", "head", None)
    specs = (rows, rows, P(None, "head", None, None, None), P(None, "head", None, None))
    return jax.shard_map(
        functools.partial(on_device, mesh.shape["dp"]),
        mesh=mesh, in_specs=specs, out_specs=specs, check_vma=False,
    )
```

```python
import functools

import jax
import jax.numpy as jnp
from jax import lax
from jax.experimental import pallas as pl
from jax.experimental.pallas import tpu as pltpu
from jax.sharding import PartitionSpec as P

EPSILON = 1e-06
E = 72
SCALE = E ** (-0.5)
RING = [[0, 2, 4, 6, 7, 5, 3, 1]]
BF = jnp.bfloat16
F32 = jnp.float32


def nn(a, b):
    return lax.dot_general(a, b, (((1,), (0,)), ((), ())), preferred_element_type=F32)


def nt(a, b):
    return lax.dot_general(a, b, (((1,), (1,)), ((), ())), preferred_element_type=F32)


def tn(a, b):
    return lax.dot_general(a, b, (((0,), (0,)), ((), ())), preferred_element_type=F32)


def normalize(rows):
    wide = rows.astype(F32)
    centered = wide - jnp.mean(wide, axis=-1, keepdims=True)
    inverse = lax.rsqrt(jnp.mean(centered * centered, axis=-1, keepdims=True) + EPSILON)
    return centered * inverse, inverse


def normalize_back(grad, inverse, normed, normed_grads):
    mean_grad = jnp.mean(normed_grads, axis=-1, keepdims=True)
    mean_cross = jnp.mean(normed_grads * normed, axis=-1, keepdims=True)
    return grad.astype(F32) + inverse * (normed_grads - mean_grad - normed * mean_cross)


def regroup(first, second):
    low = lax.broadcasted_iota(jnp.int32, first.shape, 1) < 64
    return (
        jnp.where(low, first, pltpu.roll(second, 64, 1)),
        jnp.where(low, pltpu.roll(first, 64, 1), second),
    )


def norm_kernel(at_ref, x_ref, wq_ref, wo_ref, out_ref, own_ref, parts_ref):
    wide = wo_ref[0].astype(F32)
    half = jnp.where(at_ref[0] == 0, wide[:40], wide[32:])
    hidden = normalize(x_ref[...])[0]
    block = jnp.concatenate([hidden, half], axis=0).astype(BF)
    for j in range(8):
        out_ref[j] = block
    for i in range(3):
        parts_ref[i] = wq_ref[1, i].astype(F32)
    parts_ref[3] = wo_ref[1].astype(F32)
    own_ref[...] = parts_ref[2 * at_ref[0] + at_ref[1]].astype(BF)


def frame_rows(hidden_ref, f):
    return hidden_ref[:, f * 64 : (f + 1) * 64, :].reshape(512, hidden_ref.shape[2])


def softmax(queries, key_rows):
    exponent = jnp.exp(tn(queries, key_rows) * SCALE)
    return exponent / jnp.sum(exponent, axis=1, keepdims=True)


def split3(stacked):
    return tuple(stacked[i * E : (i + 1) * E].astype(BF) for i in range(3))


def spatial_kernel(hidden_ref, w_ref, heads_ref, qkv_ref, one_ref):
    for h in range(8):
        one_ref[h] = hidden_ref[h].astype(F32)[128:].astype(BF)
    outs = []
    for f in range(2):
        qkv = nt(w_ref[...], frame_rows(hidden_ref, f))
        qkv_ref[f] = qkv.astype(BF)
        q, k, v = split3(qkv)
        weights = softmax(q, k).astype(BF)
        outs.append(nt(v, weights))
    for m in range(4):
        lanes = slice(m * 128, (m + 1) * 128)
        a, b = regroup(outs[0][:, lanes], outs[1][:, lanes])
        heads_ref[2 * m] = a.astype(BF)
        heads_ref[2 * m + 1] = b.astype(BF)


def middle_kernel(
    core_ref, x_ref, g_ref, heads_ref, mine_ref, other_ref, pass_ref, out_ref, same_ref, split_ref
):
    core = core_ref[0]
    for h in range(8):
        heads = heads_ref[h].astype(F32)
        split_ref[0, h * 40 : (h + 1) * 40] = heads[:40]
        low = jnp.zeros((8, 128), F32)
        split_ref[1, h * 40 : (h + 1) * 40] = jnp.concatenate([low, heads[40:]], axis=0)
    y = x_ref[...].astype(F32) + tn(split_ref[core].astype(BF), mine_ref[...])
    y = (y + tn(split_ref[1 - core].astype(BF), other_ref[...])).astype(BF)
    g = g_ref[...]
    for s in range(2):
        for f in range(2):
            rows = slice((2 * f + s) * 32, (2 * f + s + 1) * 32)
            out_ref[s, 0, f] = y[rows]
            out_ref[s, 1, f] = g[rows]


def temporal_kernel(
    at_ref, pair_ref, own_ref, z_ref, core_ref, both_ref,
    back_ref, keep_ref, send_ref,
    w_ref, gw_ref, in_ref, grads_ref, sems,
):
    core, odd = at_ref[0], at_ref[1]
    here, there = 2 * core, 2 * (1 - core)
    loads = (
        pltpu.make_async_copy(own_ref, w_ref.at[here + odd], sems.at[0]),
        pltpu.make_async_copy(z_ref, w_ref.at[here + 1 - odd], sems.at[1]),
        pltpu.make_async_copy(core_ref, w_ref.at[there + odd], sems.at[2]),
        pltpu.make_async_copy(both_ref, w_ref.at[there + 1 - odd], sems.at[3]),
    )
    for load in loads:
        load.start()
    depth = pair_ref.shape[-1]
    rows = jnp.concatenate([pair_ref[s, 0, f] for s in range(2) for f in range(2)], axis=0)
    grad = jnp.concatenate([pair_ref[s, 1, f] for s in range(2) for f in range(2)], axis=0)
    normed, inverse = normalize(rows)
    hidden = normed.astype(BF)
    for load in loads:
        load.wait()
    for i in range(4):
        in_ref[i] = nt(w_ref[i], grad if i == 3 else hidden)

    def rounded(value):
        return value.astype(BF).astype(F32)

    def ahead(value, r):
        return pltpu.roll(value, 128 - 32 * r, 1) if r else value

    def behind(value, r):
        return pltpu.roll(value, 32 * r, 1) if r else value

    for h in range(8):
        span = slice(h * E, (h + 1) * E)
        q, k, v, gh = (rounded(in_ref[i, span]) for i in range(4))
        ks = [ahead(k, r) for r in range(4)]
        vs = [ahead(v, r) for r in range(4)]
        exps = [jnp.exp(jnp.sum(q * kr, axis=0, keepdims=True) * SCALE) for kr in ks]
        total = exps[0] + exps[1] + exps[2] + exps[3]
        probs = [e / total for e in exps]
        weights = [rounded(p) for p in probs]
        heads = sum(w * vr for w, vr in zip(weights, vs))
        gps = [jnp.sum(gh * vr, axis=0, keepdims=True) for vr in vs]
        inner = sum(p * gp for p, gp in zip(probs, gps))
        sgs = [rounded(p * (gp - inner) * SCALE) for p, gp in zip(probs, gps)]
        gq = sum(sg * kr for sg, kr in zip(sgs, ks))
        gk = sum(behind(sg * q, r) for r, sg in enumerate(sgs))
        gv = sum(behind(w * gh, r) for r, w in enumerate(weights))
        for i, grads in enumerate((gq, gk, gv, heads)):
            grads_ref[i, span] = grads
        wide = slice(h * 2 * E, (h + 1) * 2 * E)
        qk_grads = jnp.concatenate([gq, gk], axis=0).astype(BF)
        gw_ref[0, wide] = nn(qk_grads, hidden).astype(BF)
        vo_grads = [nn(gv.astype(BF), hidden), nn(heads.astype(BF), grad)]
        gw_ref[1, wide] = jnp.concatenate(vo_grads, axis=0).astype(BF)
    stores = (
        pltpu.make_async_copy(gw_ref.at[core], keep_ref, sems.at[0]),
        pltpu.make_async_copy(gw_ref.at[1 - core], send_ref, sems.at[1]),
    )
    for store in stores:
        store.start()
    sums = [tn(grads_ref[i].astype(BF), w_ref[i]) for i in range(4)]
    normed_grads = sums[0] + sums[1] + sums[2]
    result = (rows.astype(F32) + sums[3]).astype(BF)
    total_grad = normalize_back(grad, inverse, normed, normed_grads).astype(BF)
    for s in range(2):
        for f in range(2):
            at = slice((2 * s + f) * 32, (2 * s + f + 1) * 32)
            back_ref[s, 0, f] = result[at]
            back_ref[s, 1, f] = total_grad[at]
    for store in stores:
        store.wait()


def halves(rows, size):
    return rows[:size], rows[rows.shape[0] - size :]


def local_rows(pair_ref, which):
    return jnp.concatenate([pair_ref[s, which, f] for f in range(2) for s in range(2)], axis=0)


def turn_kernel(
    core_ref, back_ref, heads_ref, mine_ref, other_ref,
    gh_ref, keep_ref, send_ref, out_ref, grad_ref, split_ref,
):
    core = core_ref[0]
    out_ref[...] = local_rows(back_ref, 0)
    grad = local_rows(back_ref, 1)
    grad_ref[...] = grad
    split_ref[core] = nt(mine_ref[...], grad)
    split_ref[1 - core] = nt(other_ref[...], grad)
    for h in range(8):
        at = h * 40
        pieces = [split_ref[0, at : at + 40], split_ref[1, at + 8 : at + 40]]
        gh_ref[h] = jnp.concatenate(pieces, axis=0).astype(BF)
        low, high = halves(nn(heads_ref[h], grad), 40)
        keep_ref[h] = jnp.where(core == 0, low, high).astype(BF)
        send_ref[h] = jnp.where(core == 0, high, low).astype(BF)


def spatial_back_kernel(
    core_ref, qkv_ref, gh_ref, hidden_ref, w_ref, mine_ref, recv_ref, terms_ref, keep_ref, send_ref
):
    for j in range(8):
        part = mine_ref[j].astype(F32) + recv_ref[j].astype(F32)
        low = jnp.zeros((8, part.shape[1]), F32)
        terms_ref[j, 128:176, :] = jnp.concatenate([part, low], axis=0).astype(BF)
    frames = ([], [])
    for m in range(4):
        pair = regroup(gh_ref[2 * m].astype(F32), gh_ref[2 * m + 1].astype(F32))
        for f in range(2):
            frames[f].append(pair[f])
    total = None
    for f in range(2):
        q, k, v = split3(qkv_ref[f].astype(F32))
        gh = jnp.concatenate(frames[f], axis=1).astype(BF)
        probs = softmax(q, k)
        gv = nn(gh, probs.astype(BF))
        gp = tn(gh, v)
        inner = jnp.sum(probs * gp, axis=1, keepdims=True)
        sg = (probs * (gp - inner) * SCALE).astype(BF)
        grads = jnp.concatenate([nt(k, sg), nn(q, sg), gv], axis=0).astype(BF)
        gw = nn(grads, frame_rows(hidden_ref, f))
        total = gw if total is None else total + gw
        terms = tn(grads, w_ref[...]).astype(BF)
        for j in range(8):
            terms_ref[j, f * 64 : (f + 1) * 64, :] = terms[j * 64 : (j + 1) * 64]
    low, high = halves(total, 112)
    keep_ref[...] = jnp.where(core_ref[0] == 0, low, high).astype(BF)
    send_ref[...] = jnp.where(core_ref[0] == 0, high, low).astype(BF)


def result_kernel(core_ref, mine_ref, other_ref, qkv_ref, out_ref, both_ref):
    core = core_ref[0]
    both_ref[core] = mine_ref[...].astype(F32)
    both_ref[1 - core] = other_ref[...].astype(F32)
    qkv = jnp.concatenate([both_ref[0, :112], both_ref[1, 8:112]], axis=0)
    for i in range(3):
        qkv_ref[0, i] = qkv[i * E : (i + 1) * E]
    out_ref[0] = jnp.concatenate([both_ref[0, 112:152], both_ref[1, 120:152]], axis=0)
    qkv_ref[1, 0] = both_ref[0, 152 : 152 + E]
    qkv_ref[1, 1] = both_ref[0, 152 + E : 152 + 2 * E]
    qkv_ref[1, 2] = both_ref[1, 152 : 152 + E]
    out_ref[1] = both_ref[1, 152 + E : 152 + 2 * E]


def last_kernel(
    terms_ref, x_ref, g_ref, keep_ref, recv_ref, two_ref, out_ref, chain_ref, rows_ref
):
    rows_ref[:112] = keep_ref[...].astype(F32) + recv_ref[...].astype(F32)
    total = terms_ref[0].astype(F32)
    for j in range(1, 8):
        total = total + terms_ref[j].astype(F32)
    rows_ref[112:152] = total[128:168]
    rows_ref[152:296] = two_ref[...].astype(F32)
    rows_ref[296:] = jnp.zeros_like(rows_ref[296:])
    for i in range(8):
        chain_ref[i] = rows_ref[i * 40 : (i + 1) * 40].astype(BF)
    normed, inverse = normalize(x_ref[...])
    out_ref[...] = normalize_back(g_ref[...], inverse, normed, total[:128]).astype(BF)


VMEM = pl.BlockSpec(memory_space=pltpu.VMEM)
SMEM = pl.BlockSpec(memory_space=pltpu.SMEM)
ANY = pl.BlockSpec(memory_space=pl.ANY)
MIB = 1024 * 1024


def shape(*dims):
    return jax.ShapeDtypeStruct(dims, BF)


def call(kernel, outs, *args, mib=24, **more):
    return pl.pallas_call(
        kernel,
        out_shape=outs,
        in_specs=more.pop("in_specs", [VMEM] * len(args)),
        out_specs=more.pop("out_specs", jax.tree.map(lambda _: VMEM, outs)),
        compiler_params=pltpu.CompilerParams(vmem_limit_bytes=mib * MIB),
        cost_estimate=pl.CostEstimate(flops=0, bytes_accessed=0, transcendentals=0),
        **more,
    )(*args)


def over_head(blocks):
    return lax.all_to_all(blocks, "head", 0, 0, tiled=True, axis_index_groups=RING)


def over_seq(blocks):
    return lax.all_to_all(blocks, "seq", 0, 0, tiled=True)


def swap_cores(value, n_dp, bit=1):
    return lax.ppermute(value, "dp", [(i, i ^ bit) for i in range(n_dp)])


def groups_of(n_dp):
    n_z = n_dp // 2
    low = min(4, n_z)
    high = n_z // low
    near = [
        [s * n_dp + 2 * (b * low + a) + c for s in range(2) for a in range(low)]
        for b in range(high)
        for c in range(2)
    ]
    far = [
        [2 * (b * low + a) + c for b in range(high)] for a in range(low) for c in range(2)
    ]
    return near, far


def sum_near(grads, near):
    parts = lax.all_to_all(grads, ("seq", "dp"), 0, 0, tiled=True, axis_index_groups=near)
    return jnp.sum(parts.astype(F32), axis=0).astype(BF)


def sum_far(part, far):
    if len(far[0]) == 1:
        return part
    copies = jnp.broadcast_to(part[None], (len(far[0]), *part.shape))
    parts = lax.all_to_all(copies, "dp", 0, 0, tiled=True, axis_index_groups=far)
    return jnp.sum(parts.astype(F32), axis=0).astype(BF)


def spread(part, near):
    copies = jnp.broadcast_to(part[None], (len(near[0]), *part.shape))
    whole = lax.all_to_all(
        copies, ("seq", "dp"), 0, 0, tiled=True, axis_index_groups=near
    )
    return whole.reshape(len(near[0]) * part.shape[0], part.shape[1])


def on_device(n_dp, latents, cotangent, w_qkv, w_out):
    depth = latents.shape[-1]
    index = lax.axis_index("dp")
    at = jnp.stack([index % 2, index // 2 % 2]).astype(jnp.int32)
    near, far = groups_of(n_dp)
    x = latents.reshape(128, depth)
    g = cotangent.reshape(128, depth)
    w_own = w_qkv[0].reshape(3 * E, depth)

    hidden, own = call(
        norm_kernel, (shape(8, 168, depth), shape(E, depth)),
        at, x, w_qkv.reshape(2, 3, E, depth), w_out.reshape(2, E, depth),
        in_specs=[SMEM] + [VMEM] * 3,
        scratch_shapes=[pltpu.VMEM((4, E, depth), F32)],
    )
    own = lax.all_gather(own, "head", axis_index_groups=RING).reshape(8 * E, depth)
    hidden = over_head(hidden)
    heads, qkv, mine_one = call(
        spatial_kernel,
        (shape(8, E, 128), shape(2, 3 * E, 512), shape(8, 40, depth)), hidden, w_own,
    )
    heads = over_head(heads)
    mine_one = mine_one.reshape(320, depth)
    other_one = swap_cores(mine_one, n_dp)
    from_z = swap_cores(own, n_dp, 2)
    from_core = swap_cores(own, n_dp)
    big = shape(16 * E, depth)
    pair, from_z = call(
        middle_kernel, (shape(2, 2, 2, 32, depth), shape(8 * E, depth)),
        at, x, g, heads, mine_one, other_one, from_z,
        in_specs=[SMEM] + [VMEM] * 5 + [ANY],
        out_specs=(VMEM, ANY),
        input_output_aliases={6: 1},
        scratch_shapes=[pltpu.VMEM((2, 320, 128), F32)],
    )
    pair = over_seq(pair)
    from_both = swap_cores(from_z, n_dp)
    back, keep, send = call(
        temporal_kernel,
        (shape(2, 2, 2, 32, depth), big, big),
        at, pair, own, from_z, from_core, from_both,
        in_specs=[SMEM, VMEM] + [ANY] * 4,
        out_specs=(VMEM, ANY, ANY),
        scratch_shapes=[
            pltpu.VMEM((4, 8 * E, depth), BF),
            pltpu.VMEM((2, 16 * E, depth), BF),
            pltpu.VMEM((4, 8 * E, 128), F32),
            pltpu.VMEM((4, 8 * E, 128), F32),
            pltpu.SemaphoreType.DMA((4,)),
        ],
        mib=40,
    )
    back = over_seq(back)
    two = (keep.astype(F32) + swap_cores(send, n_dp).astype(F32)).astype(BF)
    two = lax.psum_scatter(
        two, "head", scatter_dimension=0, tiled=True, axis_index_groups=RING
    )
    half = shape(8, 40, depth)
    gh, keep, send, output, grad_one = call(
        turn_kernel,
        (shape(8, E, 128), half, half, shape(128, depth), shape(128, depth)),
        at, back, heads, mine_one, other_one,
        in_specs=[SMEM] + [VMEM] * 4,
        scratch_shapes=[pltpu.VMEM((2, 320, 128), F32)],
    )
    gh = over_head(gh)
    half = shape(112, depth)
    terms, keep, send = call(
        spatial_back_kernel, (shape(8, 176, depth), half, half),
        at, qkv, gh, hidden, w_own, keep, swap_cores(send, n_dp),
        in_specs=[SMEM] + [VMEM] * 6,
    )
    n_near = len(near[0])
    latent_grads, chain = call(
        last_kernel, (shape(128, depth), shape(n_near, 320 // n_near, depth)),
        over_head(terms), x, grad_one, keep, swap_cores(send, n_dp), two,
        scratch_shapes=[pltpu.VMEM((320, depth), F32)],
    )
    part = sum_near(chain, near)
    mine = spread(sum_far(part, far), near)
    grad_qkv, grad_out = call(
        result_kernel,
        (
            jax.ShapeDtypeStruct((2, 3, E, depth), F32),
            jax.ShapeDtypeStruct((2, E, depth), F32),
        ),
        at, mine, swap_cores(mine, n_dp),
        in_specs=[SMEM, VMEM, VMEM],
        scratch_shapes=[pltpu.VMEM((2, 320, depth), F32)],
    )
    return (
        output.reshape(latents.shape),
        latent_grads.reshape(latents.shape),
        grad_qkv[:, None],
        grad_out[:, None],
    )


def solution(mesh):
    rows = P("dp", "seq", "head", None)
    specs = (rows, rows, P(None, "head", None, None, None), P(None, "head", None, None))
    return jax.shard_map(
        functools.partial(on_device, mesh.shape["dp"]),
        mesh=mesh, in_specs=specs, out_specs=specs, check_vma=False,
    )
```

```python
import functools

import jax
import jax.numpy as jnp
from jax import lax
from jax.experimental import pallas as pl
from jax.experimental.pallas import tpu as pltpu
from jax.sharding import PartitionSpec as P

EPSILON = 1e-06
E = 72
SCALE = E ** (-0.5)
RING = [[0, 2, 4, 6, 7, 5, 3, 1]]
BF = jnp.bfloat16
F32 = jnp.float32


def nn(a, b):
    return lax.dot_general(a, b, (((1,), (0,)), ((), ())), preferred_element_type=F32)


def nt(a, b):
    return lax.dot_general(a, b, (((1,), (1,)), ((), ())), preferred_element_type=F32)


def tn(a, b):
    return lax.dot_general(a, b, (((0,), (0,)), ((), ())), preferred_element_type=F32)


def normalize(rows):
    wide = rows.astype(F32)
    centered = wide - jnp.mean(wide, axis=-1, keepdims=True)
    inverse = lax.rsqrt(jnp.mean(centered * centered, axis=-1, keepdims=True) + EPSILON)
    return centered * inverse, inverse


def normalize_back(grad, inverse, normed, normed_grads):
    mean_grad = jnp.mean(normed_grads, axis=-1, keepdims=True)
    mean_cross = jnp.mean(normed_grads * normed, axis=-1, keepdims=True)
    return grad.astype(F32) + inverse * (normed_grads - mean_grad - normed * mean_cross)


def regroup(first, second):
    low = lax.broadcasted_iota(jnp.int32, first.shape, 1) < 64
    return (
        jnp.where(low, first, pltpu.roll(second, 64, 1)),
        jnp.where(low, pltpu.roll(first, 64, 1), second),
    )


def norm_kernel(at_ref, x_ref, wq_ref, wo_ref, out_ref):
    core = at_ref[0]
    wide = wo_ref[0].astype(F32)
    half = jnp.where(core == 0, wide[:40], wide[32:])
    qk = jnp.concatenate([wq_ref[1, 0].astype(F32), wq_ref[1, 1].astype(F32)], axis=0)
    vo = jnp.concatenate([wq_ref[1, 2].astype(F32), wo_ref[1].astype(F32)], axis=0)
    hidden = normalize(x_ref[...])[0]
    block = [hidden, jnp.where(core == 0, qk, vo), half, jnp.zeros_like(half[:8])]
    block = jnp.concatenate(block, axis=0).astype(BF)
    for j in range(8):
        out_ref[j] = block


def frame_rows(hidden_ref, f):
    return hidden_ref[:, f * 64 : (f + 1) * 64, :].reshape(512, hidden_ref.shape[2])


def softmax(queries, key_rows):
    exponent = jnp.exp(tn(queries, key_rows) * SCALE)
    return exponent / jnp.sum(exponent, axis=1, keepdims=True)


def split3(stacked):
    return tuple(stacked[i * E : (i + 1) * E].astype(BF) for i in range(3))


def spatial_kernel(hidden_ref, w_ref, heads_ref, qkv_ref, one_ref, two_ref):
    for h in range(8):
        two_ref[h * 2 * E : (h + 1) * 2 * E] = hidden_ref[h, 128 : 128 + 2 * E]
        one_ref[h] = hidden_ref[h, 272:320].astype(F32)[:40].astype(BF)
    outs = []
    for f in range(2):
        qkv = nt(w_ref[...], frame_rows(hidden_ref, f))
        qkv_ref[f] = qkv.astype(BF)
        q, k, v = split3(qkv)
        weights = softmax(q, k).astype(BF)
        outs.append(nt(v, weights))
    for m in range(4):
        lanes = slice(m * 128, (m + 1) * 128)
        a, b = regroup(outs[0][:, lanes], outs[1][:, lanes])
        heads_ref[2 * m] = a.astype(BF)
        heads_ref[2 * m + 1] = b.astype(BF)


def middle_kernel(
    core_ref, x_ref, g_ref, heads_ref, mine_ref, other_ref, out_ref, split_ref
):
    core = core_ref[0]
    for h in range(8):
        heads = heads_ref[h].astype(F32)
        split_ref[0, h * 40 : (h + 1) * 40] = heads[:40]
        low = jnp.zeros((8, 128), F32)
        split_ref[1, h * 40 : (h + 1) * 40] = jnp.concatenate([low, heads[40:]], axis=0)
    y = x_ref[...].astype(F32) + tn(split_ref[core].astype(BF), mine_ref[...])
    y = (y + tn(split_ref[1 - core].astype(BF), other_ref[...])).astype(BF)
    g = g_ref[...]
    for s in range(2):
        for f in range(2):
            rows = slice((2 * f + s) * 32, (2 * f + s + 1) * 32)
            out_ref[s, 0, f] = y[rows]
            out_ref[s, 1, f] = g[rows]


def temporal_kernel(
    core_ref, pair_ref, mine_ref, other_ref,
    back_ref, keep_ref, send_ref,
    w_ref, gw_ref, qk_ref, vg_ref, g0_ref, g1_ref, sems,
):
    core = core_ref[0]
    loads = (
        pltpu.make_async_copy(mine_ref, w_ref.at[core], sems.at[0]),
        pltpu.make_async_copy(other_ref, w_ref.at[1 - core], sems.at[1]),
    )
    for load in loads:
        load.start()
    depth = pair_ref.shape[-1]
    rows = jnp.concatenate([pair_ref[s, 0, f] for s in range(2) for f in range(2)], axis=0)
    grad = jnp.concatenate([pair_ref[s, 1, f] for s in range(2) for f in range(2)], axis=0)
    normed, inverse = normalize(rows)
    hidden = normed.astype(BF)
    both = jnp.concatenate([hidden, grad], axis=0)
    for load in loads:
        load.wait()
    qk_ref[...] = nt(w_ref[0], hidden)
    vg_ref[...] = nt(w_ref[1], both)

    def rounded(value):
        return value.astype(BF).astype(F32)

    def ahead(value, r):
        return pltpu.roll(value, 128 - 32 * r, 1) if r else value

    def behind(value, r):
        return pltpu.roll(value, 32 * r, 1) if r else value

    zeros = jnp.zeros((E, 128), F32)
    for h in range(8):
        base = h * 2 * E
        q = rounded(qk_ref[base : base + E])
        k = rounded(qk_ref[base + E : base + 2 * E])
        v = rounded(vg_ref[base : base + E, :128])
        gh = rounded(vg_ref[base + E : base + 2 * E, 128:])
        ks = [ahead(k, r) for r in range(4)]
        vs = [ahead(v, r) for r in range(4)]
        exps = [jnp.exp(jnp.sum(q * kr, axis=0, keepdims=True) * SCALE) for kr in ks]
        total = exps[0] + exps[1] + exps[2] + exps[3]
        probs = [e / total for e in exps]
        weights = [rounded(p) for p in probs]
        heads = sum(w * vr for w, vr in zip(weights, vs))
        gps = [jnp.sum(gh * vr, axis=0, keepdims=True) for vr in vs]
        inner = sum(p * gp for p, gp in zip(probs, gps))
        sgs = [rounded(p * (gp - inner) * SCALE) for p, gp in zip(probs, gps)]
        gq = sum(sg * kr for sg, kr in zip(sgs, ks))
        gk = sum(behind(sg * q, r) for r, sg in enumerate(sgs))
        gv = sum(behind(w * gh, r) for r, w in enumerate(weights))
        g0_ref[base : base + 2 * E] = jnp.concatenate([gq, gk], axis=0).astype(BF)
        g1_ref[base : base + 2 * E, :128] = jnp.concatenate([gv, zeros], axis=0).astype(BF)
        g1_ref[base : base + 2 * E, 128:] = jnp.concatenate([zeros, heads], axis=0).astype(BF)
    for h in range(8):
        span = slice(h * 2 * E, (h + 1) * 2 * E)
        gw_ref[0, span] = nn(g0_ref[span], hidden).astype(BF)
        gw_ref[1, span] = nn(g1_ref[span], both).astype(BF)
    stores = (
        pltpu.make_async_copy(gw_ref.at[core], keep_ref, sems.at[0]),
        pltpu.make_async_copy(gw_ref.at[1 - core], send_ref, sems.at[1]),
    )
    for store in stores:
        store.start()
    mixed = tn(g1_ref[...], w_ref[1])
    normed_grads = tn(g0_ref[...], w_ref[0]) + mixed[:128]
    result = (rows.astype(F32) + mixed[128:]).astype(BF)
    total_grad = normalize_back(grad, inverse, normed, normed_grads).astype(BF)
    for s in range(2):
        for f in range(2):
            at = slice((2 * s + f) * 32, (2 * s + f + 1) * 32)
            back_ref[s, 0, f] = result[at]
            back_ref[s, 1, f] = total_grad[at]
    for store in stores:
        store.wait()


def halves(rows, size):
    return rows[:size], rows[rows.shape[0] - size :]


def local_rows(pair_ref, which):
    return jnp.concatenate([pair_ref[s, which, f] for f in range(2) for s in range(2)], axis=0)


def turn_kernel(
    core_ref, back_ref, heads_ref, mine_ref, other_ref,
    gh_ref, keep_ref, send_ref, out_ref, grad_ref, split_ref,
):
    core = core_ref[0]
    out_ref[...] = local_rows(back_ref, 0)
    grad = local_rows(back_ref, 1)
    grad_ref[...] = grad
    split_ref[core] = nt(mine_ref[...], grad)
    split_ref[1 - core] = nt(other_ref[...], grad)
    for h in range(8):
        at = h * 40
        pieces = [split_ref[0, at : at + 40], split_ref[1, at + 8 : at + 40]]
        gh_ref[h] = jnp.concatenate(pieces, axis=0).astype(BF)
        low, high = halves(nn(heads_ref[h], grad), 40)
        keep_ref[h] = jnp.where(core == 0, low, high).astype(BF)
        send_ref[h] = jnp.where(core == 0, high, low).astype(BF)


def spatial_back_kernel(
    core_ref, qkv_ref, gh_ref, hidden_ref, w_ref, mine_ref, recv_ref, terms_ref, keep_ref, send_ref
):
    for j in range(8):
        part = mine_ref[j].astype(F32) + recv_ref[j].astype(F32)
        low = jnp.zeros((8, part.shape[1]), F32)
        terms_ref[j, 128:176, :] = jnp.concatenate([part, low], axis=0).astype(BF)
    frames = ([], [])
    for m in range(4):
        pair = regroup(gh_ref[2 * m].astype(F32), gh_ref[2 * m + 1].astype(F32))
        for f in range(2):
            frames[f].append(pair[f])
    total = None
    for f in range(2):
        q, k, v = split3(qkv_ref[f].astype(F32))
        gh = jnp.concatenate(frames[f], axis=1).astype(BF)
        probs = softmax(q, k)
        gv = nn(gh, probs.astype(BF))
        gp = tn(gh, v)
        inner = jnp.sum(probs * gp, axis=1, keepdims=True)
        sg = (probs * (gp - inner) * SCALE).astype(BF)
        grads = jnp.concatenate([nt(k, sg), nn(q, sg), gv], axis=0).astype(BF)
        gw = nn(grads, frame_rows(hidden_ref, f))
        total = gw if total is None else total + gw
        terms = tn(grads, w_ref[...]).astype(BF)
        for j in range(8):
            terms_ref[j, f * 64 : (f + 1) * 64, :] = terms[j * 64 : (j + 1) * 64]
    low, high = halves(total, 112)
    keep_ref[...] = jnp.where(core_ref[0] == 0, low, high).astype(BF)
    send_ref[...] = jnp.where(core_ref[0] == 0, high, low).astype(BF)


def result_kernel(core_ref, mine_ref, other_ref, qkv_ref, out_ref, both_ref):
    core = core_ref[0]
    both_ref[core] = mine_ref[...].astype(F32)
    both_ref[1 - core] = other_ref[...].astype(F32)
    qkv = jnp.concatenate([both_ref[0, :112], both_ref[1, 8:112]], axis=0)
    for i in range(3):
        qkv_ref[0, i] = qkv[i * E : (i + 1) * E]
    out_ref[0] = jnp.concatenate([both_ref[0, 112:152], both_ref[1, 120:152]], axis=0)
    qkv_ref[1, 0] = both_ref[0, 152 : 152 + E]
    qkv_ref[1, 1] = both_ref[0, 152 + E : 152 + 2 * E]
    qkv_ref[1, 2] = both_ref[1, 152 : 152 + E]
    out_ref[1] = both_ref[1, 152 + E : 152 + 2 * E]


def last_kernel(
    terms_ref, x_ref, g_ref, keep_ref, recv_ref, two_ref, out_ref, chain_ref, rows_ref
):
    rows_ref[:112] = keep_ref[...].astype(F32) + recv_ref[...].astype(F32)
    total = terms_ref[0].astype(F32)
    for j in range(1, 8):
        total = total + terms_ref[j].astype(F32)
    rows_ref[112:152] = total[128:168]
    rows_ref[152:296] = two_ref[...].astype(F32)
    rows_ref[296:] = jnp.zeros_like(rows_ref[296:])
    for i in range(8):
        chain_ref[i] = rows_ref[i * 40 : (i + 1) * 40].astype(BF)
    normed, inverse = normalize(x_ref[...])
    out_ref[...] = normalize_back(g_ref[...], inverse, normed, total[:128]).astype(BF)


VMEM = pl.BlockSpec(memory_space=pltpu.VMEM)
SMEM = pl.BlockSpec(memory_space=pltpu.SMEM)
ANY = pl.BlockSpec(memory_space=pl.ANY)
MIB = 1024 * 1024


def shape(*dims):
    return jax.ShapeDtypeStruct(dims, BF)


def call(kernel, outs, *args, mib=24, fetch=False, in_specs=None, scratch_shapes=(), **more):
    specs = list(in_specs or [VMEM] * len(args))
    scratch = list(scratch_shapes)
    moved = [i for i, spec in enumerate(specs) if spec is VMEM] if fetch else []
    n_in, n_out, n_own = len(args), len(jax.tree.leaves(outs)), len(scratch)

    def fetching(*refs):
        ins = list(refs[:n_in])
        rest = refs[n_in : n_in + n_out + n_own]
        held, sems = refs[n_in + n_out + n_own : -1], refs[-1]
        copies = [
            pltpu.make_async_copy(ins[i], to, sems.at[k])
            for k, (i, to) in enumerate(zip(moved, held))
        ]
        for copy in copies:
            copy.start()
        for copy in copies:
            copy.wait()
        for i, to in zip(moved, held):
            ins[i] = to
        kernel(*ins, *rest)

    if moved:
        scratch += [pltpu.VMEM(args[i].shape, args[i].dtype) for i in moved]
        scratch.append(pltpu.SemaphoreType.DMA((len(moved),)))
        specs = [ANY if i in moved else spec for i, spec in enumerate(specs)]
    return pl.pallas_call(
        fetching if moved else kernel,
        out_shape=outs,
        in_specs=specs,
        out_specs=more.pop("out_specs", jax.tree.map(lambda _: VMEM, outs)),
        scratch_shapes=scratch,
        compiler_params=pltpu.CompilerParams(vmem_limit_bytes=mib * MIB),
        cost_estimate=pl.CostEstimate(flops=0, bytes_accessed=0, transcendentals=0),
        **more,
    )(*args)


def over_head(blocks):
    return lax.all_to_all(blocks, "head", 0, 0, tiled=True, axis_index_groups=RING)


def over_seq(blocks):
    return lax.all_to_all(blocks, "seq", 0, 0, tiled=True)


def swap_cores(value, n_dp, bit=1):
    return lax.ppermute(value, "dp", [(i, i ^ bit) for i in range(n_dp)])


def groups_of(n_dp):
    n_z = n_dp // 2
    low = min(4, n_z)
    high = n_z // low
    near = [
        [s * n_dp + 2 * (b * low + a) + c for s in range(2) for a in range(low)]
        for b in range(high)
        for c in range(2)
    ]
    far = [
        [2 * (b * low + a) + c for b in range(high)] for a in range(low) for c in range(2)
    ]
    return near, far


def sum_near(grads, near):
    parts = lax.all_to_all(grads, ("seq", "dp"), 0, 0, tiled=True, axis_index_groups=near)
    return jnp.sum(parts.astype(F32), axis=0).astype(BF)


def sum_far(part, far):
    if len(far[0]) == 1:
        return part
    copies = jnp.broadcast_to(part[None], (len(far[0]), *part.shape))
    parts = lax.all_to_all(copies, "dp", 0, 0, tiled=True, axis_index_groups=far)
    return jnp.sum(parts.astype(F32), axis=0).astype(BF)


def spread(part, near):
    copies = jnp.broadcast_to(part[None], (len(near[0]), *part.shape))
    whole = lax.all_to_all(
        copies, ("seq", "dp"), 0, 0, tiled=True, axis_index_groups=near
    )
    return whole.reshape(len(near[0]) * part.shape[0], part.shape[1])


def on_device(n_dp, latents, cotangent, w_qkv, w_out):
    depth = latents.shape[-1]
    at = (lax.axis_index("dp") % 2).reshape(1).astype(jnp.int32)
    near, far = groups_of(n_dp)
    x = latents.reshape(128, depth)
    g = cotangent.reshape(128, depth)
    w_own = w_qkv[0].reshape(3 * E, depth)

    hidden = call(
        norm_kernel, shape(8, 320, depth),
        at, x, w_qkv.reshape(2, 3, E, depth), w_out.reshape(2, E, depth),
        in_specs=[SMEM] + [VMEM] * 3, fetch=True,
    )
    hidden = over_head(hidden)
    big = shape(16 * E, depth)
    heads, qkv, mine_one, mine_two = call(
        spatial_kernel,
        (shape(8, E, 128), shape(2, 3 * E, 512), shape(8, 40, depth), big), hidden, w_own, mib=32,
    )
    heads = over_head(heads)
    mine_one = mine_one.reshape(320, depth)
    other_one = swap_cores(mine_one, n_dp)
    other_two = swap_cores(mine_two, n_dp)
    pair = call(
        middle_kernel, shape(2, 2, 2, 32, depth), at, x, g, heads, mine_one, other_one,
        in_specs=[SMEM] + [VMEM] * 5, fetch=True,
        scratch_shapes=[pltpu.VMEM((2, 320, 128), F32)],
    )
    pair = over_seq(pair)
    back, keep, send = call(
        temporal_kernel,
        (shape(2, 2, 2, 32, depth), big, big),
        at, pair, mine_two, other_two,
        in_specs=[SMEM, VMEM, ANY, ANY],
        out_specs=(VMEM, ANY, ANY),
        scratch_shapes=[
            pltpu.VMEM((2, 16 * E, depth), BF),
            pltpu.VMEM((2, 16 * E, depth), BF),
            pltpu.VMEM((16 * E, 128), F32),
            pltpu.VMEM((16 * E, 256), F32),
            pltpu.VMEM((16 * E, 128), BF),
            pltpu.VMEM((16 * E, 256), BF),
            pltpu.SemaphoreType.DMA((2,)),
        ],
        mib=40,
    )
    back = over_seq(back)
    two = (keep.astype(F32) + swap_cores(send, n_dp).astype(F32)).astype(BF)
    two = lax.psum_scatter(
        two, "head", scatter_dimension=0, tiled=True, axis_index_groups=RING
    )
    half = shape(8, 40, depth)
    gh, keep, send, output, grad_one = call(
        turn_kernel,
        (shape(8, E, 128), half, half, shape(128, depth), shape(128, depth)),
        at, back, heads, mine_one, other_one,
        in_specs=[SMEM] + [VMEM] * 4, fetch=True,
        scratch_shapes=[pltpu.VMEM((2, 320, 128), F32)],
    )
    gh = over_head(gh)
    half = shape(112, depth)
    terms, keep, send = call(
        spatial_back_kernel, (shape(8, 176, depth), half, half),
        at, qkv, gh, hidden, w_own, keep, swap_cores(send, n_dp),
        in_specs=[SMEM] + [VMEM] * 6, mib=32,
    )
    n_near = len(near[0])
    latent_grads, chain = call(
        last_kernel, (shape(128, depth), shape(n_near, 320 // n_near, depth)),
        over_head(terms), x, grad_one, keep, swap_cores(send, n_dp), two,
        scratch_shapes=[pltpu.VMEM((320, depth), F32)], fetch=True,
    )
    part = sum_near(chain, near)
    mine = spread(sum_far(part, far), near)
    grad_qkv, grad_out = call(
        result_kernel,
        (
            jax.ShapeDtypeStruct((2, 3, E, depth), F32),
            jax.ShapeDtypeStruct((2, E, depth), F32),
        ),
        at, mine, swap_cores(mine, n_dp),
        in_specs=[SMEM, VMEM, VMEM],
        scratch_shapes=[pltpu.VMEM((2, 320, depth), F32)],
    )
    return (
        output.reshape(latents.shape),
        latent_grads.reshape(latents.shape),
        grad_qkv[:, None],
        grad_out[:, None],
    )


def solution(mesh):
    rows = P("dp", "seq", "head", None)
    specs = (rows, rows, P(None, "head", None, None, None), P(None, "head", None, None))
    return jax.shard_map(
        functools.partial(on_device, mesh.shape["dp"]),
        mesh=mesh, in_specs=specs, out_specs=specs, check_vma=False,
    )
```

```python
import functools

import jax
import jax.numpy as jnp
from jax import lax
from jax.experimental import pallas as pl
from jax.experimental.pallas import tpu as pltpu
from jax.sharding import PartitionSpec as P

EPSILON = 1e-06
E = 72
SCALE = E ** (-0.5)
RING = [[0, 2, 4, 6, 7, 5, 3, 1]]
BF = jnp.bfloat16
F32 = jnp.float32


def nn(a, b):
    return lax.dot_general(a, b, (((1,), (0,)), ((), ())), preferred_element_type=F32)


def nt(a, b):
    return lax.dot_general(a, b, (((1,), (1,)), ((), ())), preferred_element_type=F32)


def tn(a, b):
    return lax.dot_general(a, b, (((0,), (0,)), ((), ())), preferred_element_type=F32)


def normalize(rows):
    wide = rows.astype(F32)
    centered = wide - jnp.mean(wide, axis=-1, keepdims=True)
    inverse = lax.rsqrt(jnp.mean(centered * centered, axis=-1, keepdims=True) + EPSILON)
    return centered * inverse, inverse


def normalize_back(grad, inverse, normed, normed_grads):
    mean_grad = jnp.mean(normed_grads, axis=-1, keepdims=True)
    mean_cross = jnp.mean(normed_grads * normed, axis=-1, keepdims=True)
    return grad.astype(F32) + inverse * (normed_grads - mean_grad - normed * mean_cross)


def regroup(first, second):
    low = lax.broadcasted_iota(jnp.int32, first.shape, 1) < 64
    return (
        jnp.where(low, first, pltpu.roll(second, 64, 1)),
        jnp.where(low, pltpu.roll(first, 64, 1), second),
    )


def norm_kernel(at_ref, x_ref, wq_ref, wo_ref, out_ref, own_ref):
    core = at_ref[0]
    wide = wo_ref[0].astype(F32)
    half = jnp.where(core == 0, wide[:40], wide[32:])
    hidden = normalize(x_ref[...])[0]
    block = jnp.concatenate([hidden, half], axis=0).astype(BF)
    for j in range(8):
        out_ref[j] = block
    qk = jnp.concatenate([wq_ref[1, 0].astype(F32), wq_ref[1, 1].astype(F32)], axis=0)
    vo = jnp.concatenate([wq_ref[1, 2].astype(F32), wo_ref[1].astype(F32)], axis=0)
    own_ref[...] = jnp.where(core == 0, qk, vo).astype(BF)


def frame_rows(hidden_ref, f):
    return hidden_ref[:, f * 64 : (f + 1) * 64, :].reshape(512, hidden_ref.shape[2])


def softmax(queries, key_rows):
    exponent = jnp.exp(tn(queries, key_rows) * SCALE)
    return exponent / jnp.sum(exponent, axis=1, keepdims=True)


def split3(stacked):
    return tuple(stacked[i * E : (i + 1) * E].astype(BF) for i in range(3))


def spatial_kernel(hidden_ref, w_ref, heads_ref, qkv_ref, one_ref):
    for h in range(8):
        one_ref[h] = hidden_ref[h].astype(F32)[128:].astype(BF)
    outs = []
    for f in range(2):
        qkv = nt(w_ref[...], frame_rows(hidden_ref, f))
        qkv_ref[f] = qkv.astype(BF)
        q, k, v = split3(qkv)
        weights = softmax(q, k).astype(BF)
        outs.append(nt(v, weights))
    for m in range(4):
        lanes = slice(m * 128, (m + 1) * 128)
        a, b = regroup(outs[0][:, lanes], outs[1][:, lanes])
        heads_ref[2 * m] = a.astype(BF)
        heads_ref[2 * m + 1] = b.astype(BF)


def middle_kernel(
    core_ref, x_ref, g_ref, heads_ref, mine_ref, other_ref, pass_ref, out_ref, same_ref, split_ref
):
    core = core_ref[0]
    for h in range(8):
        heads = heads_ref[h].astype(F32)
        split_ref[0, h * 40 : (h + 1) * 40] = heads[:40]
        low = jnp.zeros((8, 128), F32)
        split_ref[1, h * 40 : (h + 1) * 40] = jnp.concatenate([low, heads[40:]], axis=0)
    y = x_ref[...].astype(F32) + tn(split_ref[core].astype(BF), mine_ref[...])
    y = (y + tn(split_ref[1 - core].astype(BF), other_ref[...])).astype(BF)
    g = g_ref[...]
    for s in range(2):
        for f in range(2):
            rows = slice((2 * f + s) * 32, (2 * f + s + 1) * 32)
            out_ref[s, 0, f] = y[rows]
            out_ref[s, 1, f] = g[rows]


def temporal_kernel(
    core_ref, pair_ref, mine_ref, other_ref,
    back_ref, keep_ref, send_ref,
    w_ref, gw_ref, qk_ref, vg_ref, g0_ref, g1_ref, sems,
):
    core = core_ref[0]
    loads = (
        pltpu.make_async_copy(mine_ref, w_ref.at[core], sems.at[0]),
        pltpu.make_async_copy(other_ref, w_ref.at[1 - core], sems.at[1]),
    )
    for load in loads:
        load.start()
    depth = pair_ref.shape[-1]
    rows = jnp.concatenate([pair_ref[s, 0, f] for s in range(2) for f in range(2)], axis=0)
    grad = jnp.concatenate([pair_ref[s, 1, f] for s in range(2) for f in range(2)], axis=0)
    normed, inverse = normalize(rows)
    hidden = normed.astype(BF)
    both = jnp.concatenate([hidden, grad], axis=0)
    for load in loads:
        load.wait()
    qk_ref[...] = nt(w_ref[0], hidden)
    vg_ref[...] = nt(w_ref[1], both)

    def rounded(value):
        return value.astype(BF).astype(F32)

    def ahead(value, r):
        return pltpu.roll(value, 128 - 32 * r, 1) if r else value

    def behind(value, r):
        return pltpu.roll(value, 32 * r, 1) if r else value

    zeros = jnp.zeros((E, 128), F32)
    for h in range(8):
        base = h * 2 * E
        q = rounded(qk_ref[base : base + E])
        k = rounded(qk_ref[base + E : base + 2 * E])
        v = rounded(vg_ref[base : base + E, :128])
        gh = rounded(vg_ref[base + E : base + 2 * E, 128:])
        ks = [ahead(k, r) for r in range(4)]
        vs = [ahead(v, r) for r in range(4)]
        exps = [jnp.exp(jnp.sum(q * kr, axis=0, keepdims=True) * SCALE) for kr in ks]
        total = exps[0] + exps[1] + exps[2] + exps[3]
        probs = [e / total for e in exps]
        weights = [rounded(p) for p in probs]
        heads = sum(w * vr for w, vr in zip(weights, vs))
        gps = [jnp.sum(gh * vr, axis=0, keepdims=True) for vr in vs]
        inner = sum(p * gp for p, gp in zip(probs, gps))
        sgs = [rounded(p * (gp - inner) * SCALE) for p, gp in zip(probs, gps)]
        gq = sum(sg * kr for sg, kr in zip(sgs, ks))
        gk = sum(behind(sg * q, r) for r, sg in enumerate(sgs))
        gv = sum(behind(w * gh, r) for r, w in enumerate(weights))
        g0_ref[base : base + 2 * E] = jnp.concatenate([gq, gk], axis=0).astype(BF)
        g1_ref[base : base + 2 * E, :128] = jnp.concatenate([gv, zeros], axis=0).astype(BF)
        g1_ref[base : base + 2 * E, 128:] = jnp.concatenate([zeros, heads], axis=0).astype(BF)
    for h in range(8):
        span = slice(h * 2 * E, (h + 1) * 2 * E)
        gw_ref[0, span] = nn(g0_ref[span], hidden).astype(BF)
        gw_ref[1, span] = nn(g1_ref[span], both).astype(BF)
    stores = (
        pltpu.make_async_copy(gw_ref.at[core], keep_ref, sems.at[0]),
        pltpu.make_async_copy(gw_ref.at[1 - core], send_ref, sems.at[1]),
    )
    for store in stores:
        store.start()
    mixed = tn(g1_ref[...], w_ref[1])
    normed_grads = tn(g0_ref[...], w_ref[0]) + mixed[:128]
    result = (rows.astype(F32) + mixed[128:]).astype(BF)
    total_grad = normalize_back(grad, inverse, normed, normed_grads).astype(BF)
    for s in range(2):
        for f in range(2):
            at = slice((2 * s + f) * 32, (2 * s + f + 1) * 32)
            back_ref[s, 0, f] = result[at]
            back_ref[s, 1, f] = total_grad[at]
    for store in stores:
        store.wait()


def halves(rows, size):
    return rows[:size], rows[rows.shape[0] - size :]


def local_rows(pair_ref, which):
    return jnp.concatenate([pair_ref[s, which, f] for f in range(2) for s in range(2)], axis=0)


def turn_kernel(
    core_ref, back_ref, heads_ref, mine_ref, other_ref, two_ref, recv_ref,
    gh_ref, keep_ref, send_ref, out_ref, grad_ref, sum_ref, split_ref,
):
    core = core_ref[0]
    out_ref[...] = local_rows(back_ref, 0)
    grad = local_rows(back_ref, 1)
    grad_ref[...] = grad
    split_ref[core] = nt(mine_ref[...], grad)
    split_ref[1 - core] = nt(other_ref[...], grad)
    for h in range(8):
        at = h * 40
        pieces = [split_ref[0, at : at + 40], split_ref[1, at + 8 : at + 40]]
        gh_ref[h] = jnp.concatenate(pieces, axis=0).astype(BF)
        low, high = halves(nn(heads_ref[h], grad), 40)
        keep_ref[h] = jnp.where(core == 0, low, high).astype(BF)
        send_ref[h] = jnp.where(core == 0, high, low).astype(BF)
        span = slice(h * 2 * E, (h + 1) * 2 * E)
        sum_ref[span] = (two_ref[span].astype(F32) + recv_ref[span].astype(F32)).astype(BF)


def spatial_back_kernel(
    core_ref, qkv_ref, gh_ref, hidden_ref, w_ref, mine_ref, recv_ref, terms_ref, keep_ref, send_ref
):
    for j in range(8):
        part = mine_ref[j].astype(F32) + recv_ref[j].astype(F32)
        low = jnp.zeros((8, part.shape[1]), F32)
        terms_ref[j, 128:176, :] = jnp.concatenate([part, low], axis=0).astype(BF)
    frames = ([], [])
    for m in range(4):
        pair = regroup(gh_ref[2 * m].astype(F32), gh_ref[2 * m + 1].astype(F32))
        for f in range(2):
            frames[f].append(pair[f])
    total = None
    for f in range(2):
        q, k, v = split3(qkv_ref[f].astype(F32))
        gh = jnp.concatenate(frames[f], axis=1).astype(BF)
        probs = softmax(q, k)
        gv = nn(gh, probs.astype(BF))
        gp = tn(gh, v)
        inner = jnp.sum(probs * gp, axis=1, keepdims=True)
        sg = (probs * (gp - inner) * SCALE).astype(BF)
        grads = jnp.concatenate([nt(k, sg), nn(q, sg), gv], axis=0).astype(BF)
        gw = nn(grads, frame_rows(hidden_ref, f))
        total = gw if total is None else total + gw
        terms = tn(grads, w_ref[...]).astype(BF)
        for j in range(8):
            terms_ref[j, f * 64 : (f + 1) * 64, :] = terms[j * 64 : (j + 1) * 64]
    low, high = halves(total, 112)
    keep_ref[...] = jnp.where(core_ref[0] == 0, low, high).astype(BF)
    send_ref[...] = jnp.where(core_ref[0] == 0, high, low).astype(BF)


def result_kernel(core_ref, mine_ref, other_ref, qkv_ref, out_ref, both_ref):
    core = core_ref[0]
    both_ref[core] = mine_ref[...].astype(F32)
    both_ref[1 - core] = other_ref[...].astype(F32)
    qkv = jnp.concatenate([both_ref[0, :112], both_ref[1, 8:112]], axis=0)
    for i in range(3):
        qkv_ref[0, i] = qkv[i * E : (i + 1) * E]
    out_ref[0] = jnp.concatenate([both_ref[0, 112:152], both_ref[1, 120:152]], axis=0)
    qkv_ref[1, 0] = both_ref[0, 152 : 152 + E]
    qkv_ref[1, 1] = both_ref[0, 152 + E : 152 + 2 * E]
    qkv_ref[1, 2] = both_ref[1, 152 : 152 + E]
    out_ref[1] = both_ref[1, 152 + E : 152 + 2 * E]


def last_kernel(
    terms_ref, x_ref, g_ref, keep_ref, recv_ref, two_ref, out_ref, chain_ref, rows_ref
):
    rows_ref[:112] = keep_ref[...].astype(F32) + recv_ref[...].astype(F32)
    total = terms_ref[0].astype(F32)
    for j in range(1, 8):
        total = total + terms_ref[j].astype(F32)
    rows_ref[112:152] = total[128:168]
    rows_ref[152:296] = two_ref[...].astype(F32)
    rows_ref[296:] = jnp.zeros_like(rows_ref[296:])
    for i in range(8):
        chain_ref[i] = rows_ref[i * 40 : (i + 1) * 40].astype(BF)
    normed, inverse = normalize(x_ref[...])
    out_ref[...] = normalize_back(g_ref[...], inverse, normed, total[:128]).astype(BF)


VMEM = pl.BlockSpec(memory_space=pltpu.VMEM)
SMEM = pl.BlockSpec(memory_space=pltpu.SMEM)
ANY = pl.BlockSpec(memory_space=pl.ANY)
MIB = 1024 * 1024


def shape(*dims):
    return jax.ShapeDtypeStruct(dims, BF)


def call(kernel, outs, *args, mib=24, fetch=False, in_specs=None, scratch_shapes=(), **more):
    specs = list(in_specs or [VMEM] * len(args))
    scratch = list(scratch_shapes)
    moved = [i for i, spec in enumerate(specs) if spec is VMEM] if fetch else []
    n_in, n_out, n_own = len(args), len(jax.tree.leaves(outs)), len(scratch)

    def fetching(*refs):
        ins = list(refs[:n_in])
        rest = refs[n_in : n_in + n_out + n_own]
        held, sems = refs[n_in + n_out + n_own : -1], refs[-1]
        copies = [
            pltpu.make_async_copy(ins[i], to, sems.at[k])
            for k, (i, to) in enumerate(zip(moved, held))
        ]
        for copy in copies:
            copy.start()
        for copy in copies:
            copy.wait()
        for i, to in zip(moved, held):
            ins[i] = to
        kernel(*ins, *rest)

    if moved:
        scratch += [pltpu.VMEM(args[i].shape, args[i].dtype) for i in moved]
        scratch.append(pltpu.SemaphoreType.DMA((len(moved),)))
        specs = [ANY if i in moved else spec for i, spec in enumerate(specs)]
    return pl.pallas_call(
        fetching if moved else kernel,
        out_shape=outs,
        in_specs=specs,
        out_specs=more.pop("out_specs", jax.tree.map(lambda _: VMEM, outs)),
        scratch_shapes=scratch,
        compiler_params=pltpu.CompilerParams(vmem_limit_bytes=mib * MIB),
        cost_estimate=pl.CostEstimate(flops=0, bytes_accessed=0, transcendentals=0),
        **more,
    )(*args)


def over_head(blocks):
    return lax.all_to_all(blocks, "head", 0, 0, tiled=True, axis_index_groups=RING)


def over_seq(blocks):
    return lax.all_to_all(blocks, "seq", 0, 0, tiled=True)


def swap_cores(value, n_dp, bit=1):
    return lax.ppermute(value, "dp", [(i, i ^ bit) for i in range(n_dp)])


def groups_of(n_dp):
    n_z = n_dp // 2
    low = min(4, n_z)
    high = n_z // low
    near = [
        [s * n_dp + 2 * (b * low + a) + c for s in range(2) for a in range(low)]
        for b in range(high)
        for c in range(2)
    ]
    far = [
        [2 * (b * low + a) + c for b in range(high)] for a in range(low) for c in range(2)
    ]
    return near, far


def sum_near(grads, near):
    parts = lax.all_to_all(grads, ("seq", "dp"), 0, 0, tiled=True, axis_index_groups=near)
    return jnp.sum(parts.astype(F32), axis=0).astype(BF)


def sum_far(part, far):
    if len(far[0]) == 1:
        return part
    copies = jnp.broadcast_to(part[None], (len(far[0]), *part.shape))
    parts = lax.all_to_all(copies, "dp", 0, 0, tiled=True, axis_index_groups=far)
    return jnp.sum(parts.astype(F32), axis=0).astype(BF)


def spread(part, near):
    copies = jnp.broadcast_to(part[None], (len(near[0]), *part.shape))
    whole = lax.all_to_all(
        copies, ("seq", "dp"), 0, 0, tiled=True, axis_index_groups=near
    )
    return whole.reshape(len(near[0]) * part.shape[0], part.shape[1])


def on_device(n_dp, latents, cotangent, w_qkv, w_out):
    depth = latents.shape[-1]
    at = (lax.axis_index("dp") % 2).reshape(1).astype(jnp.int32)
    near, far = groups_of(n_dp)
    x = latents.reshape(128, depth)
    g = cotangent.reshape(128, depth)
    w_own = w_qkv[0].reshape(3 * E, depth)

    hidden, own = call(
        norm_kernel, (shape(8, 168, depth), shape(2 * E, depth)),
        at, x, w_qkv.reshape(2, 3, E, depth), w_out.reshape(2, E, depth),
        in_specs=[SMEM] + [VMEM] * 3, fetch=True,
    )
    mine_two = lax.all_gather(own, "head", axis_index_groups=RING).reshape(16 * E, depth)
    hidden = over_head(hidden)
    heads, qkv, mine_one = call(
        spatial_kernel,
        (shape(8, E, 128), shape(2, 3 * E, 512), shape(8, 40, depth)), hidden, w_own,
    )
    heads = over_head(heads)
    mine_one = mine_one.reshape(320, depth)
    other_one = swap_cores(mine_one, n_dp)
    big = shape(16 * E, depth)
    pair, mine_two = call(
        middle_kernel, (shape(2, 2, 2, 32, depth), big),
        at, x, g, heads, mine_one, other_one, mine_two,
        in_specs=[SMEM] + [VMEM] * 5 + [ANY], fetch=True,
        out_specs=(VMEM, ANY),
        input_output_aliases={6: 1},
        scratch_shapes=[pltpu.VMEM((2, 320, 128), F32)],
    )
    pair = over_seq(pair)
    other_two = swap_cores(mine_two, n_dp)
    back, keep, send = call(
        temporal_kernel,
        (shape(2, 2, 2, 32, depth), big, big),
        at, pair, mine_two, other_two,
        in_specs=[SMEM, VMEM, ANY, ANY],
        out_specs=(VMEM, ANY, ANY),
        scratch_shapes=[
            pltpu.VMEM((2, 16 * E, depth), BF),
            pltpu.VMEM((2, 16 * E, depth), BF),
            pltpu.VMEM((16 * E, 128), F32),
            pltpu.VMEM((16 * E, 256), F32),
            pltpu.VMEM((16 * E, 128), BF),
            pltpu.VMEM((16 * E, 256), BF),
            pltpu.SemaphoreType.DMA((2,)),
        ],
        mib=40,
    )
    back = over_seq(back)
    half = shape(8, 40, depth)
    gh, keep, send, output, grad_one, two = call(
        turn_kernel,
        (shape(8, E, 128), half, half, shape(128, depth), shape(128, depth), big),
        at, back, heads, mine_one, other_one, keep, swap_cores(send, n_dp),
        in_specs=[SMEM] + [VMEM] * 6, fetch=True,
        scratch_shapes=[pltpu.VMEM((2, 320, 128), F32)],
    )
    two = lax.psum_scatter(
        two, "head", scatter_dimension=0, tiled=True, axis_index_groups=RING
    )
    gh = over_head(gh)
    half = shape(112, depth)
    terms, keep, send = call(
        spatial_back_kernel, (shape(8, 176, depth), half, half),
        at, qkv, gh, hidden, w_own, keep, swap_cores(send, n_dp),
        in_specs=[SMEM] + [VMEM] * 6, mib=32,
    )
    n_near = len(near[0])
    latent_grads, chain = call(
        last_kernel, (shape(128, depth), shape(n_near, 320 // n_near, depth)),
        over_head(terms), x, grad_one, keep, swap_cores(send, n_dp), two,
        scratch_shapes=[pltpu.VMEM((320, depth), F32)], fetch=True,
    )
    part = sum_near(chain, near)
    mine = spread(sum_far(part, far), near)
    grad_qkv, grad_out = call(
        result_kernel,
        (
            jax.ShapeDtypeStruct((2, 3, E, depth), F32),
            jax.ShapeDtypeStruct((2, E, depth), F32),
        ),
        at, mine, swap_cores(mine, n_dp),
        in_specs=[SMEM, VMEM, VMEM],
        scratch_shapes=[pltpu.VMEM((2, 320, depth), F32)],
    )
    return (
        output.reshape(latents.shape),
        latent_grads.reshape(latents.shape),
        grad_qkv[:, None],
        grad_out[:, None],
    )


def solution(mesh):
    rows = P("dp", "seq", "head", None)
    specs = (rows, rows, P(None, "head", None, None, None), P(None, "head", None, None))
    return jax.shard_map(
        functools.partial(on_device, mesh.shape["dp"]),
        mesh=mesh, in_specs=specs, out_specs=specs, check_vma=False,
    )
```

```python
import functools

import jax
import jax.numpy as jnp
from jax import lax
from jax.experimental import pallas as pl
from jax.experimental.pallas import tpu as pltpu
from jax.sharding import PartitionSpec as P

EPSILON = 1e-06
E = 72
SCALE = E ** (-0.5)
RING = [[0, 2, 4, 6, 7, 5, 3, 1]]
BF = jnp.bfloat16
F32 = jnp.float32


def nn(a, b):
    return lax.dot_general(a, b, (((1,), (0,)), ((), ())), preferred_element_type=F32)


def nt(a, b):
    return lax.dot_general(a, b, (((1,), (1,)), ((), ())), preferred_element_type=F32)


def tn(a, b):
    return lax.dot_general(a, b, (((0,), (0,)), ((), ())), preferred_element_type=F32)


def normalize(rows):
    wide = rows.astype(F32)
    centered = wide - jnp.mean(wide, axis=-1, keepdims=True)
    inverse = lax.rsqrt(jnp.mean(centered * centered, axis=-1, keepdims=True) + EPSILON)
    return centered * inverse, inverse


def normalize_back(grad, inverse, normed, normed_grads):
    mean_grad = jnp.mean(normed_grads, axis=-1, keepdims=True)
    mean_cross = jnp.mean(normed_grads * normed, axis=-1, keepdims=True)
    return grad.astype(F32) + inverse * (normed_grads - mean_grad - normed * mean_cross)


def regroup(first, second):
    low = lax.broadcasted_iota(jnp.int32, first.shape, 1) < 64
    return (
        jnp.where(low, first, pltpu.roll(second, 64, 1)),
        jnp.where(low, pltpu.roll(first, 64, 1), second),
    )


def norm_kernel(at_ref, x_ref, wq_ref, wo_ref, out_ref, parts_ref):
    wide = wo_ref[0].astype(F32)
    half = jnp.where(at_ref[0] == 0, wide[:40], wide[32:])
    for i in range(3):
        parts_ref[i] = wq_ref[1, i].astype(F32)
    parts_ref[3] = wo_ref[1].astype(F32)
    part = parts_ref[2 * at_ref[0] + at_ref[1]]
    hidden = normalize(x_ref[...])[0]
    block = jnp.concatenate([hidden, part, half], axis=0).astype(BF)
    for j in range(8):
        out_ref[j] = block


def frame_rows(hidden_ref, f):
    return hidden_ref[:, f * 64 : (f + 1) * 64, :].reshape(512, hidden_ref.shape[2])


def softmax(queries, key_rows):
    exponent = jnp.exp(tn(queries, key_rows) * SCALE)
    return exponent / jnp.sum(exponent, axis=1, keepdims=True)


def split3(stacked):
    return tuple(stacked[i * E : (i + 1) * E].astype(BF) for i in range(3))


def spatial_kernel(hidden_ref, w_ref, heads_ref, qkv_ref, two_ref, one_ref):
    for h in range(8):
        both = hidden_ref[h, 128:240].astype(F32)
        two_ref[h] = both[:E].astype(BF)
        one_ref[h] = both[E:].astype(BF)
    outs = []
    for f in range(2):
        qkv = nt(w_ref[...], frame_rows(hidden_ref, f))
        qkv_ref[f] = qkv.astype(BF)
        q, k, v = split3(qkv)
        weights = softmax(q, k).astype(BF)
        outs.append(nt(v, weights))
    for m in range(4):
        lanes = slice(m * 128, (m + 1) * 128)
        a, b = regroup(outs[0][:, lanes], outs[1][:, lanes])
        heads_ref[2 * m] = a.astype(BF)
        heads_ref[2 * m + 1] = b.astype(BF)


def middle_kernel(
    core_ref, x_ref, g_ref, heads_ref, mine_ref, other_ref, pass_ref, out_ref, same_ref, split_ref
):
    core = core_ref[0]
    for h in range(8):
        heads = heads_ref[h].astype(F32)
        split_ref[0, h * 40 : (h + 1) * 40] = heads[:40]
        low = jnp.zeros((8, 128), F32)
        split_ref[1, h * 40 : (h + 1) * 40] = jnp.concatenate([low, heads[40:]], axis=0)
    y = x_ref[...].astype(F32) + tn(split_ref[core].astype(BF), mine_ref[...])
    y = (y + tn(split_ref[1 - core].astype(BF), other_ref[...])).astype(BF)
    g = g_ref[...]
    for s in range(2):
        for f in range(2):
            rows = slice((2 * f + s) * 32, (2 * f + s + 1) * 32)
            out_ref[s, 0, f] = y[rows]
            out_ref[s, 1, f] = g[rows]


def temporal_kernel(
    at_ref, pair_ref, own_ref, z_ref, core_ref, both_ref,
    back_ref, keep_ref, send_ref,
    w_ref, gw_ref, in_ref, grads_ref, sems,
):
    core, odd = at_ref[0], at_ref[1]
    here, there = 2 * core, 2 * (1 - core)
    loads = (
        pltpu.make_async_copy(own_ref, w_ref.at[here + odd], sems.at[0]),
        pltpu.make_async_copy(z_ref, w_ref.at[here + 1 - odd], sems.at[1]),
        pltpu.make_async_copy(core_ref, w_ref.at[there + odd], sems.at[2]),
        pltpu.make_async_copy(both_ref, w_ref.at[there + 1 - odd], sems.at[3]),
    )
    for load in loads:
        load.start()
    depth = pair_ref.shape[-1]
    rows = jnp.concatenate([pair_ref[s, 0, f] for s in range(2) for f in range(2)], axis=0)
    grad = jnp.concatenate([pair_ref[s, 1, f] for s in range(2) for f in range(2)], axis=0)
    normed, inverse = normalize(rows)
    hidden = normed.astype(BF)
    for load in loads:
        load.wait()
    for i in range(4):
        in_ref[i] = nt(w_ref[i], grad if i == 3 else hidden)

    def rounded(value):
        return value.astype(BF).astype(F32)

    def ahead(value, r):
        return pltpu.roll(value, 128 - 32 * r, 1) if r else value

    def behind(value, r):
        return pltpu.roll(value, 32 * r, 1) if r else value

    for h in range(8):
        span = slice(h * E, (h + 1) * E)
        q, k, v, gh = (rounded(in_ref[i, span]) for i in range(4))
        ks = [ahead(k, r) for r in range(4)]
        vs = [ahead(v, r) for r in range(4)]
        exps = [jnp.exp(jnp.sum(q * kr, axis=0, keepdims=True) * SCALE) for kr in ks]
        total = exps[0] + exps[1] + exps[2] + exps[3]
        probs = [e / total for e in exps]
        weights = [rounded(p) for p in probs]
        heads = sum(w * vr for w, vr in zip(weights, vs))
        gps = [jnp.sum(gh * vr, axis=0, keepdims=True) for vr in vs]
        inner = sum(p * gp for p, gp in zip(probs, gps))
        sgs = [rounded(p * (gp - inner) * SCALE) for p, gp in zip(probs, gps)]
        gq = sum(sg * kr for sg, kr in zip(sgs, ks))
        gk = sum(behind(sg * q, r) for r, sg in enumerate(sgs))
        gv = sum(behind(w * gh, r) for r, w in enumerate(weights))
        for i, grads in enumerate((gq, gk, gv, heads)):
            grads_ref[i, span] = grads
        wide = slice(h * 2 * E, (h + 1) * 2 * E)
        qk_grads = jnp.concatenate([gq, gk], axis=0).astype(BF)
        gw_ref[0, wide] = nn(qk_grads, hidden).astype(BF)
        vo_grads = [nn(gv.astype(BF), hidden), nn(heads.astype(BF), grad)]
        gw_ref[1, wide] = jnp.concatenate(vo_grads, axis=0).astype(BF)
    stores = (
        pltpu.make_async_copy(gw_ref.at[core], keep_ref, sems.at[0]),
        pltpu.make_async_copy(gw_ref.at[1 - core], send_ref, sems.at[1]),
    )
    for store in stores:
        store.start()
    sums = [tn(grads_ref[i].astype(BF), w_ref[i]) for i in range(4)]
    normed_grads = sums[0] + sums[1] + sums[2]
    result = (rows.astype(F32) + sums[3]).astype(BF)
    total_grad = normalize_back(grad, inverse, normed, normed_grads).astype(BF)
    for s in range(2):
        for f in range(2):
            at = slice((2 * s + f) * 32, (2 * s + f + 1) * 32)
            back_ref[s, 0, f] = result[at]
            back_ref[s, 1, f] = total_grad[at]
    for store in stores:
        store.wait()


def halves(rows, size):
    return rows[:size], rows[rows.shape[0] - size :]


def local_rows(pair_ref, which):
    return jnp.concatenate([pair_ref[s, which, f] for f in range(2) for s in range(2)], axis=0)


def turn_kernel(
    core_ref, back_ref, heads_ref, mine_ref, other_ref,
    gh_ref, keep_ref, send_ref, out_ref, grad_ref, split_ref,
):
    core = core_ref[0]
    out_ref[...] = local_rows(back_ref, 0)
    grad = local_rows(back_ref, 1)
    grad_ref[...] = grad
    split_ref[core] = nt(mine_ref[...], grad)
    split_ref[1 - core] = nt(other_ref[...], grad)
    for h in range(8):
        at = h * 40
        pieces = [split_ref[0, at : at + 40], split_ref[1, at + 8 : at + 40]]
        gh_ref[h] = jnp.concatenate(pieces, axis=0).astype(BF)
        low, high = halves(nn(heads_ref[h], grad), 40)
        keep_ref[h] = jnp.where(core == 0, low, high).astype(BF)
        send_ref[h] = jnp.where(core == 0, high, low).astype(BF)


def spatial_back_kernel(
    core_ref, qkv_ref, gh_ref, hidden_ref, w_ref, mine_ref, recv_ref, terms_ref, keep_ref, send_ref
):
    for j in range(8):
        part = mine_ref[j].astype(F32) + recv_ref[j].astype(F32)
        low = jnp.zeros((8, part.shape[1]), F32)
        terms_ref[j, 128:176, :] = jnp.concatenate([part, low], axis=0).astype(BF)
    frames = ([], [])
    for m in range(4):
        pair = regroup(gh_ref[2 * m].astype(F32), gh_ref[2 * m + 1].astype(F32))
        for f in range(2):
            frames[f].append(pair[f])
    total = None
    for f in range(2):
        q, k, v = split3(qkv_ref[f].astype(F32))
        gh = jnp.concatenate(frames[f], axis=1).astype(BF)
        probs = softmax(q, k)
        gv = nn(gh, probs.astype(BF))
        gp = tn(gh, v)
        inner = jnp.sum(probs * gp, axis=1, keepdims=True)
        sg = (probs * (gp - inner) * SCALE).astype(BF)
        grads = jnp.concatenate([nt(k, sg), nn(q, sg), gv], axis=0).astype(BF)
        gw = nn(grads, frame_rows(hidden_ref, f))
        total = gw if total is None else total + gw
        terms = tn(grads, w_ref[...]).astype(BF)
        for j in range(8):
            terms_ref[j, f * 64 : (f + 1) * 64, :] = terms[j * 64 : (j + 1) * 64]
    low, high = halves(total, 112)
    keep_ref[...] = jnp.where(core_ref[0] == 0, low, high).astype(BF)
    send_ref[...] = jnp.where(core_ref[0] == 0, high, low).astype(BF)


def result_kernel(core_ref, mine_ref, other_ref, qkv_ref, out_ref, both_ref):
    core = core_ref[0]
    both_ref[core] = mine_ref[...].astype(F32)
    both_ref[1 - core] = other_ref[...].astype(F32)
    qkv = jnp.concatenate([both_ref[0, :112], both_ref[1, 8:112]], axis=0)
    for i in range(3):
        qkv_ref[0, i] = qkv[i * E : (i + 1) * E]
    out_ref[0] = jnp.concatenate([both_ref[0, 112:152], both_ref[1, 120:152]], axis=0)
    qkv_ref[1, 0] = both_ref[0, 152 : 152 + E]
    qkv_ref[1, 1] = both_ref[0, 152 + E : 152 + 2 * E]
    qkv_ref[1, 2] = both_ref[1, 152 : 152 + E]
    out_ref[1] = both_ref[1, 152 + E : 152 + 2 * E]


def last_kernel(
    terms_ref, x_ref, g_ref, keep_ref, recv_ref, two_ref, out_ref, chain_ref, rows_ref
):
    rows_ref[:112] = keep_ref[...].astype(F32) + recv_ref[...].astype(F32)
    total = terms_ref[0].astype(F32)
    for j in range(1, 8):
        total = total + terms_ref[j].astype(F32)
    rows_ref[112:152] = total[128:168]
    rows_ref[152:296] = two_ref[...].astype(F32)
    rows_ref[296:] = jnp.zeros_like(rows_ref[296:])
    for i in range(8):
        chain_ref[i] = rows_ref[i * 40 : (i + 1) * 40].astype(BF)
    normed, inverse = normalize(x_ref[...])
    out_ref[...] = normalize_back(g_ref[...], inverse, normed, total[:128]).astype(BF)


VMEM = pl.BlockSpec(memory_space=pltpu.VMEM)
SMEM = pl.BlockSpec(memory_space=pltpu.SMEM)
ANY = pl.BlockSpec(memory_space=pl.ANY)
MIB = 1024 * 1024


def shape(*dims):
    return jax.ShapeDtypeStruct(dims, BF)


def call(kernel, outs, *args, mib=24, fetch=False, in_specs=None, scratch_shapes=(), **more):
    specs = list(in_specs or [VMEM] * len(args))
    scratch = list(scratch_shapes)
    moved = [i for i, spec in enumerate(specs) if spec is VMEM] if fetch else []
    n_in, n_out, n_own = len(args), len(jax.tree.leaves(outs)), len(scratch)

    def fetching(*refs):
        ins = list(refs[:n_in])
        rest = refs[n_in : n_in + n_out + n_own]
        held, sems = refs[n_in + n_out + n_own : -1], refs[-1]
        copies = [
            pltpu.make_async_copy(ins[i], to, sems.at[k])
            for k, (i, to) in enumerate(zip(moved, held))
        ]
        for copy in copies:
            copy.start()
        for copy in copies:
            copy.wait()
        for i, to in zip(moved, held):
            ins[i] = to
        kernel(*ins, *rest)

    if moved:
        scratch += [pltpu.VMEM(args[i].shape, args[i].dtype) for i in moved]
        scratch.append(pltpu.SemaphoreType.DMA((len(moved),)))
        specs = [ANY if i in moved else spec for i, spec in enumerate(specs)]
    return pl.pallas_call(
        fetching if moved else kernel,
        out_shape=outs,
        in_specs=specs,
        out_specs=more.pop("out_specs", jax.tree.map(lambda _: VMEM, outs)),
        scratch_shapes=scratch,
        compiler_params=pltpu.CompilerParams(vmem_limit_bytes=mib * MIB),
        cost_estimate=pl.CostEstimate(flops=0, bytes_accessed=0, transcendentals=0),
        **more,
    )(*args)


def over_head(blocks):
    return lax.all_to_all(blocks, "head", 0, 0, tiled=True, axis_index_groups=RING)


def over_seq(blocks):
    return lax.all_to_all(blocks, "seq", 0, 0, tiled=True)


def swap_cores(value, n_dp, bit=1):
    return lax.ppermute(value, "dp", [(i, i ^ bit) for i in range(n_dp)])


def groups_of(n_dp):
    n_z = n_dp // 2
    low = min(4, n_z)
    high = n_z // low
    near = [
        [s * n_dp + 2 * (b * low + a) + c for s in range(2) for a in range(low)]
        for b in range(high)
        for c in range(2)
    ]
    far = [
        [2 * (b * low + a) + c for b in range(high)] for a in range(low) for c in range(2)
    ]
    return near, far


def sum_near(grads, near):
    parts = lax.all_to_all(grads, ("seq", "dp"), 0, 0, tiled=True, axis_index_groups=near)
    return jnp.sum(parts.astype(F32), axis=0).astype(BF)


def sum_far(part, far):
    if len(far[0]) == 1:
        return part
    copies = jnp.broadcast_to(part[None], (len(far[0]), *part.shape))
    parts = lax.all_to_all(copies, "dp", 0, 0, tiled=True, axis_index_groups=far)
    return jnp.sum(parts.astype(F32), axis=0).astype(BF)


def spread(part, near):
    copies = jnp.broadcast_to(part[None], (len(near[0]), *part.shape))
    whole = lax.all_to_all(
        copies, ("seq", "dp"), 0, 0, tiled=True, axis_index_groups=near
    )
    return whole.reshape(len(near[0]) * part.shape[0], part.shape[1])


def on_device(n_dp, latents, cotangent, w_qkv, w_out):
    depth = latents.shape[-1]
    index = lax.axis_index("dp")
    at = jnp.stack([index % 2, index // 2 % 2]).astype(jnp.int32)
    near, far = groups_of(n_dp)
    x = latents.reshape(128, depth)
    g = cotangent.reshape(128, depth)
    w_own = w_qkv[0].reshape(3 * E, depth)

    hidden = call(
        norm_kernel, shape(8, 240, depth),
        at, x, w_qkv.reshape(2, 3, E, depth), w_out.reshape(2, E, depth),
        in_specs=[SMEM] + [VMEM] * 3, fetch=True,
        scratch_shapes=[pltpu.VMEM((4, E, depth), F32)],
    )
    hidden = over_head(hidden)
    heads, qkv, own, mine_one = call(
        spatial_kernel,
        (shape(8, E, 128), shape(2, 3 * E, 512), shape(8, E, depth), shape(8, 40, depth)),
        hidden, w_own,
    )
    own = own.reshape(8 * E, depth)
    heads = over_head(heads)
    mine_one = mine_one.reshape(320, depth)
    other_one = swap_cores(mine_one, n_dp)
    from_z = swap_cores(own, n_dp, 2)
    from_core = swap_cores(own, n_dp)
    big = shape(16 * E, depth)
    pair, from_z = call(
        middle_kernel, (shape(2, 2, 2, 32, depth), shape(8 * E, depth)),
        at, x, g, heads, mine_one, other_one, from_z,
        in_specs=[SMEM] + [VMEM] * 5 + [ANY], fetch=True,
        out_specs=(VMEM, ANY),
        input_output_aliases={6: 1},
        scratch_shapes=[pltpu.VMEM((2, 320, 128), F32)],
    )
    pair = over_seq(pair)
    from_both = swap_cores(from_z, n_dp)
    back, keep, send = call(
        temporal_kernel,
        (shape(2, 2, 2, 32, depth), big, big),
        at, pair, own, from_z, from_core, from_both,
        in_specs=[SMEM, VMEM] + [ANY] * 4,
        out_specs=(VMEM, ANY, ANY),
        scratch_shapes=[
            pltpu.VMEM((4, 8 * E, depth), BF),
            pltpu.VMEM((2, 16 * E, depth), BF),
            pltpu.VMEM((4, 8 * E, 128), F32),
            pltpu.VMEM((4, 8 * E, 128), F32),
            pltpu.SemaphoreType.DMA((4,)),
        ],
        mib=40,
    )
    back = over_seq(back)
    two = (keep.astype(F32) + swap_cores(send, n_dp).astype(F32)).astype(BF)
    two = lax.psum_scatter(
        two, "head", scatter_dimension=0, tiled=True, axis_index_groups=RING
    )
    half = shape(8, 40, depth)
    gh, keep, send, output, grad_one = call(
        turn_kernel,
        (shape(8, E, 128), half, half, shape(128, depth), shape(128, depth)),
        at, back, heads, mine_one, other_one,
        in_specs=[SMEM] + [VMEM] * 4, fetch=True,
        scratch_shapes=[pltpu.VMEM((2, 320, 128), F32)],
    )
    gh = over_head(gh)
    half = shape(112, depth)
    terms, keep, send = call(
        spatial_back_kernel, (shape(8, 176, depth), half, half),
        at, qkv, gh, hidden, w_own, keep, swap_cores(send, n_dp),
        in_specs=[SMEM] + [VMEM] * 6, mib=32,
    )
    n_near = len(near[0])
    latent_grads, chain = call(
        last_kernel, (shape(128, depth), shape(n_near, 320 // n_near, depth)),
        over_head(terms), x, grad_one, keep, swap_cores(send, n_dp), two,
        scratch_shapes=[pltpu.VMEM((320, depth), F32)], fetch=True,
    )
    part = sum_near(chain, near)
    mine = spread(sum_far(part, far), near)
    grad_qkv, grad_out = call(
        result_kernel,
        (
            jax.ShapeDtypeStruct((2, 3, E, depth), F32),
            jax.ShapeDtypeStruct((2, E, depth), F32),
        ),
        at, mine, swap_cores(mine, n_dp),
        in_specs=[SMEM, VMEM, VMEM],
        scratch_shapes=[pltpu.VMEM((2, 320, depth), F32)],
    )
    return (
        output.reshape(latents.shape),
        latent_grads.reshape(latents.shape),
        grad_qkv[:, None],
        grad_out[:, None],
    )


def solution(mesh):
    rows = P("dp", "seq", "head", None)
    specs = (rows, rows, P(None, "head", None, None, None), P(None, "head", None, None))
    return jax.shard_map(
        functools.partial(on_device, mesh.shape["dp"]),
        mesh=mesh, in_specs=specs, out_specs=specs, check_vma=False,
    )
```

```python
import functools

import jax
import jax.numpy as jnp
from jax import lax
from jax.experimental import pallas as pl
from jax.experimental.pallas import tpu as pltpu
from jax.sharding import PartitionSpec as P

EPSILON = 1e-06
E = 72
SCALE = E ** (-0.5)
RING = [[0, 2, 4, 6, 7, 5, 3, 1]]
ALONG_X = [[0, 2, 4, 6], [1, 3, 5, 7]]
BF = jnp.bfloat16
F32 = jnp.float32


def nn(a, b):
    return lax.dot_general(a, b, (((1,), (0,)), ((), ())), preferred_element_type=F32)


def nt(a, b):
    return lax.dot_general(a, b, (((1,), (1,)), ((), ())), preferred_element_type=F32)


def tn(a, b):
    return lax.dot_general(a, b, (((0,), (0,)), ((), ())), preferred_element_type=F32)


def normalize(rows):
    wide = rows.astype(F32)
    centered = wide - jnp.mean(wide, axis=-1, keepdims=True)
    inverse = lax.rsqrt(jnp.mean(centered * centered, axis=-1, keepdims=True) + EPSILON)
    return centered * inverse, inverse


def normalize_back(grad, inverse, normed, normed_grads):
    mean_grad = jnp.mean(normed_grads, axis=-1, keepdims=True)
    mean_cross = jnp.mean(normed_grads * normed, axis=-1, keepdims=True)
    return grad.astype(F32) + inverse * (normed_grads - mean_grad - normed * mean_cross)


def regroup(first, second):
    low = lax.broadcasted_iota(jnp.int32, first.shape, 1) < 64
    return (
        jnp.where(low, first, pltpu.roll(second, 64, 1)),
        jnp.where(low, pltpu.roll(first, 64, 1), second),
    )


def norm_kernel(at_ref, x_ref, wq_ref, wo_ref, out_ref, row_ref, own_ref):
    core = at_ref[0]
    wide = wo_ref[0].astype(F32)
    half = jnp.where(core == 0, wide[:40], wide[32:])
    hidden = normalize(x_ref[...])[0]
    block = jnp.concatenate([hidden, half], axis=0).astype(BF)
    row_ref[...] = block
    for j in range(4):
        out_ref[j] = block
    qk = jnp.concatenate([wq_ref[1, 0].astype(F32), wq_ref[1, 1].astype(F32)], axis=0)
    vo = jnp.concatenate([wq_ref[1, 2].astype(F32), wo_ref[1].astype(F32)], axis=0)
    own_ref[...] = jnp.where(core == 0, qk, vo).astype(BF)


def frame_rows(near_ref, far_ref, f):
    rows = [ref[:, f * 64 : (f + 1) * 64, :].reshape(256, ref.shape[2]) for ref in (near_ref, far_ref)]
    return jnp.concatenate(rows, axis=0)


def head_at(at_ref, slot):
    return 2 * (slot % 4) + (at_ref[1] if slot < 4 else 1 - at_ref[1])


def softmax(queries, key_rows):
    exponent = jnp.exp(tn(queries, key_rows) * SCALE)
    return exponent / jnp.sum(exponent, axis=1, keepdims=True)


def split3(stacked):
    return tuple(stacked[i * E : (i + 1) * E].astype(BF) for i in range(3))


def spatial_kernel(at_ref, near_ref, far_ref, w_ref, heads_ref, qkv_ref, one_ref):
    for i in range(8):
        block = (near_ref if i < 4 else far_ref)[i % 4].astype(F32)
        one_ref[head_at(at_ref, i)] = block[128:].astype(BF)
    outs = []
    for f in range(2):
        qkv = nt(w_ref[...], frame_rows(near_ref, far_ref, f))
        qkv_ref[f] = qkv.astype(BF)
        q, k, v = split3(qkv)
        weights = softmax(q, k).astype(BF)
        outs.append(nt(v, weights))
    for m in range(4):
        lanes = slice(m * 128, (m + 1) * 128)
        a, b = regroup(outs[0][:, lanes], outs[1][:, lanes])
        heads_ref[head_at(at_ref, 2 * m)] = a.astype(BF)
        heads_ref[head_at(at_ref, 2 * m + 1)] = b.astype(BF)


def middle_kernel(
    core_ref, x_ref, g_ref, heads_ref, mine_ref, other_ref, pass_ref, out_ref, same_ref, split_ref
):
    core = core_ref[0]
    for h in range(8):
        heads = heads_ref[h].astype(F32)
        split_ref[0, h * 40 : (h + 1) * 40] = heads[:40]
        low = jnp.zeros((8, 128), F32)
        split_ref[1, h * 40 : (h + 1) * 40] = jnp.concatenate([low, heads[40:]], axis=0)
    y = x_ref[...].astype(F32) + tn(split_ref[core].astype(BF), mine_ref[...])
    y = (y + tn(split_ref[1 - core].astype(BF), other_ref[...])).astype(BF)
    g = g_ref[...]
    for s in range(2):
        for f in range(2):
            rows = slice((2 * f + s) * 32, (2 * f + s + 1) * 32)
            out_ref[s, 0, f] = y[rows]
            out_ref[s, 1, f] = g[rows]


def temporal_kernel(
    core_ref, pair_ref, mine_ref, other_ref,
    back_ref, keep_ref, send_ref,
    w_ref, gw_ref, qk_ref, vg_ref, g0_ref, g1_ref, sems,
):
    core = core_ref[0]
    loads = (
        pltpu.make_async_copy(mine_ref, w_ref.at[core], sems.at[0]),
        pltpu.make_async_copy(other_ref, w_ref.at[1 - core], sems.at[1]),
    )
    for load in loads:
        load.start()
    depth = pair_ref.shape[-1]
    rows = jnp.concatenate([pair_ref[s, 0, f] for s in range(2) for f in range(2)], axis=0)
    grad = jnp.concatenate([pair_ref[s, 1, f] for s in range(2) for f in range(2)], axis=0)
    normed, inverse = normalize(rows)
    hidden = normed.astype(BF)
    both = jnp.concatenate([hidden, grad], axis=0)
    for load in loads:
        load.wait()
    qk_ref[...] = nt(w_ref[0], hidden)
    vg_ref[...] = nt(w_ref[1], both)

    def rounded(value):
        return value.astype(BF).astype(F32)

    def ahead(value, r):
        return pltpu.roll(value, 128 - 32 * r, 1) if r else value

    def behind(value, r):
        return pltpu.roll(value, 32 * r, 1) if r else value

    zeros = jnp.zeros((E, 128), F32)
    for h in range(8):
        base = h * 2 * E
        q = rounded(qk_ref[base : base + E])
        k = rounded(qk_ref[base + E : base + 2 * E])
        v = rounded(vg_ref[base : base + E, :128])
        gh = rounded(vg_ref[base + E : base + 2 * E, 128:])
        ks = [ahead(k, r) for r in range(4)]
        vs = [ahead(v, r) for r in range(4)]
        exps = [jnp.exp(jnp.sum(q * kr, axis=0, keepdims=True) * SCALE) for kr in ks]
        total = exps[0] + exps[1] + exps[2] + exps[3]
        probs = [e / total for e in exps]
        weights = [rounded(p) for p in probs]
        heads = sum(w * vr for w, vr in zip(weights, vs))
        gps = [jnp.sum(gh * vr, axis=0, keepdims=True) for vr in vs]
        inner = sum(p * gp for p, gp in zip(probs, gps))
        sgs = [rounded(p * (gp - inner) * SCALE) for p, gp in zip(probs, gps)]
        gq = sum(sg * kr for sg, kr in zip(sgs, ks))
        gk = sum(behind(sg * q, r) for r, sg in enumerate(sgs))
        gv = sum(behind(w * gh, r) for r, w in enumerate(weights))
        g0_ref[base : base + 2 * E] = jnp.concatenate([gq, gk], axis=0).astype(BF)
        g1_ref[base : base + 2 * E, :128] = jnp.concatenate([gv, zeros], axis=0).astype(BF)
        g1_ref[base : base + 2 * E, 128:] = jnp.concatenate([zeros, heads], axis=0).astype(BF)
    for h in range(8):
        span = slice(h * 2 * E, (h + 1) * 2 * E)
        gw_ref[0, span] = nn(g0_ref[span], hidden).astype(BF)
        gw_ref[1, span] = nn(g1_ref[span], both).astype(BF)
    stores = (
        pltpu.make_async_copy(gw_ref.at[core], keep_ref, sems.at[0]),
        pltpu.make_async_copy(gw_ref.at[1 - core], send_ref, sems.at[1]),
    )
    for store in stores:
        store.start()
    mixed = tn(g1_ref[...], w_ref[1])
    normed_grads = tn(g0_ref[...], w_ref[0]) + mixed[:128]
    result = (rows.astype(F32) + mixed[128:]).astype(BF)
    total_grad = normalize_back(grad, inverse, normed, normed_grads).astype(BF)
    for s in range(2):
        for f in range(2):
            at = slice((2 * s + f) * 32, (2 * s + f + 1) * 32)
            back_ref[s, 0, f] = result[at]
            back_ref[s, 1, f] = total_grad[at]
    for store in stores:
        store.wait()


def halves(rows, size):
    return rows[:size], rows[rows.shape[0] - size :]


def local_rows(pair_ref, which):
    return jnp.concatenate([pair_ref[s, which, f] for f in range(2) for s in range(2)], axis=0)


def turn_kernel(
    core_ref, back_ref, heads_ref, mine_ref, other_ref,
    gh_ref, keep_ref, send_ref, out_ref, grad_ref, split_ref,
):
    core = core_ref[0]
    out_ref[...] = local_rows(back_ref, 0)
    grad = local_rows(back_ref, 1)
    grad_ref[...] = grad
    split_ref[core] = nt(mine_ref[...], grad)
    split_ref[1 - core] = nt(other_ref[...], grad)
    for h in range(8):
        at = h * 40
        pieces = [split_ref[0, at : at + 40], split_ref[1, at + 8 : at + 40]]
        gh_ref[h] = jnp.concatenate(pieces, axis=0).astype(BF)
        low, high = halves(nn(heads_ref[h], grad), 40)
        keep_ref[h] = jnp.where(core == 0, low, high).astype(BF)
        send_ref[h] = jnp.where(core == 0, high, low).astype(BF)


def spatial_back_kernel(
    at_ref, qkv_ref, gh_ref, near_ref, far_ref, w_ref, mine_ref, recv_ref,
    first_ref, second_ref, keep_ref, send_ref,
):
    terms_refs = [second_ref] * 4 + [first_ref] * 4
    for i in range(8):
        j = head_at(at_ref, i)
        part = mine_ref[j].astype(F32) + recv_ref[j].astype(F32)
        low = jnp.zeros((8, part.shape[1]), F32)
        terms_refs[i][i % 4, 128:176, :] = jnp.concatenate([part, low], axis=0).astype(BF)
    frames = ([], [])
    for m in range(4):
        pair = regroup(*(gh_ref[head_at(at_ref, 2 * m + i)].astype(F32) for i in range(2)))
        for f in range(2):
            frames[f].append(pair[f])
    total = None
    for f in range(2):
        q, k, v = split3(qkv_ref[f].astype(F32))
        gh = jnp.concatenate(frames[f], axis=1).astype(BF)
        probs = softmax(q, k)
        gv = nn(gh, probs.astype(BF))
        gp = tn(gh, v)
        inner = jnp.sum(probs * gp, axis=1, keepdims=True)
        sg = (probs * (gp - inner) * SCALE).astype(BF)
        grads = jnp.concatenate([nt(k, sg), nn(q, sg), gv], axis=0).astype(BF)
        gw = nn(grads, frame_rows(near_ref, far_ref, f))
        total = gw if total is None else total + gw
        terms = tn(grads, w_ref[...]).astype(BF)
        for j in range(8):
            terms_refs[j][j % 4, f * 64 : (f + 1) * 64, :] = terms[j * 64 : (j + 1) * 64]
    low, high = halves(total, 112)
    keep_ref[...] = jnp.where(at_ref[0] == 0, low, high).astype(BF)
    send_ref[...] = jnp.where(at_ref[0] == 0, high, low).astype(BF)


def result_kernel(core_ref, mine_ref, other_ref, qkv_ref, out_ref, both_ref):
    core = core_ref[0]
    both_ref[core] = mine_ref[...].astype(F32)
    both_ref[1 - core] = other_ref[...].astype(F32)
    qkv = jnp.concatenate([both_ref[0, :112], both_ref[1, 8:112]], axis=0)
    for i in range(3):
        qkv_ref[0, i] = qkv[i * E : (i + 1) * E]
    out_ref[0] = jnp.concatenate([both_ref[0, 112:152], both_ref[1, 120:152]], axis=0)
    qkv_ref[1, 0] = both_ref[0, 152 : 152 + E]
    qkv_ref[1, 1] = both_ref[0, 152 + E : 152 + 2 * E]
    qkv_ref[1, 2] = both_ref[1, 152 : 152 + E]
    out_ref[1] = both_ref[1, 152 + E : 152 + 2 * E]


def half_sum_kernel(terms_ref, pass_ref, out_ref, same_ref):
    total = terms_ref[0].astype(F32)
    for j in range(1, 4):
        total = total + terms_ref[j].astype(F32)
    out_ref[...] = total.astype(BF)


def last_kernel(
    terms_ref, half_ref, x_ref, g_ref, keep_ref, recv_ref, two_ref, out_ref, chain_ref, rows_ref
):
    rows_ref[:112] = keep_ref[...].astype(F32) + recv_ref[...].astype(F32)
    total = half_ref[...].astype(F32)
    for j in range(4):
        total = total + terms_ref[j].astype(F32)
    rows_ref[112:152] = total[128:168]
    rows_ref[152:296] = two_ref[...].astype(F32)
    rows_ref[296:] = jnp.zeros_like(rows_ref[296:])
    for i in range(8):
        chain_ref[i] = rows_ref[i * 40 : (i + 1) * 40].astype(BF)
    normed, inverse = normalize(x_ref[...])
    out_ref[...] = normalize_back(g_ref[...], inverse, normed, total[:128]).astype(BF)


VMEM = pl.BlockSpec(memory_space=pltpu.VMEM)
SMEM = pl.BlockSpec(memory_space=pltpu.SMEM)
ANY = pl.BlockSpec(memory_space=pl.ANY)
PARAMS = pltpu.CompilerParams(vmem_limit_bytes=48 * 1024 * 1024)


def shape(*dims):
    return jax.ShapeDtypeStruct(dims, BF)


def call(kernel, outs, *args, **more):
    return pl.pallas_call(
        kernel,
        out_shape=outs,
        in_specs=more.pop("in_specs", [VMEM] * len(args)),
        out_specs=more.pop("out_specs", jax.tree.map(lambda _: VMEM, outs)),
        compiler_params=PARAMS,
        cost_estimate=pl.CostEstimate(flops=0, bytes_accessed=0, transcendentals=0),
        **more,
    )(*args)


def over_head(blocks):
    return lax.all_to_all(blocks, "head", 0, 0, tiled=True)


def over_x(blocks):
    return lax.all_to_all(blocks, "head", 0, 0, tiled=True, axis_index_groups=ALONG_X)


def swap_y(value):
    return lax.ppermute(value, "head", [(i, i ^ 1) for i in range(8)])


def over_seq(blocks):
    return lax.all_to_all(blocks, "seq", 0, 0, tiled=True)


def swap_cores(value, n_dp, bit=1):
    return lax.ppermute(value, "dp", [(i, i ^ bit) for i in range(n_dp)])


def groups_of(n_dp):
    n_z = n_dp // 2
    low = min(4, n_z)
    high = n_z // low
    near = [
        [s * n_dp + 2 * (b * low + a) + c for s in range(2) for a in range(low)]
        for b in range(high)
        for c in range(2)
    ]
    far = [
        [2 * (b * low + a) + c for b in range(high)] for a in range(low) for c in range(2)
    ]
    return near, far


def sum_near(grads, near):
    parts = lax.all_to_all(grads, ("seq", "dp"), 0, 0, tiled=True, axis_index_groups=near)
    return jnp.sum(parts.astype(F32), axis=0).astype(BF)


def sum_far(part, far):
    if len(far[0]) == 1:
        return part
    copies = jnp.broadcast_to(part[None], (len(far[0]), *part.shape))
    parts = lax.all_to_all(copies, "dp", 0, 0, tiled=True, axis_index_groups=far)
    return jnp.sum(parts.astype(F32), axis=0).astype(BF)


def spread(part, near):
    copies = jnp.broadcast_to(part[None], (len(near[0]), *part.shape))
    whole = lax.all_to_all(
        copies, ("seq", "dp"), 0, 0, tiled=True, axis_index_groups=near
    )
    return whole.reshape(len(near[0]) * part.shape[0], part.shape[1])


def on_device(n_dp, latents, cotangent, w_qkv, w_out):
    depth = latents.shape[-1]
    at = jnp.stack([lax.axis_index("dp") % 2, lax.axis_index("head") % 2]).astype(jnp.int32)
    near, far = groups_of(n_dp)
    x = latents.reshape(128, depth)
    g = cotangent.reshape(128, depth)
    w_own = w_qkv[0].reshape(3 * E, depth)

    hidden, row, own = call(
        norm_kernel, (shape(4, 168, depth), shape(168, depth), shape(2 * E, depth)),
        at, x, w_qkv.reshape(2, 3, E, depth), w_out.reshape(2, E, depth),
        in_specs=[SMEM] + [VMEM] * 3,
    )
    mine_two = lax.all_gather(own, "head", axis_index_groups=RING).reshape(16 * E, depth)
    hidden = over_x(hidden)
    partner = over_x(jnp.broadcast_to(swap_y(row)[None], (4, 168, depth)))
    heads, qkv, mine_one = call(
        spatial_kernel,
        (shape(8, E, 128), shape(2, 3 * E, 512), shape(8, 40, depth)),
        at, hidden, partner, w_own,
        in_specs=[SMEM] + [VMEM] * 3,
    )
    heads = over_head(heads)
    mine_one = mine_one.reshape(320, depth)
    other_one = swap_cores(mine_one, n_dp)
    big = shape(16 * E, depth)
    pair, mine_two = call(
        middle_kernel, (shape(2, 2, 2, 32, depth), big),
        at, x, g, heads, mine_one, other_one, mine_two,
        in_specs=[SMEM] + [VMEM] * 5 + [ANY],
        out_specs=(VMEM, ANY),
        input_output_aliases={6: 1},
        scratch_shapes=[pltpu.VMEM((2, 320, 128), F32)],
    )
    pair = over_seq(pair)
    other_two = swap_cores(mine_two, n_dp)
    back, keep, send = call(
        temporal_kernel,
        (shape(2, 2, 2, 32, depth), big, big),
        at, pair, mine_two, other_two,
        in_specs=[SMEM, VMEM, ANY, ANY],
        out_specs=(VMEM, ANY, ANY),
        scratch_shapes=[
            pltpu.VMEM((2, 16 * E, depth), BF),
            pltpu.VMEM((2, 16 * E, depth), BF),
            pltpu.VMEM((16 * E, 128), F32),
            pltpu.VMEM((16 * E, 256), F32),
            pltpu.VMEM((16 * E, 128), BF),
            pltpu.VMEM((16 * E, 256), BF),
            pltpu.SemaphoreType.DMA((2,)),
        ],
    )
    back = over_seq(back)
    two = (keep.astype(F32) + swap_cores(send, n_dp).astype(F32)).astype(BF)
    two = lax.psum_scatter(
        two, "head", scatter_dimension=0, tiled=True, axis_index_groups=RING
    )
    half = shape(8, 40, depth)
    gh, keep, send, output, grad_one = call(
        turn_kernel,
        (shape(8, E, 128), half, half, shape(128, depth), shape(128, depth)),
        at, back, heads, mine_one, other_one,
        in_specs=[SMEM] + [VMEM] * 4,
        scratch_shapes=[pltpu.VMEM((2, 320, 128), F32)],
    )
    gh = over_head(gh)
    half = shape(112, depth)
    terms = shape(4, 176, depth)
    first, second, keep, send = call(
        spatial_back_kernel, (terms, terms, half, half),
        at, qkv, gh, hidden, partner, w_own, keep, swap_cores(send, n_dp),
        in_specs=[SMEM] + [VMEM] * 7,
    )
    half_sum, second = call(
        half_sum_kernel, (shape(176, depth), terms), over_x(first), second,
        in_specs=[VMEM, ANY],
        out_specs=(VMEM, ANY),
        input_output_aliases={1: 1},
    )
    n_near = len(near[0])
    latent_grads, chain = call(
        last_kernel, (shape(128, depth), shape(n_near, 320 // n_near, depth)),
        over_x(second), swap_y(half_sum), x, grad_one, keep, swap_cores(send, n_dp), two,
        scratch_shapes=[pltpu.VMEM((320, depth), F32)],
    )
    part = sum_near(chain, near)
    mine = spread(sum_far(part, far), near)
    grad_qkv, grad_out = call(
        result_kernel,
        (
            jax.ShapeDtypeStruct((2, 3, E, depth), F32),
            jax.ShapeDtypeStruct((2, E, depth), F32),
        ),
        at, mine, swap_cores(mine, n_dp),
        in_specs=[SMEM, VMEM, VMEM],
        scratch_shapes=[pltpu.VMEM((2, 320, depth), F32)],
    )
    return (
        output.reshape(latents.shape),
        latent_grads.reshape(latents.shape),
        grad_qkv[:, None],
        grad_out[:, None],
    )


def solution(mesh):
    rows = P("dp", "seq", "head", None)
    specs = (rows, rows, P(None, "head", None, None, None), P(None, "head", None, None))
    return jax.shard_map(
        functools.partial(on_device, mesh.shape["dp"]),
        mesh=mesh, in_specs=specs, out_specs=specs, check_vma=False,
    )
```

```python
import functools

import jax
import jax.numpy as jnp
from jax import lax
from jax.experimental import pallas as pl
from jax.experimental.pallas import tpu as pltpu
from jax.sharding import PartitionSpec as P

EPSILON = 1e-06
E = 72
SCALE = E ** (-0.5)
RING = [[0, 2, 4, 6, 7, 5, 3, 1]]
ALONG_X = [[0, 2, 4, 6], [1, 3, 5, 7]]
BF = jnp.bfloat16
F32 = jnp.float32


def nn(a, b):
    return lax.dot_general(a, b, (((1,), (0,)), ((), ())), preferred_element_type=F32)


def nt(a, b):
    return lax.dot_general(a, b, (((1,), (1,)), ((), ())), preferred_element_type=F32)


def tn(a, b):
    return lax.dot_general(a, b, (((0,), (0,)), ((), ())), preferred_element_type=F32)


def normalize(rows):
    wide = rows.astype(F32)
    centered = wide - jnp.mean(wide, axis=-1, keepdims=True)
    inverse = lax.rsqrt(jnp.mean(centered * centered, axis=-1, keepdims=True) + EPSILON)
    return centered * inverse, inverse


def normalize_back(grad, inverse, normed, normed_grads):
    mean_grad = jnp.mean(normed_grads, axis=-1, keepdims=True)
    mean_cross = jnp.mean(normed_grads * normed, axis=-1, keepdims=True)
    return grad.astype(F32) + inverse * (normed_grads - mean_grad - normed * mean_cross)


def regroup(first, second):
    low = lax.broadcasted_iota(jnp.int32, first.shape, 1) < 64
    return (
        jnp.where(low, first, pltpu.roll(second, 64, 1)),
        jnp.where(low, pltpu.roll(first, 64, 1), second),
    )


def norm_kernel(at_ref, x_ref, wq_ref, wo_ref, out_ref, row_ref, own_ref):
    core = at_ref[0]
    wide = wo_ref[0].astype(F32)
    half = jnp.where(core == 0, wide[:40], wide[32:])
    hidden = normalize(x_ref[...])[0]
    block = jnp.concatenate([hidden, half], axis=0).astype(BF)
    row_ref[...] = block
    for j in range(4):
        out_ref[j] = block
    qk = jnp.concatenate([wq_ref[1, 0].astype(F32), wq_ref[1, 1].astype(F32)], axis=0)
    vo = jnp.concatenate([wq_ref[1, 2].astype(F32), wo_ref[1].astype(F32)], axis=0)
    own_ref[...] = jnp.where(core == 0, qk, vo).astype(BF)


def frame_rows(near_ref, far_ref, f):
    rows = [ref[:, f * 64 : (f + 1) * 64, :].reshape(256, ref.shape[2]) for ref in (near_ref, far_ref)]
    return jnp.concatenate(rows, axis=0)


def head_at(at_ref, slot):
    return 2 * (slot % 4) + (at_ref[1] if slot < 4 else 1 - at_ref[1])


def softmax(queries, key_rows):
    exponent = jnp.exp(tn(queries, key_rows) * SCALE)
    return exponent / jnp.sum(exponent, axis=1, keepdims=True)


def split3(stacked):
    return tuple(stacked[i * E : (i + 1) * E].astype(BF) for i in range(3))


def spatial_kernel(at_ref, near_ref, far_ref, w_ref, heads_ref, qkv_ref, one_ref):
    for i in range(8):
        block = (near_ref if i < 4 else far_ref)[i % 4].astype(F32)
        one_ref[head_at(at_ref, i)] = block[128:].astype(BF)
    outs = []
    for f in range(2):
        qkv = nt(w_ref[...], frame_rows(near_ref, far_ref, f))
        qkv_ref[f] = qkv.astype(BF)
        q, k, v = split3(qkv)
        weights = softmax(q, k).astype(BF)
        outs.append(nt(v, weights))
    for m in range(4):
        lanes = slice(m * 128, (m + 1) * 128)
        a, b = regroup(outs[0][:, lanes], outs[1][:, lanes])
        heads_ref[head_at(at_ref, 2 * m)] = a.astype(BF)
        heads_ref[head_at(at_ref, 2 * m + 1)] = b.astype(BF)


def middle_kernel(
    core_ref, x_ref, g_ref, heads_ref, mine_ref, other_ref, pass_ref, out_ref, same_ref, split_ref
):
    core = core_ref[0]
    for h in range(8):
        heads = heads_ref[h].astype(F32)
        split_ref[0, h * 40 : (h + 1) * 40] = heads[:40]
        low = jnp.zeros((8, 128), F32)
        split_ref[1, h * 40 : (h + 1) * 40] = jnp.concatenate([low, heads[40:]], axis=0)
    y = x_ref[...].astype(F32) + tn(split_ref[core].astype(BF), mine_ref[...])
    y = (y + tn(split_ref[1 - core].astype(BF), other_ref[...])).astype(BF)
    g = g_ref[...]
    for s in range(2):
        for f in range(2):
            rows = slice((2 * f + s) * 32, (2 * f + s + 1) * 32)
            out_ref[s, 0, f] = y[rows]
            out_ref[s, 1, f] = g[rows]


def temporal_kernel(
    core_ref, pair_ref, mine_ref, other_ref,
    back_ref, keep_ref, send_ref,
    w_ref, gw_ref, qk_ref, vg_ref, g0_ref, g1_ref, sems,
):
    core = core_ref[0]
    loads = (
        pltpu.make_async_copy(mine_ref, w_ref.at[core], sems.at[0]),
        pltpu.make_async_copy(other_ref, w_ref.at[1 - core], sems.at[1]),
    )
    for load in loads:
        load.start()
    depth = pair_ref.shape[-1]
    rows = jnp.concatenate([pair_ref[s, 0, f] for s in range(2) for f in range(2)], axis=0)
    grad = jnp.concatenate([pair_ref[s, 1, f] for s in range(2) for f in range(2)], axis=0)
    normed, inverse = normalize(rows)
    hidden = normed.astype(BF)
    both = jnp.concatenate([hidden, grad], axis=0)
    for load in loads:
        load.wait()
    qk_ref[...] = nt(w_ref[0], hidden)
    vg_ref[...] = nt(w_ref[1], both)

    def rounded(value):
        return value.astype(BF).astype(F32)

    def ahead(value, r):
        return pltpu.roll(value, 128 - 32 * r, 1) if r else value

    def behind(value, r):
        return pltpu.roll(value, 32 * r, 1) if r else value

    zeros = jnp.zeros((E, 128), F32)
    for h in range(8):
        base = h * 2 * E
        q = rounded(qk_ref[base : base + E])
        k = rounded(qk_ref[base + E : base + 2 * E])
        v = rounded(vg_ref[base : base + E, :128])
        gh = rounded(vg_ref[base + E : base + 2 * E, 128:])
        ks = [ahead(k, r) for r in range(4)]
        vs = [ahead(v, r) for r in range(4)]
        exps = [jnp.exp(jnp.sum(q * kr, axis=0, keepdims=True) * SCALE) for kr in ks]
        total = exps[0] + exps[1] + exps[2] + exps[3]
        probs = [e / total for e in exps]
        weights = [rounded(p) for p in probs]
        heads = sum(w * vr for w, vr in zip(weights, vs))
        gps = [jnp.sum(gh * vr, axis=0, keepdims=True) for vr in vs]
        inner = sum(p * gp for p, gp in zip(probs, gps))
        sgs = [rounded(p * (gp - inner) * SCALE) for p, gp in zip(probs, gps)]
        gq = sum(sg * kr for sg, kr in zip(sgs, ks))
        gk = sum(behind(sg * q, r) for r, sg in enumerate(sgs))
        gv = sum(behind(w * gh, r) for r, w in enumerate(weights))
        g0_ref[base : base + 2 * E] = jnp.concatenate([gq, gk], axis=0).astype(BF)
        g1_ref[base : base + 2 * E, :128] = jnp.concatenate([gv, zeros], axis=0).astype(BF)
        g1_ref[base : base + 2 * E, 128:] = jnp.concatenate([zeros, heads], axis=0).astype(BF)
    for h in range(8):
        span = slice(h * 2 * E, (h + 1) * 2 * E)
        gw_ref[0, span] = nn(g0_ref[span], hidden).astype(BF)
        gw_ref[1, span] = nn(g1_ref[span], both).astype(BF)
    stores = (
        pltpu.make_async_copy(gw_ref.at[core], keep_ref, sems.at[0]),
        pltpu.make_async_copy(gw_ref.at[1 - core], send_ref, sems.at[1]),
    )
    for store in stores:
        store.start()
    mixed = tn(g1_ref[...], w_ref[1])
    normed_grads = tn(g0_ref[...], w_ref[0]) + mixed[:128]
    result = (rows.astype(F32) + mixed[128:]).astype(BF)
    total_grad = normalize_back(grad, inverse, normed, normed_grads).astype(BF)
    for s in range(2):
        for f in range(2):
            at = slice((2 * s + f) * 32, (2 * s + f + 1) * 32)
            back_ref[s, 0, f] = result[at]
            back_ref[s, 1, f] = total_grad[at]
    for store in stores:
        store.wait()


def halves(rows, size):
    return rows[:size], rows[rows.shape[0] - size :]


def local_rows(pair_ref, which):
    return jnp.concatenate([pair_ref[s, which, f] for f in range(2) for s in range(2)], axis=0)


def turn_kernel(
    core_ref, back_ref, heads_ref, mine_ref, other_ref,
    gh_ref, keep_ref, send_ref, out_ref, grad_ref, split_ref,
):
    core = core_ref[0]
    out_ref[...] = local_rows(back_ref, 0)
    grad = local_rows(back_ref, 1)
    grad_ref[...] = grad
    split_ref[core] = nt(mine_ref[...], grad)
    split_ref[1 - core] = nt(other_ref[...], grad)
    for h in range(8):
        at = h * 40
        pieces = [split_ref[0, at : at + 40], split_ref[1, at + 8 : at + 40]]
        gh_ref[h] = jnp.concatenate(pieces, axis=0).astype(BF)
        low, high = halves(nn(heads_ref[h], grad), 40)
        keep_ref[h] = jnp.where(core == 0, low, high).astype(BF)
        send_ref[h] = jnp.where(core == 0, high, low).astype(BF)


def spatial_back_kernel(
    at_ref, qkv_ref, gh_ref, near_ref, far_ref, w_ref,
    a0_ref, a1_ref, a2_ref, a3_ref, b0_ref, b1_ref, b2_ref, b3_ref, keep_ref, send_ref, rows_ref,
):
    frames = ([], [])
    for m in range(4):
        pair = regroup(*(gh_ref[head_at(at_ref, 2 * m + i)].astype(F32) for i in range(2)))
        for f in range(2):
            frames[f].append(pair[f])
    total = None
    for f in range(2):
        q, k, v = split3(qkv_ref[f].astype(F32))
        gh = jnp.concatenate(frames[f], axis=1).astype(BF)
        probs = softmax(q, k)
        gv = nn(gh, probs.astype(BF))
        gp = tn(gh, v)
        inner = jnp.sum(probs * gp, axis=1, keepdims=True)
        sg = (probs * (gp - inner) * SCALE).astype(BF)
        grads = jnp.concatenate([nt(k, sg), nn(q, sg), gv], axis=0).astype(BF)
        gw = nn(grads, frame_rows(near_ref, far_ref, f))
        total = gw if total is None else total + gw
        terms = tn(grads, w_ref[...]).astype(BF)
        for j in range(8):
            rows_ref[j, f * 64 : (f + 1) * 64, :] = terms[j * 64 : (j + 1) * 64]
    ahead = ((a0_ref, b0_ref), (a1_ref, b1_ref), (a2_ref, b2_ref), (a3_ref, b3_ref))
    for k, (other_ref, own_ref) in enumerate(ahead):
        x_at = lax.rem(at_ref[2] + k, 4)
        own_ref[...] = rows_ref[x_at]
        other_ref[...] = rows_ref[4 + x_at]
    low, high = halves(total, 112)
    keep_ref[...] = jnp.where(at_ref[0] == 0, low, high).astype(BF)
    send_ref[...] = jnp.where(at_ref[0] == 0, high, low).astype(BF)


def result_kernel(core_ref, mine_ref, other_ref, qkv_ref, out_ref, both_ref):
    core = core_ref[0]
    both_ref[core] = mine_ref[...].astype(F32)
    both_ref[1 - core] = other_ref[...].astype(F32)
    qkv = jnp.concatenate([both_ref[0, :112], both_ref[1, 8:112]], axis=0)
    for i in range(3):
        qkv_ref[0, i] = qkv[i * E : (i + 1) * E]
    out_ref[0] = jnp.concatenate([both_ref[0, 112:152], both_ref[1, 120:152]], axis=0)
    qkv_ref[1, 0] = both_ref[0, 152 : 152 + E]
    qkv_ref[1, 1] = both_ref[0, 152 + E : 152 + 2 * E]
    qkv_ref[1, 2] = both_ref[1, 152 : 152 + E]
    out_ref[1] = both_ref[1, 152 + E : 152 + 2 * E]


def chain_kernel(keep_ref, recv_ref, parts_ref, two_ref, chain_ref, rows_ref):
    rows_ref[:112] = keep_ref[...].astype(F32) + recv_ref[...].astype(F32)
    rows_ref[112:152] = block_sum(parts_ref)
    rows_ref[152:296] = two_ref[...].astype(F32)
    rows_ref[296:] = jnp.zeros_like(rows_ref[296:])
    n, size = chain_ref.shape[:2]
    for i in range(n):
        chain_ref[i] = rows_ref[i * size : (i + 1) * size].astype(BF)


def block_sum(ref):
    total = ref[0].astype(F32)
    for j in range(1, ref.shape[0]):
        total = total + ref[j].astype(F32)
    return total


def copy_sum(blocks_ref, out_ref):
    total = block_sum(blocks_ref).astype(BF)
    for i in range(out_ref.shape[0]):
        out_ref[i] = total


def half_sum_kernel(t0_ref, t1_ref, t2_ref, t3_ref, grads_ref, out_ref, copies_ref):
    out_ref[...] = row_sum(t0_ref, t1_ref, t2_ref, t3_ref).astype(BF)
    copy_sum(grads_ref, copies_ref)


def row_sum(*refs):
    total = refs[0][...].astype(F32)
    for ref in refs[1:]:
        total = total + ref[...].astype(F32)
    return total


def last_kernel(
    t0_ref, t1_ref, t2_ref, t3_ref, half_ref, x_ref, g_ref, grads_ref, out_ref, copies_ref
):
    copy_sum(grads_ref, copies_ref)
    total = row_sum(t0_ref, t1_ref, t2_ref, t3_ref, half_ref)
    normed, inverse = normalize(x_ref[...])
    out_ref[...] = normalize_back(g_ref[...], inverse, normed, total).astype(BF)


VMEM = pl.BlockSpec(memory_space=pltpu.VMEM)
SMEM = pl.BlockSpec(memory_space=pltpu.SMEM)
ANY = pl.BlockSpec(memory_space=pl.ANY)
PARAMS = pltpu.CompilerParams(vmem_limit_bytes=48 * 1024 * 1024)


def shape(*dims):
    return jax.ShapeDtypeStruct(dims, BF)


def call(kernel, outs, *args, **more):
    return pl.pallas_call(
        kernel,
        out_shape=outs,
        in_specs=more.pop("in_specs", [VMEM] * len(args)),
        out_specs=more.pop("out_specs", jax.tree.map(lambda _: VMEM, outs)),
        compiler_params=PARAMS,
        cost_estimate=pl.CostEstimate(flops=0, bytes_accessed=0, transcendentals=0),
        **more,
    )(*args)


def over_head(blocks):
    return lax.all_to_all(blocks, "head", 0, 0, tiled=True)


def over_x(blocks):
    return lax.all_to_all(blocks, "head", 0, 0, tiled=True, axis_index_groups=ALONG_X)


def shift_x(blocks):
    perms = [[(i, (i + 2 * k) % 8) for i in range(8)] for k in range(4)]
    moved = [lax.ppermute(blocks[k], "head", perms[k]) for k in (2, 1, 3)]
    return [blocks[0], *moved]


def swap_y(value):
    return lax.ppermute(value, "head", [(i, i ^ 1) for i in range(8)])


def over_seq(blocks):
    return lax.all_to_all(blocks, "seq", 0, 0, tiled=True)


def swap_cores(value, n_dp, bit=1):
    return lax.ppermute(value, "dp", [(i, i ^ bit) for i in range(n_dp)])


def groups_of(n_dp):
    n_z = n_dp // 2
    low = min(4, n_z)
    high = n_z // low
    near = [
        [s * n_dp + 2 * (b * low + a) + c for s in range(2) for a in range(low)]
        for b in range(high)
        for c in range(2)
    ]
    far = [
        [2 * (b * low + a) + c for b in range(high)] for a in range(low) for c in range(2)
    ]
    return near, far


def over_near(blocks, near):
    return lax.all_to_all(blocks, ("seq", "dp"), 0, 0, tiled=True, axis_index_groups=near)


def on_device(n_dp, latents, cotangent, w_qkv, w_out):
    depth = latents.shape[-1]
    index = lax.axis_index("head")
    at = jnp.stack([lax.axis_index("dp") % 2, index % 2, index // 2]).astype(jnp.int32)
    near, far = groups_of(n_dp)
    x = latents.reshape(128, depth)
    g = cotangent.reshape(128, depth)
    w_own = w_qkv[0].reshape(3 * E, depth)

    hidden, row, own = call(
        norm_kernel, (shape(4, 168, depth), shape(168, depth), shape(2 * E, depth)),
        at, x, w_qkv.reshape(2, 3, E, depth), w_out.reshape(2, E, depth),
        in_specs=[SMEM] + [VMEM] * 3,
    )
    mine_two = lax.all_gather(own, "head", axis_index_groups=RING).reshape(16 * E, depth)
    hidden = over_x(hidden)
    partner = over_x(jnp.broadcast_to(swap_y(row)[None], (4, 168, depth)))
    heads, qkv, mine_one = call(
        spatial_kernel,
        (shape(8, E, 128), shape(2, 3 * E, 512), shape(8, 40, depth)),
        at, hidden, partner, w_own,
        in_specs=[SMEM] + [VMEM] * 3,
    )
    heads = over_head(heads)
    mine_one = mine_one.reshape(320, depth)
    other_one = swap_cores(mine_one, n_dp)
    big = shape(16 * E, depth)
    pair, mine_two = call(
        middle_kernel, (shape(2, 2, 2, 32, depth), big),
        at, x, g, heads, mine_one, other_one, mine_two,
        in_specs=[SMEM] + [VMEM] * 5 + [ANY],
        out_specs=(VMEM, ANY),
        input_output_aliases={6: 1},
        scratch_shapes=[pltpu.VMEM((2, 320, 128), F32)],
    )
    pair = over_seq(pair)
    other_two = swap_cores(mine_two, n_dp)
    back, keep, send = call(
        temporal_kernel,
        (shape(2, 2, 2, 32, depth), big, big),
        at, pair, mine_two, other_two,
        in_specs=[SMEM, VMEM, ANY, ANY],
        out_specs=(VMEM, ANY, ANY),
        scratch_shapes=[
            pltpu.VMEM((2, 16 * E, depth), BF),
            pltpu.VMEM((2, 16 * E, depth), BF),
            pltpu.VMEM((16 * E, 128), F32),
            pltpu.VMEM((16 * E, 256), F32),
            pltpu.VMEM((16 * E, 128), BF),
            pltpu.VMEM((16 * E, 256), BF),
            pltpu.SemaphoreType.DMA((2,)),
        ],
    )
    back = over_seq(back)
    two = (keep.astype(F32) + swap_cores(send, n_dp).astype(F32)).astype(BF)
    two = lax.psum_scatter(
        two, "head", scatter_dimension=0, tiled=True, axis_index_groups=RING
    )
    half = shape(8, 40, depth)
    gh, keep, send, output, grad_one = call(
        turn_kernel,
        (shape(8, E, 128), half, half, shape(128, depth), shape(128, depth)),
        at, back, heads, mine_one, other_one,
        in_specs=[SMEM] + [VMEM] * 4,
        scratch_shapes=[pltpu.VMEM((2, 320, 128), F32)],
    )
    gh = over_head(gh)
    parts = over_head((keep.astype(F32) + swap_cores(send, n_dp).astype(F32)).astype(BF))
    half, row = shape(112, depth), shape(128, depth)
    *terms, keep, send = call(
        spatial_back_kernel, (*[row] * 8, half, half),
        at, qkv, gh, hidden, partner, w_own,
        in_specs=[SMEM] + [VMEM] * 5,
        scratch_shapes=[pltpu.VMEM((8, 128, depth), BF)],
    )
    n_near, n_far = len(near[0]), len(far[0])
    size = 320 // n_near
    chain = call(
        chain_kernel, shape(n_near, size, depth), keep, swap_cores(send, n_dp), parts, two,
        scratch_shapes=[pltpu.VMEM((320, depth), F32)],
    )
    half, copies = call(
        half_sum_kernel, (row, shape(n_far, size, depth)),
        *shift_x(terms[:4]), over_near(chain, near),
    )
    summed = lax.all_to_all(copies, "dp", 0, 0, tiled=True, axis_index_groups=far)
    latent_grads, copies = call(
        last_kernel, (shape(128, depth), shape(n_near, size, depth)),
        *shift_x(terms[4:]), swap_y(half), x, grad_one, summed,
    )
    mine = over_near(copies, near).reshape(320, depth)
    grad_qkv, grad_out = call(
        result_kernel,
        (
            jax.ShapeDtypeStruct((2, 3, E, depth), F32),
            jax.ShapeDtypeStruct((2, E, depth), F32),
        ),
        at, mine, swap_cores(mine, n_dp),
        in_specs=[SMEM, VMEM, VMEM],
        scratch_shapes=[pltpu.VMEM((2, 320, depth), F32)],
    )
    return (
        output.reshape(latents.shape),
        latent_grads.reshape(latents.shape),
        grad_qkv[:, None],
        grad_out[:, None],
    )


def solution(mesh):
    rows = P("dp", "seq", "head", None)
    specs = (rows, rows, P(None, "head", None, None, None), P(None, "head", None, None))
    return jax.shard_map(
        functools.partial(on_device, mesh.shape["dp"]),
        mesh=mesh, in_specs=specs, out_specs=specs, check_vma=False,
    )
```

```python
import functools

import jax
import jax.numpy as jnp
from jax import lax
from jax.experimental import pallas as pl
from jax.experimental.pallas import tpu as pltpu
from jax.sharding import PartitionSpec as P

EPSILON = 1e-06
E = 72
SCALE = E ** (-0.5)
RING = [[0, 2, 4, 6, 7, 5, 3, 1]]
ALONG_X = [[0, 2, 4, 6], [1, 3, 5, 7]]
BF = jnp.bfloat16
F32 = jnp.float32


def nn(a, b):
    return lax.dot_general(a, b, (((1,), (0,)), ((), ())), preferred_element_type=F32)


def nt(a, b):
    return lax.dot_general(a, b, (((1,), (1,)), ((), ())), preferred_element_type=F32)


def tn(a, b):
    return lax.dot_general(a, b, (((0,), (0,)), ((), ())), preferred_element_type=F32)


def normalize(rows):
    wide = rows.astype(F32)
    centered = wide - jnp.mean(wide, axis=-1, keepdims=True)
    inverse = lax.rsqrt(jnp.mean(centered * centered, axis=-1, keepdims=True) + EPSILON)
    return centered * inverse, inverse


def normalize_back(grad, inverse, normed, normed_grads):
    mean_grad = jnp.mean(normed_grads, axis=-1, keepdims=True)
    mean_cross = jnp.mean(normed_grads * normed, axis=-1, keepdims=True)
    return grad.astype(F32) + inverse * (normed_grads - mean_grad - normed * mean_cross)


def regroup(first, second):
    low = lax.broadcasted_iota(jnp.int32, first.shape, 1) < 64
    return (
        jnp.where(low, first, pltpu.roll(second, 64, 1)),
        jnp.where(low, pltpu.roll(first, 64, 1), second),
    )


def norm_kernel(at_ref, x_ref, wq_ref, wo_ref, out_ref, row_ref, own_ref):
    core = at_ref[0]
    wide = wo_ref[0].astype(F32)
    half = jnp.where(core == 0, wide[:40], wide[32:])
    hidden = normalize(x_ref[...])[0]
    block = jnp.concatenate([hidden, half], axis=0).astype(BF)
    row_ref[...] = block
    for j in range(4):
        out_ref[j] = block
    qk = jnp.concatenate([wq_ref[1, 0].astype(F32), wq_ref[1, 1].astype(F32)], axis=0)
    vo = jnp.concatenate([wq_ref[1, 2].astype(F32), wo_ref[1].astype(F32)], axis=0)
    own_ref[...] = jnp.where(core == 0, qk, vo).astype(BF)


def frame_rows(near_ref, far_ref, f):
    rows = [ref[:, f * 64 : (f + 1) * 64, :].reshape(256, ref.shape[2]) for ref in (near_ref, far_ref)]
    return jnp.concatenate(rows, axis=0)


def head_at(at_ref, slot):
    return 2 * (slot % 4) + (at_ref[1] if slot < 4 else 1 - at_ref[1])


def softmax(queries, key_rows):
    exponent = jnp.exp(tn(queries, key_rows) * SCALE)
    return exponent / jnp.sum(exponent, axis=1, keepdims=True)


def split3(stacked):
    return tuple(stacked[i * E : (i + 1) * E].astype(BF) for i in range(3))


def spatial_kernel(at_ref, near_ref, far_ref, w_ref, heads_ref, qkv_ref, one_ref):
    for i in range(8):
        block = (near_ref if i < 4 else far_ref)[i % 4].astype(F32)
        one_ref[head_at(at_ref, i)] = block[128:].astype(BF)
    outs = []
    for f in range(2):
        qkv = nt(w_ref[...], frame_rows(near_ref, far_ref, f))
        qkv_ref[f] = qkv.astype(BF)
        q, k, v = split3(qkv)
        weights = softmax(q, k).astype(BF)
        outs.append(nt(v, weights))
    for m in range(4):
        lanes = slice(m * 128, (m + 1) * 128)
        a, b = regroup(outs[0][:, lanes], outs[1][:, lanes])
        heads_ref[head_at(at_ref, 2 * m)] = a.astype(BF)
        heads_ref[head_at(at_ref, 2 * m + 1)] = b.astype(BF)


def middle_kernel(
    core_ref, x_ref, g_ref, heads_ref, mine_ref, other_ref, pass_ref, out_ref, same_ref, split_ref
):
    core = core_ref[0]
    for h in range(8):
        heads = heads_ref[h].astype(F32)
        split_ref[0, h * 40 : (h + 1) * 40] = heads[:40]
        low = jnp.zeros((8, 128), F32)
        split_ref[1, h * 40 : (h + 1) * 40] = jnp.concatenate([low, heads[40:]], axis=0)
    y = x_ref[...].astype(F32) + tn(split_ref[core].astype(BF), mine_ref[...])
    y = (y + tn(split_ref[1 - core].astype(BF), other_ref[...])).astype(BF)
    g = g_ref[...]
    for s in range(2):
        for f in range(2):
            rows = slice((2 * f + s) * 32, (2 * f + s + 1) * 32)
            out_ref[s, 0, f] = y[rows]
            out_ref[s, 1, f] = g[rows]


def temporal_kernel(
    core_ref, pair_ref, mine_ref, other_ref,
    back_ref, keep_ref, send_ref,
    w_ref, gw_ref, qk_ref, vg_ref, g0_ref, g1_ref, sems,
):
    core = core_ref[0]
    loads = (
        pltpu.make_async_copy(mine_ref, w_ref.at[core], sems.at[0]),
        pltpu.make_async_copy(other_ref, w_ref.at[1 - core], sems.at[1]),
    )
    for load in loads:
        load.start()
    depth = pair_ref.shape[-1]
    rows = jnp.concatenate([pair_ref[s, 0, f] for s in range(2) for f in range(2)], axis=0)
    grad = jnp.concatenate([pair_ref[s, 1, f] for s in range(2) for f in range(2)], axis=0)
    normed, inverse = normalize(rows)
    hidden = normed.astype(BF)
    both = jnp.concatenate([hidden, grad], axis=0)
    for load in loads:
        load.wait()
    qk_ref[...] = nt(w_ref[0], hidden)
    vg_ref[...] = nt(w_ref[1], both)

    def rounded(value):
        return value.astype(BF).astype(F32)

    def ahead(value, r):
        return pltpu.roll(value, 128 - 32 * r, 1) if r else value

    def behind(value, r):
        return pltpu.roll(value, 32 * r, 1) if r else value

    zeros = jnp.zeros((E, 128), F32)
    for h in range(8):
        base = h * 2 * E
        q = rounded(qk_ref[base : base + E])
        k = rounded(qk_ref[base + E : base + 2 * E])
        v = rounded(vg_ref[base : base + E, :128])
        gh = rounded(vg_ref[base + E : base + 2 * E, 128:])
        ks = [ahead(k, r) for r in range(4)]
        vs = [ahead(v, r) for r in range(4)]
        exps = [jnp.exp(jnp.sum(q * kr, axis=0, keepdims=True) * SCALE) for kr in ks]
        total = exps[0] + exps[1] + exps[2] + exps[3]
        probs = [e / total for e in exps]
        weights = [rounded(p) for p in probs]
        heads = sum(w * vr for w, vr in zip(weights, vs))
        gps = [jnp.sum(gh * vr, axis=0, keepdims=True) for vr in vs]
        inner = sum(p * gp for p, gp in zip(probs, gps))
        sgs = [rounded(p * (gp - inner) * SCALE) for p, gp in zip(probs, gps)]
        gq = sum(sg * kr for sg, kr in zip(sgs, ks))
        gk = sum(behind(sg * q, r) for r, sg in enumerate(sgs))
        gv = sum(behind(w * gh, r) for r, w in enumerate(weights))
        g0_ref[base : base + 2 * E] = jnp.concatenate([gq, gk], axis=0).astype(BF)
        g1_ref[base : base + 2 * E, :128] = jnp.concatenate([gv, zeros], axis=0).astype(BF)
        g1_ref[base : base + 2 * E, 128:] = jnp.concatenate([zeros, heads], axis=0).astype(BF)
    for h in range(8):
        span = slice(h * 2 * E, (h + 1) * 2 * E)
        gw_ref[0, span] = nn(g0_ref[span], hidden).astype(BF)
        gw_ref[1, span] = nn(g1_ref[span], both).astype(BF)
    stores = (
        pltpu.make_async_copy(gw_ref.at[core], keep_ref, sems.at[0]),
        pltpu.make_async_copy(gw_ref.at[1 - core], send_ref, sems.at[1]),
    )
    for store in stores:
        store.start()
    mixed = tn(g1_ref[...], w_ref[1])
    normed_grads = tn(g0_ref[...], w_ref[0]) + mixed[:128]
    result = (rows.astype(F32) + mixed[128:]).astype(BF)
    total_grad = normalize_back(grad, inverse, normed, normed_grads).astype(BF)
    for s in range(2):
        for f in range(2):
            at = slice((2 * s + f) * 32, (2 * s + f + 1) * 32)
            back_ref[s, 0, f] = result[at]
            back_ref[s, 1, f] = total_grad[at]
    for store in stores:
        store.wait()


def halves(rows, size):
    return rows[:size], rows[rows.shape[0] - size :]


def local_rows(pair_ref, which):
    return jnp.concatenate([pair_ref[s, which, f] for f in range(2) for s in range(2)], axis=0)


def turn_kernel(
    core_ref, back_ref, heads_ref, mine_ref, other_ref,
    gh_ref, keep_ref, send_ref, out_ref, grad_ref, split_ref,
):
    core = core_ref[0]
    out_ref[...] = local_rows(back_ref, 0)
    grad = local_rows(back_ref, 1)
    grad_ref[...] = grad
    split_ref[core] = nt(mine_ref[...], grad)
    split_ref[1 - core] = nt(other_ref[...], grad)
    for h in range(8):
        at = h * 40
        pieces = [split_ref[0, at : at + 40], split_ref[1, at + 8 : at + 40]]
        gh_ref[h] = jnp.concatenate(pieces, axis=0).astype(BF)
        low, high = halves(nn(heads_ref[h], grad), 40)
        keep_ref[h] = jnp.where(core == 0, low, high).astype(BF)
        send_ref[h] = jnp.where(core == 0, high, low).astype(BF)


def spatial_back_kernel(
    at_ref, qkv_ref, gh_ref, near_ref, far_ref, w_ref,
    a0_ref, a1_ref, a2_ref, a3_ref, b0_ref, b1_ref, b2_ref, b3_ref, keep_ref, send_ref, rows_ref, sems,
):
    frames = ([], [])
    for m in range(4):
        pair = regroup(*(gh_ref[head_at(at_ref, 2 * m + i)].astype(F32) for i in range(2)))
        for f in range(2):
            frames[f].append(pair[f])
    total = None
    for f in range(2):
        q, k, v = split3(qkv_ref[f].astype(F32))
        gh = jnp.concatenate(frames[f], axis=1).astype(BF)
        probs = softmax(q, k)
        gv = nn(gh, probs.astype(BF))
        gp = tn(gh, v)
        inner = jnp.sum(probs * gp, axis=1, keepdims=True)
        sg = (probs * (gp - inner) * SCALE).astype(BF)
        grads = jnp.concatenate([nt(k, sg), nn(q, sg), gv], axis=0).astype(BF)
        gw = nn(grads, frame_rows(near_ref, far_ref, f))
        total = gw if total is None else total + gw
        terms = tn(grads, w_ref[...]).astype(BF)
        for j in range(8):
            rows_ref[j, f * 64 : (f + 1) * 64, :] = terms[j * 64 : (j + 1) * 64]
    copies = []
    ahead = ((a0_ref, b0_ref), (a1_ref, b1_ref), (a2_ref, b2_ref), (a3_ref, b3_ref))
    for k, (other_ref, own_ref) in enumerate(ahead):
        x_at = lax.rem(at_ref[2] + k, 4)
        copies.append(pltpu.make_async_copy(rows_ref.at[x_at], own_ref, sems.at[k]))
        copies.append(pltpu.make_async_copy(rows_ref.at[4 + x_at], other_ref, sems.at[4 + k]))
    for copy in copies:
        copy.start()
    low, high = halves(total, 112)
    keep_ref[...] = jnp.where(at_ref[0] == 0, low, high).astype(BF)
    send_ref[...] = jnp.where(at_ref[0] == 0, high, low).astype(BF)
    for copy in copies:
        copy.wait()


def result_kernel(core_ref, mine_ref, other_ref, qkv_ref, out_ref, both_ref):
    core = core_ref[0]
    both_ref[core] = mine_ref[...].astype(F32)
    both_ref[1 - core] = other_ref[...].astype(F32)
    qkv = jnp.concatenate([both_ref[0, :112], both_ref[1, 8:112]], axis=0)
    for i in range(3):
        qkv_ref[0, i] = qkv[i * E : (i + 1) * E]
    out_ref[0] = jnp.concatenate([both_ref[0, 112:152], both_ref[1, 120:152]], axis=0)
    qkv_ref[1, 0] = both_ref[0, 152 : 152 + E]
    qkv_ref[1, 1] = both_ref[0, 152 + E : 152 + 2 * E]
    qkv_ref[1, 2] = both_ref[1, 152 : 152 + E]
    out_ref[1] = both_ref[1, 152 + E : 152 + 2 * E]


def chain_kernel(keep_ref, recv_ref, parts_ref, two_ref, chain_ref, rows_ref):
    rows_ref[:112] = keep_ref[...].astype(F32) + recv_ref[...].astype(F32)
    rows_ref[112:152] = block_sum(parts_ref)
    rows_ref[152:296] = two_ref[...].astype(F32)
    rows_ref[296:] = jnp.zeros_like(rows_ref[296:])
    n, size = chain_ref.shape[:2]
    for i in range(n):
        chain_ref[i] = rows_ref[i * size : (i + 1) * size].astype(BF)


def block_sum(ref):
    total = ref[0].astype(F32)
    for j in range(1, ref.shape[0]):
        total = total + ref[j].astype(F32)
    return total


def copy_sum(blocks_ref, out_ref):
    total = block_sum(blocks_ref).astype(BF)
    for i in range(out_ref.shape[0]):
        out_ref[i] = total


def half_sum_kernel(t0_ref, t1_ref, t2_ref, t3_ref, grads_ref, out_ref, copies_ref):
    out_ref[...] = row_sum(t0_ref, t1_ref, t2_ref, t3_ref).astype(BF)
    copy_sum(grads_ref, copies_ref)


def row_sum(*refs):
    total = refs[0][...].astype(F32)
    for ref in refs[1:]:
        total = total + ref[...].astype(F32)
    return total


def last_kernel(
    t0_ref, t1_ref, t2_ref, t3_ref, half_ref, x_ref, g_ref, grads_ref, out_ref, copies_ref
):
    copy_sum(grads_ref, copies_ref)
    total = row_sum(t0_ref, t1_ref, t2_ref, t3_ref, half_ref)
    normed, inverse = normalize(x_ref[...])
    out_ref[...] = normalize_back(g_ref[...], inverse, normed, total).astype(BF)


VMEM = pl.BlockSpec(memory_space=pltpu.VMEM)
SMEM = pl.BlockSpec(memory_space=pltpu.SMEM)
HBM = pl.BlockSpec(memory_space=pltpu.HBM)
MIB = 1024 * 1024


def shape(*dims):
    return jax.ShapeDtypeStruct(dims, BF)


def call(kernel, outs, *args, mib=48, fetch=(), in_specs=None, scratch_shapes=(), **more):
    specs = list(in_specs or [VMEM] * len(args))
    scratch = list(scratch_shapes)
    moved = list(fetch)
    n_in, n_out, n_own = len(args), len(jax.tree.leaves(outs)), len(scratch)

    def fetching(*refs):
        ins = list(refs[:n_in])
        rest = refs[n_in : n_in + n_out + n_own]
        held, sems = refs[n_in + n_out + n_own : -1], refs[-1]
        copies = [
            pltpu.make_async_copy(ins[i], to, sems.at[k])
            for k, (i, to) in enumerate(zip(moved, held))
        ]
        for copy in copies:
            copy.start()
        for copy in copies:
            copy.wait()
        for i, to in zip(moved, held):
            ins[i] = to
        kernel(*ins, *rest)

    if moved:
        scratch += [pltpu.VMEM(args[i].shape, args[i].dtype) for i in moved]
        scratch.append(pltpu.SemaphoreType.DMA((len(moved),)))
        specs = [HBM if i in moved else spec for i, spec in enumerate(specs)]
    return pl.pallas_call(
        fetching if moved else kernel,
        out_shape=outs,
        in_specs=specs,
        out_specs=more.pop("out_specs", jax.tree.map(lambda _: VMEM, outs)),
        scratch_shapes=scratch,
        compiler_params=pltpu.CompilerParams(vmem_limit_bytes=mib * MIB),
        cost_estimate=pl.CostEstimate(flops=0, bytes_accessed=0, transcendentals=0),
        **more,
    )(*args)


def over_head(blocks):
    return lax.all_to_all(blocks, "head", 0, 0, tiled=True)


def over_x(blocks):
    return lax.all_to_all(blocks, "head", 0, 0, tiled=True, axis_index_groups=ALONG_X)


def shift_x(blocks):
    perms = [[(i, (i + 2 * k) % 8) for i in range(8)] for k in range(4)]
    moved = [lax.ppermute(blocks[k], "head", perms[k]) for k in (2, 1, 3)]
    return [blocks[0], *moved]


def swap_y(value):
    return lax.ppermute(value, "head", [(i, i ^ 1) for i in range(8)])


def over_seq(blocks):
    return lax.all_to_all(blocks, "seq", 0, 0, tiled=True)


def swap_cores(value, n_dp, bit=1):
    return lax.ppermute(value, "dp", [(i, i ^ bit) for i in range(n_dp)])


def groups_of(n_dp):
    n_z = n_dp // 2
    low = min(4, n_z)
    high = n_z // low
    near = [
        [s * n_dp + 2 * (b * low + a) + c for s in range(2) for a in range(low)]
        for b in range(high)
        for c in range(2)
    ]
    far = [
        [2 * (b * low + a) + c for b in range(high)] for a in range(low) for c in range(2)
    ]
    return near, far


def over_near(blocks, near):
    return lax.all_to_all(blocks, ("seq", "dp"), 0, 0, tiled=True, axis_index_groups=near)


def on_device(n_dp, latents, cotangent, w_qkv, w_out):
    depth = latents.shape[-1]
    index = lax.axis_index("head")
    at = jnp.stack([lax.axis_index("dp") % 2, index % 2, index // 2]).astype(jnp.int32)
    near, far = groups_of(n_dp)
    x = latents.reshape(128, depth)
    g = cotangent.reshape(128, depth)
    w_own = w_qkv[0].reshape(3 * E, depth)

    hidden, row, own = call(
        norm_kernel, (shape(4, 168, depth), shape(168, depth), shape(2 * E, depth)),
        at, x, w_qkv.reshape(2, 3, E, depth), w_out.reshape(2, E, depth),
        in_specs=[SMEM] + [VMEM] * 3, fetch=(1, 2, 3), mib=60,
    )
    mine_two = lax.all_gather(own, "head", axis_index_groups=RING).reshape(16 * E, depth)
    hidden = over_x(hidden)
    partner = over_x(jnp.broadcast_to(swap_y(row)[None], (4, 168, depth)))
    heads, qkv, mine_one = call(
        spatial_kernel,
        (shape(8, E, 128), shape(2, 3 * E, 512), shape(8, 40, depth)),
        at, hidden, partner, w_own,
        in_specs=[SMEM] + [VMEM] * 3,
    )
    heads = over_head(heads)
    mine_one = mine_one.reshape(320, depth)
    other_one = swap_cores(mine_one, n_dp)
    big = shape(16 * E, depth)
    pair, mine_two = call(
        middle_kernel, (shape(2, 2, 2, 32, depth), big),
        at, x, g, heads, mine_one, other_one, mine_two,
        in_specs=[SMEM] + [VMEM] * 5 + [HBM], fetch=(1, 2, 3, 4, 5), mib=62,
        out_specs=(VMEM, HBM),
        input_output_aliases={6: 1},
        scratch_shapes=[pltpu.VMEM((2, 320, 128), F32)],
    )
    pair = over_seq(pair)
    other_two = swap_cores(mine_two, n_dp)
    back, keep, send = call(
        temporal_kernel,
        (shape(2, 2, 2, 32, depth), big, big),
        at, pair, mine_two, other_two,
        in_specs=[SMEM, VMEM, HBM, HBM],
        out_specs=(VMEM, HBM, HBM),
        scratch_shapes=[
            pltpu.VMEM((2, 16 * E, depth), BF),
            pltpu.VMEM((2, 16 * E, depth), BF),
            pltpu.VMEM((16 * E, 128), F32),
            pltpu.VMEM((16 * E, 256), F32),
            pltpu.VMEM((16 * E, 128), BF),
            pltpu.VMEM((16 * E, 256), BF),
            pltpu.SemaphoreType.DMA((2,)),
        ],
    )
    back = over_seq(back)
    two = (keep.astype(F32) + swap_cores(send, n_dp).astype(F32)).astype(BF)
    two = lax.psum_scatter(
        two, "head", scatter_dimension=0, tiled=True, axis_index_groups=RING
    )
    half = shape(8, 40, depth)
    gh, keep, send, output, grad_one = call(
        turn_kernel,
        (shape(8, E, 128), half, half, shape(128, depth), shape(128, depth)),
        at, back, heads, mine_one, other_one,
        in_specs=[SMEM] + [VMEM] * 4,
        scratch_shapes=[pltpu.VMEM((2, 320, 128), F32)],
    )
    gh = over_head(gh)
    parts = over_head((keep.astype(F32) + swap_cores(send, n_dp).astype(F32)).astype(BF))
    half, row = shape(112, depth), shape(128, depth)
    *terms, keep, send = call(
        spatial_back_kernel, (*[row] * 8, half, half),
        at, qkv, gh, hidden, partner, w_own,
        in_specs=[SMEM] + [VMEM] * 5, fetch=(1, 2, 3, 4, 5), mib=62,
        out_specs=(*[HBM] * 8, VMEM, VMEM),
        scratch_shapes=[pltpu.VMEM((8, 128, depth), BF), pltpu.SemaphoreType.DMA((8,))],
    )
    n_near, n_far = len(near[0]), len(far[0])
    size = 320 // n_near
    chain = call(
        chain_kernel, shape(n_near, size, depth), keep, swap_cores(send, n_dp), parts, two,
        scratch_shapes=[pltpu.VMEM((320, depth), F32)],
    )
    half, copies = call(
        half_sum_kernel, (row, shape(n_far, size, depth)),
        *shift_x(terms[:4]), over_near(chain, near),
    )
    summed = lax.all_to_all(copies, "dp", 0, 0, tiled=True, axis_index_groups=far)
    latent_grads, copies = call(
        last_kernel, (shape(128, depth), shape(n_near, size, depth)),
        *shift_x(terms[4:]), swap_y(half), x, grad_one, summed,
        fetch=(0, 1, 2, 3, 4, 5, 6, 7), mib=60,
    )
    mine = over_near(copies, near).reshape(320, depth)
    grad_qkv, grad_out = call(
        result_kernel,
        (
            jax.ShapeDtypeStruct((2, 3, E, depth), F32),
            jax.ShapeDtypeStruct((2, E, depth), F32),
        ),
        at, mine, swap_cores(mine, n_dp),
        in_specs=[SMEM, VMEM, VMEM],
        scratch_shapes=[pltpu.VMEM((2, 320, depth), F32)],
    )
    return (
        output.reshape(latents.shape),
        latent_grads.reshape(latents.shape),
        grad_qkv[:, None],
        grad_out[:, None],
    )


def solution(mesh):
    rows = P("dp", "seq", "head", None)
    specs = (rows, rows, P(None, "head", None, None, None), P(None, "head", None, None))
    return jax.shard_map(
        functools.partial(on_device, mesh.shape["dp"]),
        mesh=mesh, in_specs=specs, out_specs=specs, check_vma=False,
    )
```

```python
import functools

import jax
import jax.numpy as jnp
from jax import lax
from jax.experimental import pallas as pl
from jax.experimental.pallas import tpu as pltpu
from jax.sharding import PartitionSpec as P

EPSILON = 1e-06
E = 72
SCALE = E ** (-0.5)
RING = [[0, 2, 4, 6, 7, 5, 3, 1]]
ALONG_X = [[0, 2, 4, 6], [1, 3, 5, 7]]
BF = jnp.bfloat16
F32 = jnp.float32


def nn(a, b):
    return lax.dot_general(a, b, (((1,), (0,)), ((), ())), preferred_element_type=F32)


def nt(a, b):
    return lax.dot_general(a, b, (((1,), (1,)), ((), ())), preferred_element_type=F32)


def tn(a, b):
    return lax.dot_general(a, b, (((0,), (0,)), ((), ())), preferred_element_type=F32)


def normalize(rows):
    wide = rows.astype(F32)
    centered = wide - jnp.mean(wide, axis=-1, keepdims=True)
    inverse = lax.rsqrt(jnp.mean(centered * centered, axis=-1, keepdims=True) + EPSILON)
    return centered * inverse, inverse


def normalize_back(grad, inverse, normed, normed_grads):
    mean_grad = jnp.mean(normed_grads, axis=-1, keepdims=True)
    mean_cross = jnp.mean(normed_grads * normed, axis=-1, keepdims=True)
    return grad.astype(F32) + inverse * (normed_grads - mean_grad - normed * mean_cross)


def regroup(first, second):
    low = lax.broadcasted_iota(jnp.int32, first.shape, 1) < 64
    return (
        jnp.where(low, first, pltpu.roll(second, 64, 1)),
        jnp.where(low, pltpu.roll(first, 64, 1), second),
    )


def norm_kernel(at_ref, x_ref, wq_ref, wo_ref, out_ref, row_ref, own_ref):
    core = at_ref[0]
    wide = wo_ref[0].astype(F32)
    half = jnp.where(core == 0, wide[:40], wide[32:])
    hidden = normalize(x_ref[...])[0]
    block = jnp.concatenate([hidden, half], axis=0).astype(BF)
    row_ref[...] = block
    for j in range(4):
        out_ref[j] = block
    qk = jnp.concatenate([wq_ref[1, 0].astype(F32), wq_ref[1, 1].astype(F32)], axis=0)
    vo = jnp.concatenate([wq_ref[1, 2].astype(F32), wo_ref[1].astype(F32)], axis=0)
    own_ref[...] = jnp.where(core == 0, qk, vo).astype(BF)


def frame_rows(near_ref, far_ref, f):
    rows = [ref[:, f * 64 : (f + 1) * 64, :].reshape(256, ref.shape[2]) for ref in (near_ref, far_ref)]
    return jnp.concatenate(rows, axis=0)


def head_at(at_ref, slot):
    return 2 * (slot % 4) + (at_ref[1] if slot < 4 else 1 - at_ref[1])


def softmax(queries, key_rows):
    exponent = jnp.exp(tn(queries, key_rows) * SCALE)
    return exponent / jnp.sum(exponent, axis=1, keepdims=True)


def split3(stacked):
    return tuple(stacked[i * E : (i + 1) * E].astype(BF) for i in range(3))


def spatial_kernel(at_ref, near_ref, far_ref, w_ref, heads_ref, qkv_ref, one_ref):
    for i in range(8):
        block = (near_ref if i < 4 else far_ref)[i % 4].astype(F32)
        one_ref[head_at(at_ref, i)] = block[128:].astype(BF)
    outs = []
    for f in range(2):
        qkv = nt(w_ref[...], frame_rows(near_ref, far_ref, f))
        qkv_ref[f] = qkv.astype(BF)
        q, k, v = split3(qkv)
        weights = softmax(q, k).astype(BF)
        outs.append(nt(v, weights))
    for m in range(4):
        lanes = slice(m * 128, (m + 1) * 128)
        a, b = regroup(outs[0][:, lanes], outs[1][:, lanes])
        heads_ref[head_at(at_ref, 2 * m)] = a.astype(BF)
        heads_ref[head_at(at_ref, 2 * m + 1)] = b.astype(BF)


def middle_kernel(
    core_ref, x_ref, g_ref, heads_ref, mine_ref, other_ref, pass_ref, out_ref, same_ref, split_ref
):
    core = core_ref[0]
    for h in range(8):
        heads = heads_ref[h].astype(F32)
        split_ref[0, h * 40 : (h + 1) * 40] = heads[:40]
        low = jnp.zeros((8, 128), F32)
        split_ref[1, h * 40 : (h + 1) * 40] = jnp.concatenate([low, heads[40:]], axis=0)
    y = x_ref[...].astype(F32) + tn(split_ref[core].astype(BF), mine_ref[...])
    y = (y + tn(split_ref[1 - core].astype(BF), other_ref[...])).astype(BF)
    g = g_ref[...]
    for s in range(2):
        for f in range(2):
            rows = slice((2 * f + s) * 32, (2 * f + s + 1) * 32)
            out_ref[s, 0, f] = y[rows]
            out_ref[s, 1, f] = g[rows]


def temporal_kernel(
    core_ref, pair_ref, mine_ref, other_ref,
    back_ref, keep_ref, send_ref,
    w_ref, gw_ref, qk_ref, vg_ref, g0_ref, g1_ref, sems,
):
    core = core_ref[0]
    loads = (
        pltpu.make_async_copy(mine_ref, w_ref.at[core], sems.at[0]),
        pltpu.make_async_copy(other_ref, w_ref.at[1 - core], sems.at[1]),
    )
    for load in loads:
        load.start()
    depth = pair_ref.shape[-1]
    rows = jnp.concatenate([pair_ref[s, 0, f] for s in range(2) for f in range(2)], axis=0)
    grad = jnp.concatenate([pair_ref[s, 1, f] for s in range(2) for f in range(2)], axis=0)
    normed, inverse = normalize(rows)
    hidden = normed.astype(BF)
    both = jnp.concatenate([hidden, grad], axis=0)
    for load in loads:
        load.wait()
    qk_ref[...] = nt(w_ref[0], hidden)
    vg_ref[...] = nt(w_ref[1], both)

    def rounded(value):
        return value.astype(BF).astype(F32)

    def ahead(value, r):
        return pltpu.roll(value, 128 - 32 * r, 1) if r else value

    def behind(value, r):
        return pltpu.roll(value, 32 * r, 1) if r else value

    zeros = jnp.zeros((E, 128), F32)
    for h in range(8):
        base = h * 2 * E
        q = rounded(qk_ref[base : base + E])
        k = rounded(qk_ref[base + E : base + 2 * E])
        v = rounded(vg_ref[base : base + E, :128])
        gh = rounded(vg_ref[base + E : base + 2 * E, 128:])
        ks = [ahead(k, r) for r in range(4)]
        vs = [ahead(v, r) for r in range(4)]
        exps = [jnp.exp(jnp.sum(q * kr, axis=0, keepdims=True) * SCALE) for kr in ks]
        total = exps[0] + exps[1] + exps[2] + exps[3]
        probs = [e / total for e in exps]
        weights = [rounded(p) for p in probs]
        heads = sum(w * vr for w, vr in zip(weights, vs))
        gps = [jnp.sum(gh * vr, axis=0, keepdims=True) for vr in vs]
        inner = sum(p * gp for p, gp in zip(probs, gps))
        sgs = [rounded(p * (gp - inner) * SCALE) for p, gp in zip(probs, gps)]
        gq = sum(sg * kr for sg, kr in zip(sgs, ks))
        gk = sum(behind(sg * q, r) for r, sg in enumerate(sgs))
        gv = sum(behind(w * gh, r) for r, w in enumerate(weights))
        g0_ref[base : base + 2 * E] = jnp.concatenate([gq, gk], axis=0).astype(BF)
        g1_ref[base : base + 2 * E, :128] = jnp.concatenate([gv, zeros], axis=0).astype(BF)
        g1_ref[base : base + 2 * E, 128:] = jnp.concatenate([zeros, heads], axis=0).astype(BF)
    for h in range(8):
        span = slice(h * 2 * E, (h + 1) * 2 * E)
        gw_ref[0, span] = nn(g0_ref[span], hidden).astype(BF)
        gw_ref[1, span] = nn(g1_ref[span], both).astype(BF)
    stores = (
        pltpu.make_async_copy(gw_ref.at[core], keep_ref, sems.at[0]),
        pltpu.make_async_copy(gw_ref.at[1 - core], send_ref, sems.at[1]),
    )
    for store in stores:
        store.start()
    mixed = tn(g1_ref[...], w_ref[1])
    normed_grads = tn(g0_ref[...], w_ref[0]) + mixed[:128]
    result = (rows.astype(F32) + mixed[128:]).astype(BF)
    total_grad = normalize_back(grad, inverse, normed, normed_grads).astype(BF)
    for s in range(2):
        for f in range(2):
            at = slice((2 * s + f) * 32, (2 * s + f + 1) * 32)
            back_ref[s, 0, f] = result[at]
            back_ref[s, 1, f] = total_grad[at]
    for store in stores:
        store.wait()


def halves(rows, size):
    return rows[:size], rows[rows.shape[0] - size :]


def local_rows(pair_ref, which):
    return jnp.concatenate([pair_ref[s, which, f] for f in range(2) for s in range(2)], axis=0)


def turn_kernel(
    core_ref, back_ref, heads_ref, mine_ref, other_ref,
    gh_ref, keep_ref, send_ref, out_ref, grad_ref, split_ref,
):
    core = core_ref[0]
    out_ref[...] = local_rows(back_ref, 0)
    grad = local_rows(back_ref, 1)
    grad_ref[...] = grad
    split_ref[core] = nt(mine_ref[...], grad)
    split_ref[1 - core] = nt(other_ref[...], grad)
    for h in range(8):
        at = h * 40
        pieces = [split_ref[0, at : at + 40], split_ref[1, at + 8 : at + 40]]
        gh_ref[h] = jnp.concatenate(pieces, axis=0).astype(BF)
        low, high = halves(nn(heads_ref[h], grad), 40)
        keep_ref[h] = jnp.where(core == 0, low, high).astype(BF)
        send_ref[h] = jnp.where(core == 0, high, low).astype(BF)


def spatial_back_kernel(
    at_ref, qkv_ref, gh_ref, near_ref, far_ref, w_ref,
    a0_ref, a1_ref, a2_ref, a3_ref, b0_ref, b1_ref, b2_ref, b3_ref, keep_ref, send_ref, rows_ref, sems,
):
    frames = ([], [])
    for m in range(4):
        pair = regroup(*(gh_ref[head_at(at_ref, 2 * m + i)].astype(F32) for i in range(2)))
        for f in range(2):
            frames[f].append(pair[f])
    total = None
    for f in range(2):
        q, k, v = split3(qkv_ref[f].astype(F32))
        gh = jnp.concatenate(frames[f], axis=1).astype(BF)
        probs = softmax(q, k)
        gv = nn(gh, probs.astype(BF))
        gp = tn(gh, v)
        inner = jnp.sum(probs * gp, axis=1, keepdims=True)
        sg = (probs * (gp - inner) * SCALE).astype(BF)
        grads = jnp.concatenate([nt(k, sg), nn(q, sg), gv], axis=0).astype(BF)
        gw = nn(grads, frame_rows(near_ref, far_ref, f))
        total = gw if total is None else total + gw
        terms = tn(grads, w_ref[...]).astype(BF)
        for j in range(8):
            rows_ref[j, f * 64 : (f + 1) * 64, :] = terms[j * 64 : (j + 1) * 64]
    copies = []
    ahead = ((a0_ref, b0_ref), (a1_ref, b1_ref), (a2_ref, b2_ref), (a3_ref, b3_ref))
    for k, (other_ref, own_ref) in enumerate(ahead):
        x_at = lax.rem(at_ref[2] + k, 4)
        copies.append(pltpu.make_async_copy(rows_ref.at[x_at], own_ref, sems.at[k]))
        copies.append(pltpu.make_async_copy(rows_ref.at[4 + x_at], other_ref, sems.at[4 + k]))
    for copy in copies:
        copy.start()
    low, high = halves(total, 112)
    keep_ref[...] = jnp.where(at_ref[0] == 0, low, high).astype(BF)
    send_ref[...] = jnp.where(at_ref[0] == 0, high, low).astype(BF)
    for copy in copies:
        copy.wait()


def result_kernel(core_ref, mine_ref, other_ref, qkv_ref, out_ref, both_ref):
    core = core_ref[0]
    both_ref[core] = mine_ref[...].astype(F32)
    both_ref[1 - core] = other_ref[...].astype(F32)
    qkv = jnp.concatenate([both_ref[0, :112], both_ref[1, 8:112]], axis=0)
    for i in range(3):
        qkv_ref[0, i] = qkv[i * E : (i + 1) * E]
    out_ref[0] = jnp.concatenate([both_ref[0, 112:152], both_ref[1, 120:152]], axis=0)
    qkv_ref[1, 0] = both_ref[0, 152 : 152 + E]
    qkv_ref[1, 1] = both_ref[0, 152 + E : 152 + 2 * E]
    qkv_ref[1, 2] = both_ref[1, 152 : 152 + E]
    out_ref[1] = both_ref[1, 152 + E : 152 + 2 * E]


def chain_kernel(keep_ref, recv_ref, parts_ref, two_ref, chain_ref, rows_ref):
    rows_ref[:112] = keep_ref[...].astype(F32) + recv_ref[...].astype(F32)
    rows_ref[112:152] = block_sum(parts_ref)
    rows_ref[152:296] = two_ref[...].astype(F32)
    rows_ref[296:] = jnp.zeros_like(rows_ref[296:])
    n, size = chain_ref.shape[:2]
    for i in range(n):
        chain_ref[i] = rows_ref[i * size : (i + 1) * size].astype(BF)


def block_sum(ref):
    total = ref[0].astype(F32)
    for j in range(1, ref.shape[0]):
        total = total + ref[j].astype(F32)
    return total


def copy_sum(blocks_ref, out_ref):
    total = block_sum(blocks_ref).astype(BF)
    for i in range(out_ref.shape[0]):
        out_ref[i] = total


def half_sum_kernel(t0_ref, t1_ref, t2_ref, t3_ref, grads_ref, out_ref, copies_ref):
    out_ref[...] = row_sum(t0_ref, t1_ref, t2_ref, t3_ref).astype(BF)
    copy_sum(grads_ref, copies_ref)


def row_sum(*refs):
    total = refs[0][...].astype(F32)
    for ref in refs[1:]:
        total = total + ref[...].astype(F32)
    return total


def copy_kernel(grads_ref, *refs):
    copy_sum(grads_ref, refs[4])


def last_kernel(t0_ref, t1_ref, t2_ref, t3_ref, half_ref, x_ref, g_ref, out_ref):
    total = row_sum(t0_ref, t1_ref, t2_ref, t3_ref, half_ref)
    normed, inverse = normalize(x_ref[...])
    out_ref[...] = normalize_back(g_ref[...], inverse, normed, total).astype(BF)


VMEM = pl.BlockSpec(memory_space=pltpu.VMEM)
SMEM = pl.BlockSpec(memory_space=pltpu.SMEM)
HBM = pl.BlockSpec(memory_space=pltpu.HBM)
MIB = 1024 * 1024


def shape(*dims):
    return jax.ShapeDtypeStruct(dims, BF)


def call(kernel, outs, *args, mib=48, fetch=(), in_specs=None, scratch_shapes=(), **more):
    specs = list(in_specs or [VMEM] * len(args))
    scratch = list(scratch_shapes)
    moved = list(fetch)
    n_in, n_out, n_own = len(args), len(jax.tree.leaves(outs)), len(scratch)

    def fetching(*refs):
        ins = list(refs[:n_in])
        rest = refs[n_in : n_in + n_out + n_own]
        held, sems = refs[n_in + n_out + n_own : -1], refs[-1]
        copies = [
            pltpu.make_async_copy(ins[i], to, sems.at[k])
            for k, (i, to) in enumerate(zip(moved, held))
        ]
        for copy in copies:
            copy.start()
        for copy in copies:
            copy.wait()
        for i, to in zip(moved, held):
            ins[i] = to
        kernel(*ins, *rest)

    if moved:
        scratch += [pltpu.VMEM(args[i].shape, args[i].dtype) for i in moved]
        scratch.append(pltpu.SemaphoreType.DMA((len(moved),)))
        specs = [HBM if i in moved else spec for i, spec in enumerate(specs)]
    return pl.pallas_call(
        fetching if moved else kernel,
        out_shape=outs,
        in_specs=specs,
        out_specs=more.pop("out_specs", jax.tree.map(lambda _: VMEM, outs)),
        scratch_shapes=scratch,
        compiler_params=pltpu.CompilerParams(vmem_limit_bytes=mib * MIB),
        cost_estimate=pl.CostEstimate(flops=0, bytes_accessed=0, transcendentals=0),
        **more,
    )(*args)


def over_head(blocks):
    return lax.all_to_all(blocks, "head", 0, 0, tiled=True)


def over_x(blocks):
    return lax.all_to_all(blocks, "head", 0, 0, tiled=True, axis_index_groups=ALONG_X)


def shift_x(blocks):
    perms = [[(i, (i + 2 * k) % 8) for i in range(8)] for k in range(4)]
    moved = [lax.ppermute(blocks[k], "head", perms[k]) for k in (2, 1, 3)]
    return [blocks[0], *moved]


def swap_y(value):
    return lax.ppermute(value, "head", [(i, i ^ 1) for i in range(8)])


def over_seq(blocks):
    return lax.all_to_all(blocks, "seq", 0, 0, tiled=True)


def swap_cores(value, n_dp, bit=1):
    return lax.ppermute(value, "dp", [(i, i ^ bit) for i in range(n_dp)])


def groups_of(n_dp):
    n_z = n_dp // 2
    low = min(4, n_z)
    high = n_z // low
    near = [
        [s * n_dp + 2 * (b * low + a) + c for s in range(2) for a in range(low)]
        for b in range(high)
        for c in range(2)
    ]
    far = [
        [2 * (b * low + a) + c for b in range(high)] for a in range(low) for c in range(2)
    ]
    return near, far


def over_near(blocks, near):
    return lax.all_to_all(blocks, ("seq", "dp"), 0, 0, tiled=True, axis_index_groups=near)


def on_device(n_dp, latents, cotangent, w_qkv, w_out):
    depth = latents.shape[-1]
    index = lax.axis_index("head")
    at = jnp.stack([lax.axis_index("dp") % 2, index % 2, index // 2]).astype(jnp.int32)
    near, far = groups_of(n_dp)
    x = latents.reshape(128, depth)
    g = cotangent.reshape(128, depth)
    w_own = w_qkv[0].reshape(3 * E, depth)

    hidden, row, own = call(
        norm_kernel, (shape(4, 168, depth), shape(168, depth), shape(2 * E, depth)),
        at, x, w_qkv.reshape(2, 3, E, depth), w_out.reshape(2, E, depth),
        in_specs=[SMEM] + [VMEM] * 3, fetch=(1, 2, 3), mib=60,
    )
    mine_two = lax.all_gather(own, "head", axis_index_groups=RING).reshape(16 * E, depth)
    hidden = over_x(hidden)
    partner = over_x(jnp.broadcast_to(swap_y(row)[None], (4, 168, depth)))
    heads, qkv, mine_one = call(
        spatial_kernel,
        (shape(8, E, 128), shape(2, 3 * E, 512), shape(8, 40, depth)),
        at, hidden, partner, w_own,
        in_specs=[SMEM] + [VMEM] * 3,
    )
    heads = over_head(heads)
    mine_one = mine_one.reshape(320, depth)
    other_one = swap_cores(mine_one, n_dp)
    big = shape(16 * E, depth)
    pair, mine_two = call(
        middle_kernel, (shape(2, 2, 2, 32, depth), big),
        at, x, g, heads, mine_one, other_one, mine_two,
        in_specs=[SMEM] + [VMEM] * 5 + [HBM], fetch=(1, 2, 3, 4, 5), mib=62,
        out_specs=(VMEM, HBM),
        input_output_aliases={6: 1},
        scratch_shapes=[pltpu.VMEM((2, 320, 128), F32)],
    )
    pair = over_seq(pair)
    other_two = swap_cores(mine_two, n_dp)
    back, keep, send = call(
        temporal_kernel,
        (shape(2, 2, 2, 32, depth), big, big),
        at, pair, mine_two, other_two,
        in_specs=[SMEM, VMEM, HBM, HBM],
        out_specs=(VMEM, HBM, HBM),
        scratch_shapes=[
            pltpu.VMEM((2, 16 * E, depth), BF),
            pltpu.VMEM((2, 16 * E, depth), BF),
            pltpu.VMEM((16 * E, 128), F32),
            pltpu.VMEM((16 * E, 256), F32),
            pltpu.VMEM((16 * E, 128), BF),
            pltpu.VMEM((16 * E, 256), BF),
            pltpu.SemaphoreType.DMA((2,)),
        ],
        mib=60,
    )
    back = over_seq(back)
    two = (keep.astype(F32) + swap_cores(send, n_dp).astype(F32)).astype(BF)
    two = lax.psum_scatter(
        two, "head", scatter_dimension=0, tiled=True, axis_index_groups=RING
    )
    half = shape(8, 40, depth)
    gh, keep, send, output, grad_one = call(
        turn_kernel,
        (shape(8, E, 128), half, half, shape(128, depth), shape(128, depth)),
        at, back, heads, mine_one, other_one,
        in_specs=[SMEM] + [VMEM] * 4,
        scratch_shapes=[pltpu.VMEM((2, 320, 128), F32)],
    )
    gh = over_head(gh)
    parts = over_head((keep.astype(F32) + swap_cores(send, n_dp).astype(F32)).astype(BF))
    half, row = shape(112, depth), shape(128, depth)
    *terms, keep, send = call(
        spatial_back_kernel, (*[row] * 8, half, half),
        at, qkv, gh, hidden, partner, w_own,
        in_specs=[SMEM] + [VMEM] * 5, fetch=(1, 2, 3, 4, 5), mib=62,
        out_specs=(*[HBM] * 8, VMEM, VMEM),
        scratch_shapes=[pltpu.VMEM((8, 128, depth), BF), pltpu.SemaphoreType.DMA((8,))],
    )
    n_near, n_far = len(near[0]), len(far[0])
    size = 320 // n_near
    chain = call(
        chain_kernel, shape(n_near, size, depth), keep, swap_cores(send, n_dp), parts, two,
        fetch=(0, 1, 2, 3), mib=60,
        scratch_shapes=[pltpu.VMEM((320, depth), F32)],
    )
    half, copies = call(
        half_sum_kernel, (row, shape(n_far, size, depth)),
        *shift_x(terms[:4]), over_near(chain, near),
    )
    summed = lax.all_to_all(copies, "dp", 0, 0, tiled=True, axis_index_groups=far)
    own, *moved = shift_x(terms[4:])
    copies, *moved = call(
        copy_kernel, (shape(n_near, size, depth), *[row] * 4), summed, *moved, swap_y(half),
        in_specs=[VMEM] + [HBM] * 4,
        out_specs=(VMEM, *[HBM] * 4),
        input_output_aliases={i: i for i in range(1, 5)},
    )
    latent_grads = call(
        last_kernel, row, own, *moved, x, grad_one, fetch=(0, 1, 2, 3, 4, 5, 6), mib=60
    )
    mine = over_near(copies, near).reshape(320, depth)
    grad_qkv, grad_out = call(
        result_kernel,
        (
            jax.ShapeDtypeStruct((2, 3, E, depth), F32),
            jax.ShapeDtypeStruct((2, E, depth), F32),
        ),
        at, mine, swap_cores(mine, n_dp),
        in_specs=[SMEM, VMEM, VMEM],
        scratch_shapes=[pltpu.VMEM((2, 320, depth), F32)],
    )
    return (
        output.reshape(latents.shape),
        latent_grads.reshape(latents.shape),
        grad_qkv[:, None],
        grad_out[:, None],
    )


def solution(mesh):
    rows = P("dp", "seq", "head", None)
    specs = (rows, rows, P(None, "head", None, None, None), P(None, "head", None, None))
    return jax.shard_map(
        functools.partial(on_device, mesh.shape["dp"]),
        mesh=mesh, in_specs=specs, out_specs=specs, check_vma=False,
    )
```

```python
import functools

import jax
import jax.numpy as jnp
from jax import lax
from jax.experimental import pallas as pl
from jax.experimental.pallas import tpu as pltpu
from jax.sharding import PartitionSpec as P

EPSILON = 1e-06
E = 72
SCALE = E ** (-0.5)
RING = [[0, 2, 4, 6, 7, 5, 3, 1]]
ALONG_X = [[0, 2, 4, 6], [1, 3, 5, 7]]
BF = jnp.bfloat16
F32 = jnp.float32


def nn(a, b):
    return lax.dot_general(a, b, (((1,), (0,)), ((), ())), preferred_element_type=F32)


def nt(a, b):
    return lax.dot_general(a, b, (((1,), (1,)), ((), ())), preferred_element_type=F32)


def tn(a, b):
    return lax.dot_general(a, b, (((0,), (0,)), ((), ())), preferred_element_type=F32)


def normalize(rows):
    wide = rows.astype(F32)
    centered = wide - jnp.mean(wide, axis=-1, keepdims=True)
    inverse = lax.rsqrt(jnp.mean(centered * centered, axis=-1, keepdims=True) + EPSILON)
    return centered * inverse, inverse


def normalize_back(grad, inverse, normed, normed_grads):
    mean_grad = jnp.mean(normed_grads, axis=-1, keepdims=True)
    mean_cross = jnp.mean(normed_grads * normed, axis=-1, keepdims=True)
    return grad.astype(F32) + inverse * (normed_grads - mean_grad - normed * mean_cross)


def regroup(first, second):
    low = lax.broadcasted_iota(jnp.int32, first.shape, 1) < 64
    return (
        jnp.where(low, first, pltpu.roll(second, 64, 1)),
        jnp.where(low, pltpu.roll(first, 64, 1), second),
    )


def norm_kernel(at_ref, x_ref, wq_ref, wo_ref, out_ref, row_ref, own_ref):
    core = at_ref[0]
    wide = wo_ref[0].astype(F32)
    half = jnp.where(core == 0, wide[:40], wide[32:])
    hidden = normalize(x_ref[...])[0]
    block = jnp.concatenate([hidden, half], axis=0).astype(BF)
    row_ref[...] = block
    for j in range(4):
        out_ref[j] = block
    qk = jnp.concatenate([wq_ref[1, 0].astype(F32), wq_ref[1, 1].astype(F32)], axis=0)
    vo = jnp.concatenate([wq_ref[1, 2].astype(F32), wo_ref[1].astype(F32)], axis=0)
    own_ref[...] = jnp.where(core == 0, qk, vo).astype(BF)


def frame_rows(near_ref, far_ref, f):
    rows = [ref[:, f * 64 : (f + 1) * 64, :].reshape(256, ref.shape[2]) for ref in (near_ref, far_ref)]
    return jnp.concatenate(rows, axis=0)


def head_at(at_ref, slot):
    return 2 * (slot % 4) + (at_ref[1] if slot < 4 else 1 - at_ref[1])


def softmax(queries, key_rows):
    exponent = jnp.exp(tn(queries, key_rows) * SCALE)
    return exponent / jnp.sum(exponent, axis=1, keepdims=True)


def split3(stacked):
    return tuple(stacked[i * E : (i + 1) * E].astype(BF) for i in range(3))


def spatial_kernel(at_ref, near_ref, far_ref, w_ref, heads_ref, qkv_ref, one_ref):
    for i in range(8):
        block = (near_ref if i < 4 else far_ref)[i % 4].astype(F32)
        one_ref[head_at(at_ref, i)] = block[128:].astype(BF)
    outs = []
    for f in range(2):
        qkv = nt(w_ref[...], frame_rows(near_ref, far_ref, f))
        qkv_ref[f] = qkv.astype(BF)
        q, k, v = split3(qkv)
        weights = softmax(q, k).astype(BF)
        outs.append(nt(v, weights))
    for m in range(4):
        lanes = slice(m * 128, (m + 1) * 128)
        a, b = regroup(outs[0][:, lanes], outs[1][:, lanes])
        heads_ref[head_at(at_ref, 2 * m)] = a.astype(BF)
        heads_ref[head_at(at_ref, 2 * m + 1)] = b.astype(BF)


def middle_kernel(
    core_ref, x_ref, g_ref, heads_ref, mine_ref, other_ref, pass_ref, out_ref, same_ref, split_ref
):
    core = core_ref[0]
    for h in range(8):
        heads = heads_ref[h].astype(F32)
        split_ref[0, h * 40 : (h + 1) * 40] = heads[:40]
        low = jnp.zeros((8, 128), F32)
        split_ref[1, h * 40 : (h + 1) * 40] = jnp.concatenate([low, heads[40:]], axis=0)
    y = x_ref[...].astype(F32) + tn(split_ref[core].astype(BF), mine_ref[...])
    y = (y + tn(split_ref[1 - core].astype(BF), other_ref[...])).astype(BF)
    g = g_ref[...]
    for s in range(2):
        for f in range(2):
            rows = slice((2 * f + s) * 32, (2 * f + s + 1) * 32)
            out_ref[s, 0, f] = y[rows]
            out_ref[s, 1, f] = g[rows]


def temporal_kernel(
    core_ref, pair_ref, mine_ref, other_ref,
    back_ref, keep_ref, send_ref,
    w_ref, gw_ref, qk_ref, vg_ref, g0_ref, g1_ref, sems,
):
    core = core_ref[0]
    loads = (
        pltpu.make_async_copy(mine_ref, w_ref.at[core], sems.at[0]),
        pltpu.make_async_copy(other_ref, w_ref.at[1 - core], sems.at[1]),
    )
    for load in loads:
        load.start()
    depth = pair_ref.shape[-1]
    rows = jnp.concatenate([pair_ref[s, 0, f] for s in range(2) for f in range(2)], axis=0)
    grad = jnp.concatenate([pair_ref[s, 1, f] for s in range(2) for f in range(2)], axis=0)
    normed, inverse = normalize(rows)
    hidden = normed.astype(BF)
    both = jnp.concatenate([hidden, grad], axis=0)
    for load in loads:
        load.wait()
    qk_ref[...] = nt(w_ref[0], hidden)
    vg_ref[...] = nt(w_ref[1], both)

    def rounded(value):
        return value.astype(BF).astype(F32)

    def ahead(value, r):
        return pltpu.roll(value, 128 - 32 * r, 1) if r else value

    def behind(value, r):
        return pltpu.roll(value, 32 * r, 1) if r else value

    zeros = jnp.zeros((E, 128), F32)
    for h in range(8):
        base = h * 2 * E
        q = rounded(qk_ref[base : base + E])
        k = rounded(qk_ref[base + E : base + 2 * E])
        v = rounded(vg_ref[base : base + E, :128])
        gh = rounded(vg_ref[base + E : base + 2 * E, 128:])
        ks = [ahead(k, r) for r in range(4)]
        vs = [ahead(v, r) for r in range(4)]
        exps = [jnp.exp(jnp.sum(q * kr, axis=0, keepdims=True) * SCALE) for kr in ks]
        total = exps[0] + exps[1] + exps[2] + exps[3]
        probs = [e / total for e in exps]
        weights = [rounded(p) for p in probs]
        heads = sum(w * vr for w, vr in zip(weights, vs))
        gps = [jnp.sum(gh * vr, axis=0, keepdims=True) for vr in vs]
        inner = sum(p * gp for p, gp in zip(probs, gps))
        sgs = [rounded(p * (gp - inner) * SCALE) for p, gp in zip(probs, gps)]
        gq = sum(sg * kr for sg, kr in zip(sgs, ks))
        gk = sum(behind(sg * q, r) for r, sg in enumerate(sgs))
        gv = sum(behind(w * gh, r) for r, w in enumerate(weights))
        g0_ref[base : base + 2 * E] = jnp.concatenate([gq, gk], axis=0).astype(BF)
        g1_ref[base : base + 2 * E, :128] = jnp.concatenate([gv, zeros], axis=0).astype(BF)
        g1_ref[base : base + 2 * E, 128:] = jnp.concatenate([zeros, heads], axis=0).astype(BF)
    for h in range(8):
        span = slice(h * 2 * E, (h + 1) * 2 * E)
        gw_ref[0, span] = nn(g0_ref[span], hidden).astype(BF)
        gw_ref[1, span] = nn(g1_ref[span], both).astype(BF)
    stores = (
        pltpu.make_async_copy(gw_ref.at[core], keep_ref, sems.at[0]),
        pltpu.make_async_copy(gw_ref.at[1 - core], send_ref, sems.at[1]),
    )
    for store in stores:
        store.start()
    mixed = tn(g1_ref[...], w_ref[1])
    normed_grads = tn(g0_ref[...], w_ref[0]) + mixed[:128]
    result = (rows.astype(F32) + mixed[128:]).astype(BF)
    total_grad = normalize_back(grad, inverse, normed, normed_grads).astype(BF)
    for s in range(2):
        for f in range(2):
            at = slice((2 * s + f) * 32, (2 * s + f + 1) * 32)
            back_ref[s, 0, f] = result[at]
            back_ref[s, 1, f] = total_grad[at]
    for store in stores:
        store.wait()


def halves(rows, size):
    return rows[:size], rows[rows.shape[0] - size :]


def local_rows(pair_ref, which):
    return jnp.concatenate([pair_ref[s, which, f] for f in range(2) for s in range(2)], axis=0)


def turn_kernel(
    core_ref, back_ref, heads_ref, mine_ref, other_ref,
    gh_ref, keep_ref, send_ref, out_ref, grad_ref, split_ref,
):
    core = core_ref[0]
    out_ref[...] = local_rows(back_ref, 0)
    grad = local_rows(back_ref, 1)
    grad_ref[...] = grad
    split_ref[core] = nt(mine_ref[...], grad)
    split_ref[1 - core] = nt(other_ref[...], grad)
    for h in range(8):
        at = h * 40
        pieces = [split_ref[0, at : at + 40], split_ref[1, at + 8 : at + 40]]
        gh_ref[h] = jnp.concatenate(pieces, axis=0).astype(BF)
        low, high = halves(nn(heads_ref[h], grad), 40)
        keep_ref[h] = jnp.where(core == 0, low, high).astype(BF)
        send_ref[h] = jnp.where(core == 0, high, low).astype(BF)


def spatial_back_kernel(
    at_ref, qkv_ref, gh_ref, near_ref, far_ref, w_ref,
    a0_ref, a1_ref, a2_ref, a3_ref, b0_ref, b1_ref, b2_ref, b3_ref, keep_ref, send_ref, rows_ref, sems,
):
    frames = ([], [])
    for m in range(4):
        pair = regroup(*(gh_ref[head_at(at_ref, 2 * m + i)].astype(F32) for i in range(2)))
        for f in range(2):
            frames[f].append(pair[f])
    total = None
    for f in range(2):
        q, k, v = split3(qkv_ref[f].astype(F32))
        gh = jnp.concatenate(frames[f], axis=1).astype(BF)
        probs = softmax(q, k)
        gv = nn(gh, probs.astype(BF))
        gp = tn(gh, v)
        inner = jnp.sum(probs * gp, axis=1, keepdims=True)
        sg = (probs * (gp - inner) * SCALE).astype(BF)
        grads = jnp.concatenate([nt(k, sg), nn(q, sg), gv], axis=0).astype(BF)
        gw = nn(grads, frame_rows(near_ref, far_ref, f))
        total = gw if total is None else total + gw
        terms = tn(grads, w_ref[...]).astype(BF)
        for j in range(8):
            rows_ref[j, f * 64 : (f + 1) * 64, :] = terms[j * 64 : (j + 1) * 64]
    copies = []
    ahead = ((a0_ref, b0_ref), (a1_ref, b1_ref), (a2_ref, b2_ref), (a3_ref, b3_ref))
    for k, (other_ref, own_ref) in enumerate(ahead):
        x_at = lax.rem(at_ref[2] + k, 4)
        copies.append(pltpu.make_async_copy(rows_ref.at[x_at], own_ref, sems.at[k]))
        copies.append(pltpu.make_async_copy(rows_ref.at[4 + x_at], other_ref, sems.at[4 + k]))
    for copy in copies:
        copy.start()
    low, high = halves(total, 112)
    keep_ref[...] = jnp.where(at_ref[0] == 0, low, high).astype(BF)
    send_ref[...] = jnp.where(at_ref[0] == 0, high, low).astype(BF)
    for copy in copies:
        copy.wait()


def result_kernel(core_ref, mine_ref, other_ref, qkv_ref, out_ref, both_ref):
    core = core_ref[0]
    both_ref[core] = mine_ref[...].astype(F32)
    both_ref[1 - core] = other_ref[...].astype(F32)
    qkv = jnp.concatenate([both_ref[0, :112], both_ref[1, 8:112]], axis=0)
    for i in range(3):
        qkv_ref[0, i] = qkv[i * E : (i + 1) * E]
    out_ref[0] = jnp.concatenate([both_ref[0, 112:152], both_ref[1, 120:152]], axis=0)
    qkv_ref[1, 0] = both_ref[0, 152 : 152 + E]
    qkv_ref[1, 1] = both_ref[0, 152 + E : 152 + 2 * E]
    qkv_ref[1, 2] = both_ref[1, 152 : 152 + E]
    out_ref[1] = both_ref[1, 152 + E : 152 + 2 * E]


def chain_kernel(keep_ref, recv_ref, parts_ref, two_ref, chain_ref, rows_ref):
    rows_ref[:112] = keep_ref[...].astype(F32) + recv_ref[...].astype(F32)
    rows_ref[112:152] = block_sum(parts_ref)
    rows_ref[152:296] = two_ref[...].astype(F32)
    rows_ref[296:] = jnp.zeros_like(rows_ref[296:])
    n, size = chain_ref.shape[:2]
    for i in range(n):
        chain_ref[i] = rows_ref[i * size : (i + 1) * size].astype(BF)


def block_sum(ref):
    total = ref[0].astype(F32)
    for j in range(1, ref.shape[0]):
        total = total + ref[j].astype(F32)
    return total


def copy_sum(blocks_ref, out_ref):
    total = block_sum(blocks_ref).astype(BF)
    for i in range(out_ref.shape[0]):
        out_ref[i] = total


def half_sum_kernel(t0_ref, t1_ref, t2_ref, t3_ref, grads_ref, out_ref, copies_ref):
    out_ref[...] = row_sum(t0_ref, t1_ref, t2_ref, t3_ref).astype(BF)
    copy_sum(grads_ref, copies_ref)


def row_sum(*refs):
    total = refs[0][...].astype(F32)
    for ref in refs[1:]:
        total = total + ref[...].astype(F32)
    return total


def copy_kernel(grads_ref, *refs):
    copy_sum(grads_ref, refs[4])


def last_kernel(t0_ref, t1_ref, t2_ref, t3_ref, half_ref, x_ref, g_ref, out_ref):
    total = row_sum(t0_ref, t1_ref, t2_ref, t3_ref, half_ref)
    normed, inverse = normalize(x_ref[...])
    out_ref[...] = normalize_back(g_ref[...], inverse, normed, total).astype(BF)


VMEM = pl.BlockSpec(memory_space=pltpu.VMEM)
SMEM = pl.BlockSpec(memory_space=pltpu.SMEM)
HBM = pl.BlockSpec(memory_space=pltpu.HBM)
MIB = 1024 * 1024


def shape(*dims):
    return jax.ShapeDtypeStruct(dims, BF)


def call(kernel, outs, *args, mib=48, fetch=(), in_specs=None, scratch_shapes=(), **more):
    specs = list(in_specs or [VMEM] * len(args))
    scratch = list(scratch_shapes)
    moved = list(fetch)
    n_in, n_out, n_own = len(args), len(jax.tree.leaves(outs)), len(scratch)

    def fetching(*refs):
        ins = list(refs[:n_in])
        rest = refs[n_in : n_in + n_out + n_own]
        held, sems = refs[n_in + n_out + n_own : -1], refs[-1]
        copies = [
            pltpu.make_async_copy(ins[i], to, sems.at[k])
            for k, (i, to) in enumerate(zip(moved, held))
        ]
        for copy in copies:
            copy.start()
        for copy in copies:
            copy.wait()
        for i, to in zip(moved, held):
            ins[i] = to
        kernel(*ins, *rest)

    if moved:
        scratch += [pltpu.VMEM(args[i].shape, args[i].dtype) for i in moved]
        scratch.append(pltpu.SemaphoreType.DMA((len(moved),)))
        specs = [HBM if i in moved else spec for i, spec in enumerate(specs)]
    return pl.pallas_call(
        fetching if moved else kernel,
        out_shape=outs,
        in_specs=specs,
        out_specs=more.pop("out_specs", jax.tree.map(lambda _: VMEM, outs)),
        scratch_shapes=scratch,
        compiler_params=pltpu.CompilerParams(vmem_limit_bytes=mib * MIB),
        cost_estimate=pl.CostEstimate(flops=0, bytes_accessed=0, transcendentals=0),
        **more,
    )(*args)


def over_head(blocks):
    return lax.all_to_all(blocks, "head", 0, 0, tiled=True)


def over_x(blocks):
    return lax.all_to_all(blocks, "head", 0, 0, tiled=True, axis_index_groups=ALONG_X)


def shift_x(blocks):
    perms = [[(i, (i + 2 * k) % 8) for i in range(8)] for k in range(4)]
    moved = [lax.ppermute(blocks[k], "head", perms[k]) for k in (2, 1, 3)]
    return [blocks[0], *moved]


def swap_y(value):
    return lax.ppermute(value, "head", [(i, i ^ 1) for i in range(8)])


def over_seq(blocks):
    return lax.all_to_all(blocks, "seq", 0, 0, tiled=True)


def swap_cores(value, n_dp, bit=1):
    return lax.ppermute(value, "dp", [(i, i ^ bit) for i in range(n_dp)])


def groups_of(n_dp):
    n_z = n_dp // 2
    low = min(4, n_z)
    high = n_z // low
    near = [
        [s * n_dp + 2 * (b * low + a) + c for s in range(2) for a in range(low)]
        for b in range(high)
        for c in range(2)
    ]
    far = [
        [2 * (b * low + a) + c for b in range(high)] for a in range(low) for c in range(2)
    ]
    return near, far


def over_near(blocks, near):
    return lax.all_to_all(blocks, ("seq", "dp"), 0, 0, tiled=True, axis_index_groups=near)


def on_device(n_dp, latents, cotangent, w_qkv, w_out):
    depth = latents.shape[-1]
    index = lax.axis_index("head")
    at = jnp.stack([lax.axis_index("dp") % 2, index % 2, index // 2]).astype(jnp.int32)
    near, far = groups_of(n_dp)
    x = latents.reshape(128, depth)
    g = cotangent.reshape(128, depth)
    w_own = w_qkv[0].reshape(3 * E, depth)

    hidden, row, own = call(
        norm_kernel, (shape(4, 168, depth), shape(168, depth), shape(2 * E, depth)),
        at, x, w_qkv.reshape(2, 3, E, depth), w_out.reshape(2, E, depth),
        in_specs=[SMEM] + [VMEM] * 3, fetch=(1, 2, 3), mib=60,
    )
    mine_two = lax.all_gather(own, "head", axis_index_groups=RING).reshape(16 * E, depth)
    hidden = over_x(hidden)
    partner = over_x(jnp.broadcast_to(swap_y(row)[None], (4, 168, depth)))
    heads, qkv, mine_one = call(
        spatial_kernel,
        (shape(8, E, 128), shape(2, 3 * E, 512), shape(8, 40, depth)),
        at, hidden, partner, w_own,
        in_specs=[SMEM] + [VMEM] * 3,
    )
    heads = over_head(heads)
    mine_one = mine_one.reshape(320, depth)
    other_one = swap_cores(mine_one, n_dp)
    big = shape(16 * E, depth)
    pair, mine_two = call(
        middle_kernel, (shape(2, 2, 2, 32, depth), big),
        at, x, g, heads, mine_one, other_one, mine_two,
        in_specs=[SMEM] + [VMEM] * 5 + [HBM], fetch=(1, 2, 3, 4, 5), mib=62,
        out_specs=(VMEM, HBM),
        input_output_aliases={6: 1},
        scratch_shapes=[pltpu.VMEM((2, 320, 128), F32)],
    )
    pair = over_seq(pair)
    other_two = swap_cores(mine_two, n_dp)
    back, keep, send = call(
        temporal_kernel,
        (shape(2, 2, 2, 32, depth), big, big),
        at, pair, mine_two, other_two,
        in_specs=[SMEM, VMEM, HBM, HBM],
        out_specs=(VMEM, HBM, HBM),
        scratch_shapes=[
            pltpu.VMEM((2, 16 * E, depth), BF),
            pltpu.VMEM((2, 16 * E, depth), BF),
            pltpu.VMEM((16 * E, 128), F32),
            pltpu.VMEM((16 * E, 256), F32),
            pltpu.VMEM((16 * E, 128), BF),
            pltpu.VMEM((16 * E, 256), BF),
            pltpu.SemaphoreType.DMA((2,)),
        ],
    )
    back = over_seq(back)
    two = (keep.astype(F32) + swap_cores(send, n_dp).astype(F32)).astype(BF)
    two = lax.psum_scatter(
        two, "head", scatter_dimension=0, tiled=True, axis_index_groups=RING
    )
    half = shape(8, 40, depth)
    gh, keep, send, output, grad_one = call(
        turn_kernel,
        (shape(8, E, 128), half, half, shape(128, depth), shape(128, depth)),
        at, back, heads, mine_one, other_one,
        in_specs=[SMEM] + [VMEM] * 4,
        scratch_shapes=[pltpu.VMEM((2, 320, 128), F32)],
    )
    gh = over_head(gh)
    parts = over_head((keep.astype(F32) + swap_cores(send, n_dp).astype(F32)).astype(BF))
    half, row = shape(112, depth), shape(128, depth)
    *terms, keep, send = call(
        spatial_back_kernel, (*[row] * 8, half, half),
        at, qkv, gh, hidden, partner, w_own,
        in_specs=[SMEM] + [VMEM] * 5, fetch=(1, 2, 3, 4, 5), mib=62,
        out_specs=(*[HBM] * 8, VMEM, VMEM),
        scratch_shapes=[pltpu.VMEM((8, 128, depth), BF), pltpu.SemaphoreType.DMA((8,))],
    )
    n_near, n_far = len(near[0]), len(far[0])
    size = 320 // n_near
    chain = call(
        chain_kernel, shape(n_near, size, depth), keep, swap_cores(send, n_dp), parts, two,
        fetch=(0, 1, 2, 3), mib=60,
        scratch_shapes=[pltpu.VMEM((320, depth), F32)],
    )
    half, copies = call(
        half_sum_kernel, (row, shape(n_far, size, depth)),
        *shift_x(terms[:4]), over_near(chain, near),
    )
    summed = lax.all_to_all(copies, "dp", 0, 0, tiled=True, axis_index_groups=far)
    own, *moved = shift_x(terms[4:])
    copies, *moved = call(
        copy_kernel, (shape(n_near, size, depth), *[row] * 4), summed, *moved, swap_y(half),
        in_specs=[VMEM] + [HBM] * 4,
        out_specs=(VMEM, *[HBM] * 4),
        input_output_aliases={i: i for i in range(1, 5)},
    )
    latent_grads = call(
        last_kernel, row, own, *moved, x, grad_one, fetch=(0, 1, 2, 3, 4, 5, 6), mib=60
    )
    mine = over_near(copies, near).reshape(320, depth)
    grad_qkv, grad_out = call(
        result_kernel,
        (
            jax.ShapeDtypeStruct((2, 3, E, depth), F32),
            jax.ShapeDtypeStruct((2, E, depth), F32),
        ),
        at, mine, swap_cores(mine, n_dp),
        in_specs=[SMEM, VMEM, VMEM],
        scratch_shapes=[pltpu.VMEM((2, 320, depth), F32)],
    )
    return (
        output.reshape(latents.shape),
        latent_grads.reshape(latents.shape),
        grad_qkv[:, None],
        grad_out[:, None],
    )


def solution(mesh):
    rows = P("dp", "seq", "head", None)
    specs = (rows, rows, P(None, "head", None, None, None), P(None, "head", None, None))
    return jax.shard_map(
        functools.partial(on_device, mesh.shape["dp"]),
        mesh=mesh, in_specs=specs, out_specs=specs, check_vma=False,
    )
```
